128 devices in a mesh: dp: 2 (over core), ctx: 8 (over z, x_lo), tp: 8 (over x_hi, y).
Axes of the slice: x: 4 (x_hi: 2, x_lo: 2; x = x_hi * 2 + x_lo), y: 4, z: 4, core: 2. Of those that a mesh axis runs over, the one named last changes fastest.
Arguments:
- clean: bfloat16 [2, 2048, 5120], P('dp', 'ctx'), may hold values from -6 to 6
- noise: bfloat16 [2, 2048, 5120], P('dp', 'ctx'), may hold values from -6 to 6
- timestep: int32 [2], P('dp'), may hold values from 200 to 999
- teacher_gain: float32 [5120], replicated, may hold values from 0.7 to 2.8
- critic_gain: float32 [5120], replicated, may hold values from 0.7 to 2.8
- teacher_qkv: bfloat16 [5120, 3, 3072], P('dp', None, 'tp'), may hold values from -0.11879111 to 0.11879111
- critic_qkv: bfloat16 [5120, 3, 3072], P('dp', None, 'tp'), may hold values from -0.11879111 to 0.11879111
- teacher_out: bfloat16 [3072, 5120], P('tp', 'dp'), may hold values from -0.625 to 0.625
- critic_out: bfloat16 [3072, 5120], P('tp', 'dp'), may hold values from -0.625 to 0.625
Outputs:
- kl_grad: bfloat16 [2, 2048, 5120], P('dp', 'ctx', 'tp')
The draws below stay inside these ranges and needn't reach their ends.
All inputs are finite; a program needn't handle non-finite values.
Results may differ from the reference program's by a relative error of at most 0.019.
The reference program's roundings to bfloat16 on the way count: a program that leaves them out, or rounds other values in their place, can miss the bound.
Values may be sent and summed in bfloat16 or wider, within the bound.
No kernel may reach another device: no remote copies, remote signals or barrier semaphores. Data moves between devices by JAX's collectives and lax.ppermute only.
A program may use at most 128 MiB of HBM per device.

```python
import jax
import jax.numpy as jnp
from jax import lax

D = 5120
HEADS = 24
HD = 128
HQ = 3072
SEQ = 2048
CLIPS = 2


def gain_values(key):
    return jax.random.uniform(key, (D,), jnp.float32, 0.7, 1.3)


def projection_values(key):
    base_key = jax.random.fold_in(key, 0)
    spread = (2.0 / D) ** 0.5
    return jnp.clip(jax.random.normal(base_key, (D, 3, HQ), jnp.float32), -6.0, 6.0) * spread


def draw_teacher_gain(key, part):
    key = jax.random.fold_in(key, 11)
    return gain_values(key)


def draw_critic_gain(key, part):
    key = jax.random.fold_in(key, 12)
    return gain_values(key)


def draw_teacher_qkv(key, part):
    key = jax.random.fold_in(key, 13)
    return projection_values(key).astype(jnp.bfloat16)


def draw_critic_qkv(key, part):
    key = jax.random.fold_in(key, 14)
    return projection_values(key).astype(jnp.bfloat16)


def levels(rng, shape, pieces, smallest, top_value):
    def one(position, shards_of):
        heights = jax.random.uniform(jax.random.fold_in(jax.random.fold_in(rng, 6), position), (shards_of,), jnp.float32, smallest / len(pieces), top_value / len(pieces))
        return jnp.repeat(jnp.exp(heights), shape[position] // shards_of).reshape((-1,) + (1,) * (len(shape) - position - 1))

    loudness = one(*pieces[0])
    for cut in pieces[1:]:
        loudness = loudness * one(*cut)
    return loudness


def gaussian(key, dims, scale, most, shards=(), kind=jnp.bfloat16):
    loudness = levels(key, dims, shards, -0.22, 0.18) if shards else 1.0
    entries = jax.random.normal(key, dims, jnp.float32) * scale * loudness
    return jnp.minimum(jnp.maximum(entries, -most), most).astype(kind)


def setup_inputs(seed: int = 0) -> dict:
    arg_keys = jax.random.split(jax.random.key(seed), 10)
    clean = gaussian(arg_keys[0], (CLIPS, SEQ, D), 1.0, 6.0, ((0, 2), (1, 8)))
    noise = gaussian(arg_keys[1], (CLIPS, SEQ, D), 1.0, 6.0, ((0, 2), (1, 8)))
    timestep = jax.random.randint(arg_keys[2], (CLIPS,), 200, 1000).astype(jnp.int32)
    teacher_gain = draw_teacher_gain(jax.random.fold_in(arg_keys[9], 71), 0)
    critic_gain = draw_critic_gain(jax.random.fold_in(arg_keys[9], 71), 0)
    teacher_qkv = draw_teacher_qkv(jax.random.fold_in(arg_keys[9], 71), 0)
    critic_qkv = draw_critic_qkv(jax.random.fold_in(arg_keys[9], 71), 0)
    teacher_out = gaussian(arg_keys[7], (HQ, D), (max(HQ // 36, 1)) ** -0.5, 0.625, ((0, 8), (1, 2)))
    critic_out = gaussian(arg_keys[8], (HQ, D), (max(HQ // 36, 1)) ** -0.5, 0.625, ((0, 8), (1, 2)))
    return {"clean": clean, "noise": noise, "timestep": timestep, "teacher_gain": teacher_gain, "critic_gain": critic_gain, "teacher_qkv": teacher_qkv, "critic_qkv": critic_qkv, "teacher_out": teacher_out, "critic_out": critic_out}


def rounded(value):
    return lax.optimization_barrier(value.astype(jnp.bfloat16))

def head_attention(inputs):
    query, keys, values = inputs
    score = jnp.einsum('cqd,ckd->cqk', query.astype(jnp.float32), keys.astype(jnp.float32)) * HD ** (-0.5)
    peak = lax.optimization_barrier(jnp.max(score, axis=-1, keepdims=True))
    weights = jnp.exp(score - peak)
    total = lax.optimization_barrier(jnp.sum(weights, axis=-1))
    prob = rounded(weights).astype(jnp.float32)
    summed = jnp.einsum('cqk,ckd->cqd', prob, values.astype(jnp.float32))
    return (summed / total[..., None]).astype(jnp.bfloat16)

def velocity(noisy, gain, qkv_weight, out_weight):
    inverse = lax.rsqrt(lax.optimization_barrier(jnp.mean(noisy * noisy, axis=-1, keepdims=True)) + 1e-06)
    normed = rounded(noisy * inverse * gain).astype(jnp.float32)
    proj = jnp.einsum('csd,dkp->cskp', normed, qkv_weight.astype(jnp.float32))
    proj = rounded(proj)
    clips, tokens = (proj.shape[0], proj.shape[1])
    split = proj.reshape(clips, tokens, 3, HEADS, HD)
    query = jnp.transpose(split[:, :, 0], (2, 0, 1, 3))
    keys = jnp.transpose(split[:, :, 1], (2, 0, 1, 3))
    values = jnp.transpose(split[:, :, 2], (2, 0, 1, 3))
    attn = lax.map(head_attention, (query, keys, values))
    attn = jnp.transpose(attn, (1, 2, 0, 3)).reshape(clips, tokens, HEADS * HD)
    return jnp.einsum('csp,pe->cse', attn.astype(jnp.float32), out_weight.astype(jnp.float32))

def reference(clean, noise, timestep, teacher_gain, critic_gain, teacher_qkv, critic_qkv, teacher_out, critic_out):
    step = (timestep.astype(jnp.float32) + 1.0) / 1000.0
    level = (5.0 * step / (1.0 + 4.0 * step))[:, None, None]
    noisy = (1.0 - level) * clean.astype(jnp.float32) + level * noise.astype(jnp.float32)
    teacher_v = velocity(noisy, teacher_gain, teacher_qkv, teacher_out)
    critic_v = velocity(noisy, critic_gain, critic_qkv, critic_out)
    return (level * (teacher_v - critic_v)).astype(jnp.bfloat16)
```

```python
import jax
import jax.numpy as jnp
import numpy as np
from jax import lax
from jax.experimental import pallas as pl
from jax.experimental.pallas import tpu as pltpu
from jax.sharding import PartitionSpec as P

HD = 128
AXES = ("dp", "ctx", "tp")
Z, XL, XH, Y = 4, 2, 2, 4
MIB = 1024 * 1024


def moved(core=0, z=0, xl=0, xh=0, y=0):
    pairs = []
    for d in range(2):
        for a in range(Z):
            for b in range(XL):
                for e in range(XH):
                    for f in range(Y):
                        source = ((d * Z + a) * XL + b) * XH * Y + e * Y + f
                        target = (
                            (((d + core) % 2) * Z + (a + z) % Z) * XL + (b + xl) % XL
                        ) * XH * Y + ((e + xh) % XH) * Y + (f + y) % Y
                        pairs.append((source, target))
    return pairs


CORE = moved(core=1)


def send(value, pairs):
    return lax.ppermute(value, AXES, pairs)


Z_GROUPS = [[a * XL + b for a in range(Z)] for b in range(XL)]


def over_z(value):
    return lax.all_to_all(value, "ctx", 0, 0, axis_index_groups=Z_GROUPS, tiled=True)


def params(mib, grid=0):
    return pltpu.CompilerParams(
        vmem_limit_bytes=mib * MIB, dimension_semantics=("arbitrary",) * grid
    )


def cost(flops, size, exps=0):
    return pl.CostEstimate(flops=flops, bytes_accessed=size, transcendentals=exps)


def norm_kernel(core_ref, step_ref, clean_ref, noise_ref, gt_ref, gc_ref, keep_ref, send_ref, noisy_ref):
    rows, width = noisy_ref.shape
    half = width // 2
    core = core_ref[0]
    step = (jnp.full((rows, 1), step_ref[0], jnp.int32).astype(jnp.float32) + 1.0) / 1000.0
    level = 5.0 * step / (1.0 + 4.0 * step)
    noisy = (1.0 - level) * clean_ref[...].astype(jnp.float32) + level * noise_ref[
        ...
    ].astype(jnp.float32)
    noisy_ref[...] = noisy
    inverse = lax.rsqrt(jnp.mean(noisy * noisy, axis=-1, keepdims=True) + 1e-06)
    for out, which in ((send_ref, 1 - core), (keep_ref, core)):
        columns = pl.ds(pl.multiple_of(which * half, 128), half)
        scaled = noisy_ref[:, columns] * inverse
        out[0] = (scaled * gt_ref[:, columns]).astype(jnp.bfloat16)
        out[1] = (scaled * gc_ref[:, columns]).astype(jnp.bfloat16)


def norm(core, timestep, clean, noise, gt, gc):
    tokens, width = clean.shape
    rows = 32
    count = tokens // rows
    half = width // 2
    shape = jax.ShapeDtypeStruct((2, tokens, half), jnp.bfloat16)
    out = pl.BlockSpec(
        (2, rows, half), lambda i, c, s: (0, lax.rem(i + c[0] * (count // 2), count), 0)
    )
    row = pl.BlockSpec((rows, width), lambda i, c, s: (i, 0))
    gain = pl.BlockSpec((1, width), lambda i, c, s: (0, 0))
    return pl.pallas_call(
        norm_kernel,
        grid_spec=pltpu.PrefetchScalarGridSpec(
            num_scalar_prefetch=2,
            grid=(count,),
            in_specs=[row, row, gain, gain],
            out_specs=[out, out],
            scratch_shapes=[pltpu.VMEM((rows, width), jnp.float32)],
        ),
        out_shape=[shape, shape],
        compiler_params=params(24, 1),
        cost_estimate=cost(10 * tokens * width, 8 * tokens * width),
        name="norm",
    )(core, timestep, clean, noise, gt, gc)


def project_kernel(a_ref, w_ref, top_ref, bottom_ref):
    value = jnp.dot(a_ref[0], w_ref[0], preferred_element_type=jnp.float32)
    rows = value.shape[0] // 2
    top_ref[0] = value[:rows]
    bottom_ref[0] = value[rows:]


def project(a, model, w):
    _, tokens, depth = a.shape
    kinds, _, panel = w.shape
    shape = jax.ShapeDtypeStruct((kinds, tokens // 2, panel), jnp.float32)
    out = pl.BlockSpec((1, tokens // 2, panel), lambda j: (j, 0, 0))
    return pl.pallas_call(
        project_kernel,
        grid=(kinds,),
        in_specs=[
            pl.BlockSpec((1, tokens, depth), lambda j: (model, 0, 0)),
            pl.BlockSpec((1, depth, panel), lambda j: (j, 0, 0)),
        ],
        out_specs=[out, out],
        out_shape=[shape, shape],
        compiler_params=params(24, 1),
        cost_estimate=cost(
            2 * tokens * depth * panel * kinds, 2 * depth * (tokens + panel * kinds)
        ),
        name="project",
    )(a, w)


def join_kernel(core_ref, *refs):
    out = refs[-1]
    core = core_ref[0]
    for model in range(2):
        own, own_more, other, other_more = refs[4 * model : 4 * model + 4]
        out[2 * model + core, 0] = (own[0] + own_more[0]).astype(jnp.bfloat16)
        out[2 * model + 1 - core, 0] = (other[0] + other_more[0]).astype(jnp.bfloat16)


def join(core, parts, first, kinds):
    _, rows, panel = parts[0].shape
    return pl.pallas_call(
        join_kernel,
        grid_spec=pltpu.PrefetchScalarGridSpec(
            num_scalar_prefetch=1,
            grid=(kinds,),
            in_specs=[
                pl.BlockSpec((1, rows, panel), lambda j, c: (first + j, 0, 0)) for _ in parts
            ],
            out_specs=pl.BlockSpec((4, 1, rows, panel), lambda j, c: (0, j, 0, 0)),
        ),
        out_shape=jax.ShapeDtypeStruct((4, kinds, rows, panel), jnp.bfloat16),
        compiler_params=params(24, 1),
        cost_estimate=cost(4 * rows * panel * kinds, 40 * rows * panel * kinds),
        name="join",
    )(core, *parts)


def attend_kernel(count, q_ref, *refs):
    keys, values, out = refs[:count], refs[count : 2 * count], refs[-1]
    groups, rows, _ = q_ref.shape
    factor = float(np.log2(np.e)) * HD**-0.5
    step = 2
    for g in range(0, groups, step):
        query = q_ref[g : g + step].reshape(step * rows, HD)
        scores = [
            lax.dot_general(
                query,
                k[...].reshape(-1, HD),
                (((1,), (1,)), ((), ())),
                preferred_element_type=jnp.float32,
            )
            for k in keys
        ]
        peak = jnp.max(scores[0], axis=-1, keepdims=True)
        for s in scores[1:]:
            peak = jnp.maximum(peak, jnp.max(s, axis=-1, keepdims=True))
        total = None
        summed = None
        for s, v in zip(scores, values):
            weights = jnp.exp2((s - peak) * factor)
            part = jnp.sum(weights, axis=-1, keepdims=True)
            product = jnp.dot(
                weights.astype(jnp.bfloat16),
                v[...].reshape(-1, HD),
                preferred_element_type=jnp.float32,
            )
            total = part if total is None else total + part
            summed = product if summed is None else summed + product
        out[g : g + step] = (summed / total).astype(jnp.bfloat16).reshape(step, rows, HD)


def attend(q, blocks):
    groups, _, rows, panel = q.shape
    heads = panel // HD
    count = len(blocks)
    length = sum(b.shape[0] * b.shape[2] for b in blocks)
    q_spec = pl.BlockSpec((groups, None, rows, HD), lambda h: (0, 0, 0, h))
    k_spec = pl.BlockSpec((groups, None, rows, HD), lambda h: (0, 0, 0, h))
    v_spec = pl.BlockSpec((groups, None, rows, HD), lambda h: (0, 1, 0, h))
    tokens = groups * rows
    return pl.pallas_call(
        lambda *refs: attend_kernel(count, *refs),
        grid=(heads,),
        in_specs=[q_spec] + [k_spec] * count + [v_spec] * count,
        out_specs=pl.BlockSpec((groups, rows, HD), lambda h: (0, 0, h)),
        out_shape=jax.ShapeDtypeStruct((groups, rows, panel), jnp.bfloat16),
        compiler_params=params(40, 1),
        cost_estimate=cost(
            4 * tokens * length * panel, 4 * panel * (tokens + length), tokens * length * heads
        ),
        name="attend",
    )(q, *blocks, *blocks)


def pick_kernel(place_ref, t_ref, c_ref, out_ref):
    out_ref[0] = t_ref[...]
    out_ref[1] = c_ref[...]


def pick(place, t, c):
    rows, width = t.shape
    part = width // Y
    spec = pl.BlockSpec((rows, part), lambda i, p: (0, p[0]))
    return pl.pallas_call(
        pick_kernel,
        grid_spec=pltpu.PrefetchScalarGridSpec(
            num_scalar_prefetch=1,
            grid=(1,),
            in_specs=[spec, spec],
            out_specs=pl.BlockSpec((2, rows, part), lambda i, p: (0, 0, 0)),
        ),
        out_shape=jax.ShapeDtypeStruct((2, rows, part), t.dtype),
        compiler_params=params(16, 1),
        cost_estimate=cost(0, 8 * rows * part),
        name="pick",
    )(place, t, c)


def finish_kernel(count, swap_ref, *refs):
    attn, mine, other = refs[:count], refs[count : 2 * count], refs[2 * count : 3 * count]
    keep_ref, send_ref = refs[-2:]

    def product(weights):
        total = None
        for a, w in zip(attn, weights):
            for model in range(2):
                left = a[2 * model : 2 * model + 2]
                left = left.reshape(-1, left.shape[-1])
                value = jnp.dot(left, w[model], preferred_element_type=jnp.float32)
                if total is None:
                    total = value
                else:
                    total = total + value if model == 0 else total - value
        return total

    first = product(mine)
    second = product(other)

    @pl.when(swap_ref[0] == 0)
    def _():
        keep_ref[...] = first
        send_ref[...] = second.astype(jnp.bfloat16)

    @pl.when(swap_ref[0] != 0)
    def _():
        keep_ref[...] = second
        send_ref[...] = first.astype(jnp.bfloat16)


def finish(swap, attn, mine, other):
    count = len(attn)
    _, rows, panel = attn[0].shape
    width = mine[0].shape[2]
    whole = pl.BlockSpec(memory_space=pltpu.VMEM)
    return pl.pallas_call(
        lambda *refs: finish_kernel(count, *refs),
        in_specs=[pl.BlockSpec(memory_space=pltpu.SMEM)] + [whole] * (3 * count),
        out_specs=[whole, whole],
        out_shape=[
            jax.ShapeDtypeStruct((2 * rows, width), jnp.float32),
            jax.ShapeDtypeStruct((2 * rows, width), jnp.bfloat16),
        ],
        compiler_params=params(40),
        cost_estimate=cost(
            16 * count * rows * panel * width, 8 * count * panel * width, 0
        ),
        name="finish",
    )(swap, *attn, *mine, *other)


def local(
    clean,
    noise,
    timestep,
    teacher_gain,
    critic_gain,
    teacher_qkv,
    critic_qkv,
    teacher_out,
    critic_out,
):
    core = lax.axis_index("dp")
    tp = lax.axis_index("tp")
    xh, y = tp // Y, tp % Y
    core_ref = core.reshape(1).astype(jnp.int32)

    mine = []
    for shift in range(Y):
        place = ((y + shift) % Y).reshape(1).astype(jnp.int32)
        block = pick(place, teacher_out, critic_out)
        mine.append(send(block, moved(y=shift)) if shift else block)
    other = [send(block, CORE) for block in mine]

    step = (timestep.astype(jnp.float32) + 1.0) / 1000.0
    level = 5.0 * step / (1.0 + 4.0 * step)
    other_level = send(level, CORE)

    keep, away = norm(
        core_ref,
        timestep,
        clean[0],
        noise[0],
        teacher_gain[None],
        critic_gain[None],
    )
    came = send(away, CORE)
    weights = [jnp.transpose(w, (1, 0, 2)) for w in (teacher_qkv, critic_qkv)]
    own = [project(keep, m, weights[m]) for m in range(2)]
    other_more = [send(own[m][1], CORE) for m in range(2)]
    cross = [project(came, m, weights[m]) for m in range(2)]
    own_more = [send(cross[m][0], CORE) for m in range(2)]
    parts = []
    for m in range(2):
        parts += [own[m][0], own_more[m], cross[m][1], other_more[m]]

    pair = over_z(join(core_ref, parts, 1, 2))
    pair_x = send(pair, moved(xl=1))
    query = over_z(join(core_ref, parts, 0, 1))
    pair_c = send(pair, CORE)
    pair_xc = send(pair_x, CORE)
    attn = over_z(attend(query, [pair, pair_c, pair_x, pair_xc]))

    gathered = [attn] + [send(attn, moved(y=shift)) for shift in range(1, Y)]
    kept, away = finish((core ^ xh).reshape(1).astype(jnp.int32), gathered, mine, other)
    value = kept + send(away, moved(xh=1)).astype(jnp.float32)
    rows = value.shape[0] // 2
    first, second = value[:rows], value[rows:]
    own_part = (level * jnp.where(core == 0, first, second)).astype(jnp.bfloat16)
    other_part = (other_level * jnp.where(core == 0, second, first)).astype(jnp.bfloat16)
    came_part = send(other_part, CORE)
    return jnp.where(
        core == 0,
        jnp.concatenate([own_part, came_part]),
        jnp.concatenate([came_part, own_part]),
    )[None]


def solution(mesh):
    placed = (
        P("dp", "ctx", None),
        P("dp", "ctx", None),
        P("dp"),
        P(),
        P(),
        P("dp", None, "tp"),
        P("dp", None, "tp"),
        P("tp", "dp"),
        P("tp", "dp"),
    )
    return jax.shard_map(
        local, mesh=mesh, in_specs=placed, out_specs=P("dp", "ctx", "tp"), check_vma=False
    )
```

```python
import jax
import jax.numpy as jnp
import numpy as np
from jax import lax
from jax.experimental import pallas as pl
from jax.experimental.pallas import tpu as pltpu
from jax.sharding import PartitionSpec as P

HD = 128
AXES = ("dp", "ctx", "tp")
Z, XL, XH, Y = 4, 2, 2, 4
MIB = 1024 * 1024


def moved(core=0, z=0, xl=0, xh=0, y=0):
    pairs = []
    for d in range(2):
        for a in range(Z):
            for b in range(XL):
                for e in range(XH):
                    for f in range(Y):
                        source = ((d * Z + a) * XL + b) * XH * Y + e * Y + f
                        target = (
                            (((d + core) % 2) * Z + (a + z) % Z) * XL + (b + xl) % XL
                        ) * XH * Y + ((e + xh) % XH) * Y + (f + y) % Y
                        pairs.append((source, target))
    return pairs


CORE = moved(core=1)


def send(value, pairs):
    return lax.ppermute(value, AXES, pairs)


Z_GROUPS = [[a * XL + b for a in range(Z)] for b in range(XL)]


def over_z(value):
    return lax.all_to_all(value, "ctx", 0, 0, axis_index_groups=Z_GROUPS, tiled=True)


def in_hbm(value):
    return pltpu.with_memory_space_constraint(value, pltpu.HBM)


def params(mib, grid=0):
    return pltpu.CompilerParams(
        vmem_limit_bytes=mib * MIB, dimension_semantics=("arbitrary",) * grid
    )


def cost(flops, size, exps=0):
    return pl.CostEstimate(flops=flops, bytes_accessed=size, transcendentals=exps)


def norm_kernel(
    core_ref, step_ref, clean_ref, noise_ref, gt_ref, gc_ref, w_ref,
    keep_ref, send_ref, held_ref,
    clean_buf, noise_buf, noisy_ref, keep_buf, send_buf, in_sem, out_sem, w_sem,
):
    tokens, width = clean_buf.shape
    rows = noisy_ref.shape[0]
    count = tokens // rows
    half = width // 2
    core = core_ref[0]

    def arrival(i):
        part = pl.ds(pl.multiple_of(i * rows, rows), rows)
        return (
            pltpu.make_async_copy(clean_ref.at[part], clean_buf.at[part], in_sem.at[0, i]),
            pltpu.make_async_copy(noise_ref.at[part], noise_buf.at[part], in_sem.at[1, i]),
        )

    def leaving(i):
        part = pl.ds(pl.multiple_of(i * rows, rows), rows)
        place = lax.rem(i + core * (count // 2), count)
        place = pl.ds(pl.multiple_of(place * rows, rows), rows)
        return (
            pltpu.make_async_copy(send_buf.at[:, part], send_ref.at[:, place], out_sem.at[0, i]),
            pltpu.make_async_copy(keep_buf.at[:, part], keep_ref.at[:, place], out_sem.at[1, i]),
        )

    held = [
        pltpu.make_async_copy(w_ref.at[j], held_ref.at[j], w_sem.at[j])
        for j in range(w_ref.shape[0])
    ]
    for i in range(count):
        for copy in arrival(i):
            copy.start()
    for copy in held:
        copy.start()
    step = (jnp.full((rows, 1), step_ref[0], jnp.int32).astype(jnp.float32) + 1.0) / 1000.0
    level = 5.0 * step / (1.0 + 4.0 * step)

    @pl.loop(0, count)
    def _(i):
        for copy in arrival(i):
            copy.wait()
        part = pl.ds(pl.multiple_of(i * rows, rows), rows)
        noisy = (1.0 - level) * clean_buf[part, :].astype(jnp.float32) + level * noise_buf[
            part, :
        ].astype(jnp.float32)
        noisy_ref[...] = noisy
        inverse = lax.rsqrt(jnp.mean(noisy * noisy, axis=-1, keepdims=True) + 1e-06)
        for out, which in ((send_buf, 1 - core), (keep_buf, core)):
            for t in range(half // HD):
                place = which * (half // HD) + t
                columns = pl.ds(pl.multiple_of(place * HD, HD), HD)
                scaled = noisy_ref[:, columns] * inverse
                out[0, part, t * HD : (t + 1) * HD] = (
                    scaled * gt_ref[pl.ds(place, 1), :]
                ).astype(jnp.bfloat16)
                out[1, part, t * HD : (t + 1) * HD] = (
                    scaled * gc_ref[pl.ds(place, 1), :]
                ).astype(jnp.bfloat16)
        for copy in leaving(i):
            copy.start()

    for i in range(count):
        for copy in leaving(i):
            copy.wait()
    for copy in held:
        copy.wait()


def norm(core, timestep, clean, noise, gt, gc, w):
    tokens, width = clean.shape
    rows = 32
    count = tokens // rows
    half = width // 2
    shape = jax.ShapeDtypeStruct((2, tokens, half), jnp.bfloat16)
    scalar = pl.BlockSpec(memory_space=pltpu.SMEM)
    far = pl.BlockSpec(memory_space=pltpu.HBM)
    anywhere = pl.BlockSpec(memory_space=pl.ANY)
    near = pl.BlockSpec(memory_space=pltpu.VMEM)
    return pl.pallas_call(
        norm_kernel,
        in_specs=[scalar, scalar, far, far, near, near, far],
        out_specs=[anywhere, anywhere, anywhere],
        scratch_shapes=[
            pltpu.VMEM((tokens, width), jnp.bfloat16),
            pltpu.VMEM((tokens, width), jnp.bfloat16),
            pltpu.VMEM((rows, width), jnp.float32),
            pltpu.VMEM((2, tokens, half), jnp.bfloat16),
            pltpu.VMEM((2, tokens, half), jnp.bfloat16),
            pltpu.SemaphoreType.DMA((2, count)),
            pltpu.SemaphoreType.DMA((2, count)),
            pltpu.SemaphoreType.DMA((w.shape[0],)),
        ],
        out_shape=[shape, shape, jax.ShapeDtypeStruct(w.shape, w.dtype)],
        compiler_params=params(24),
        cost_estimate=cost(10 * tokens * width, 8 * tokens * width),
        name="norm",
    )(core, timestep, clean, noise, gt, gc, w)


def project_kernel(copies, carried, made, *refs):
    inputs, outputs, sem = refs[: 2 + carried], refs[2 + carried : -1], refs[-1]
    a_ref, w_ref = inputs[:2]
    top_ref, bottom_ref = outputs[:2]
    j = pl.program_id(0)
    moves = copies(inputs[2:], outputs[2:], sem) if made else []

    @pl.when(j == 0)
    def _():
        for copy in moves:
            copy.start()

    value = jnp.dot(a_ref[0], w_ref[0], preferred_element_type=jnp.float32)
    rows = value.shape[0] // 2
    top_ref[0] = value[:rows]
    bottom_ref[0] = value[rows:]

    @pl.when(j == pl.num_programs(0) - 1)
    def _():
        for copy in moves:
            copy.wait()


def project(a, model, w, copies=None, given=(), specs=(), made=()):
    _, tokens, depth = a.shape
    kinds, _, panel = w.shape
    shape = jax.ShapeDtypeStruct((kinds, tokens // 2, panel), jnp.float32)
    out = pl.BlockSpec((1, tokens // 2, panel), lambda j: (j, 0, 0))
    anywhere = pl.BlockSpec(memory_space=pl.ANY)
    return pl.pallas_call(
        lambda *refs: project_kernel(copies, len(given), len(made), *refs),
        grid=(kinds,),
        in_specs=[
            pl.BlockSpec((1, tokens, depth), lambda j: (model, 0, 0)),
            pl.BlockSpec((1, depth, panel), lambda j: (j, 0, 0)),
        ]
        + list(specs),
        out_specs=[out, out] + [anywhere] * len(made),
        out_shape=[shape, shape] + list(made),
        scratch_shapes=[pltpu.SemaphoreType.DMA((8,))],
        compiler_params=params(24, 1),
        cost_estimate=cost(
            2 * tokens * depth * panel * kinds, 2 * depth * (tokens + panel * kinds)
        ),
        name="project",
    )(a, w, *given)


def hold_copies(given, made, sem):
    return [
        pltpu.make_async_copy(given[0].at[j], made[0].at[j], sem.at[j])
        for j in range(given[0].shape[0])
    ]


def pick_copies(given, made, sem):
    y_ref, *sources = given
    part = made[0].shape[2]
    moves = []
    for shift in range(1, Y):
        place = lax.rem(y_ref[0] + shift, Y)
        columns = pl.ds(pl.multiple_of(place * part, 128), part)
        for model in range(2):
            moves.append(
                pltpu.make_async_copy(
                    sources[model].at[:, columns],
                    made[shift - 1].at[model],
                    sem.at[2 * (shift - 1) + model],
                )
            )
    return moves


def join_kernel(core_ref, *refs):
    out = refs[-1]
    core = core_ref[0]
    for model in range(2):
        own, own_more, other, other_more = refs[4 * model : 4 * model + 4]
        out[2 * model + core, 0] = (own[0] + own_more[0]).astype(jnp.bfloat16)
        out[2 * model + 1 - core, 0] = (other[0] + other_more[0]).astype(jnp.bfloat16)


def join(core, parts, first, kinds):
    _, rows, panel = parts[0].shape
    return pl.pallas_call(
        join_kernel,
        grid_spec=pltpu.PrefetchScalarGridSpec(
            num_scalar_prefetch=1,
            grid=(kinds,),
            in_specs=[
                pl.BlockSpec((1, rows, panel), lambda j, c: (first + j, 0, 0)) for _ in parts
            ],
            out_specs=pl.BlockSpec((4, 1, rows, panel), lambda j, c: (0, j, 0, 0)),
        ),
        out_shape=jax.ShapeDtypeStruct((4, kinds, rows, panel), jnp.bfloat16),
        compiler_params=params(24, 1),
        cost_estimate=cost(4 * rows * panel * kinds, 40 * rows * panel * kinds),
        name="join",
    )(core, *parts)


def attend_kernel(count, q_ref, *refs):
    keys, values, out = refs[:count], refs[count : 2 * count], refs[-1]
    groups, rows, _ = q_ref.shape
    factor = float(np.log2(np.e)) * HD**-0.5
    step = 2
    for g in range(0, groups, step):
        query = q_ref[g : g + step].reshape(step * rows, HD)
        scores = [
            lax.dot_general(
                query,
                k[...].reshape(-1, HD),
                (((1,), (1,)), ((), ())),
                preferred_element_type=jnp.float32,
            )
            for k in keys
        ]
        peak = jnp.max(scores[0], axis=-1, keepdims=True)
        for s in scores[1:]:
            peak = jnp.maximum(peak, jnp.max(s, axis=-1, keepdims=True))
        total = None
        summed = None
        for s, v in zip(scores, values):
            weights = jnp.exp2((s - peak) * factor)
            part = jnp.sum(weights, axis=-1, keepdims=True)
            product = jnp.dot(
                weights.astype(jnp.bfloat16),
                v[...].reshape(-1, HD),
                preferred_element_type=jnp.float32,
            )
            total = part if total is None else total + part
            summed = product if summed is None else summed + product
        out[g : g + step] = (summed / total).astype(jnp.bfloat16).reshape(step, rows, HD)


def attend(q, blocks):
    groups, _, rows, panel = q.shape
    heads = panel // HD
    count = len(blocks)
    length = sum(b.shape[0] * b.shape[2] for b in blocks)
    q_spec = pl.BlockSpec((groups, None, rows, HD), lambda h: (0, 0, 0, h))
    k_spec = pl.BlockSpec((groups, None, rows, HD), lambda h: (0, 0, 0, h))
    v_spec = pl.BlockSpec((groups, None, rows, HD), lambda h: (0, 1, 0, h))
    tokens = groups * rows
    return pl.pallas_call(
        lambda *refs: attend_kernel(count, *refs),
        grid=(heads,),
        in_specs=[q_spec] + [k_spec] * count + [v_spec] * count,
        out_specs=pl.BlockSpec((groups, rows, HD), lambda h: (0, 0, h)),
        out_shape=jax.ShapeDtypeStruct((groups, rows, panel), jnp.bfloat16),
        compiler_params=params(40, 1),
        cost_estimate=cost(
            4 * tokens * length * panel, 4 * panel * (tokens + length), tokens * length * heads
        ),
        name="attend",
    )(q, *blocks, *blocks)


def pick_kernel(place_ref, t_ref, c_ref, out_ref):
    out_ref[0] = t_ref[...]
    out_ref[1] = c_ref[...]


def pick(place, t, c):
    rows, width = t.shape
    part = width // Y
    spec = pl.BlockSpec((rows, part), lambda i, p: (0, p[0]))
    return pl.pallas_call(
        pick_kernel,
        grid_spec=pltpu.PrefetchScalarGridSpec(
            num_scalar_prefetch=1,
            grid=(1,),
            in_specs=[spec, spec],
            out_specs=pl.BlockSpec((2, rows, part), lambda i, p: (0, 0, 0)),
        ),
        out_shape=jax.ShapeDtypeStruct((2, rows, part), t.dtype),
        compiler_params=params(16, 1),
        cost_estimate=cost(0, 8 * rows * part),
        name="pick",
    )(place, t, c)


def finish_kernel(count, swap_ref, *refs):
    attn, mine, other = refs[:count], refs[count : 2 * count], refs[2 * count : 3 * count]
    keep_ref, send_ref = refs[-2:]

    def product(weights):
        total = None
        for a, w in zip(attn, weights):
            for model in range(2):
                left = a[2 * model : 2 * model + 2]
                left = left.reshape(-1, left.shape[-1])
                value = jnp.dot(left, w[model], preferred_element_type=jnp.float32)
                if total is None:
                    total = value
                else:
                    total = total + value if model == 0 else total - value
        return total

    first = product(mine)
    second = product(other)

    @pl.when(swap_ref[0] == 0)
    def _():
        keep_ref[...] = first
        send_ref[...] = second.astype(jnp.bfloat16)

    @pl.when(swap_ref[0] != 0)
    def _():
        keep_ref[...] = second
        send_ref[...] = first.astype(jnp.bfloat16)


def finish(swap, attn, mine, other):
    count = len(attn)
    _, rows, panel = attn[0].shape
    width = mine[0].shape[2]
    whole = pl.BlockSpec(memory_space=pltpu.VMEM)
    return pl.pallas_call(
        lambda *refs: finish_kernel(count, *refs),
        in_specs=[pl.BlockSpec(memory_space=pltpu.SMEM)] + [whole] * (3 * count),
        out_specs=[whole, whole],
        out_shape=[
            jax.ShapeDtypeStruct((2 * rows, width), jnp.float32),
            jax.ShapeDtypeStruct((2 * rows, width), jnp.bfloat16),
        ],
        compiler_params=params(40),
        cost_estimate=cost(
            16 * count * rows * panel * width, 8 * count * panel * width, 0
        ),
        name="finish",
    )(swap, *attn, *mine, *other)


def local(
    clean,
    noise,
    timestep,
    teacher_gain,
    critic_gain,
    teacher_qkv,
    critic_qkv,
    teacher_out,
    critic_out,
):
    core = lax.axis_index("dp")
    tp = lax.axis_index("tp")
    xh, y = tp // Y, tp % Y
    core_ref = core.reshape(1).astype(jnp.int32)

    step = (timestep.astype(jnp.float32) + 1.0) / 1000.0
    level = 5.0 * step / (1.0 + 4.0 * step)
    other_level = send(level, CORE)

    weights = [in_hbm(jnp.transpose(w, (1, 0, 2))) for w in (teacher_qkv, critic_qkv)]
    teacher_out, critic_out = in_hbm(teacher_out), in_hbm(critic_out)
    tiles = (teacher_gain.shape[0] // HD, HD)
    keep, away, weights_t = norm(
        core_ref,
        timestep,
        in_hbm(clean[0]),
        in_hbm(noise[0]),
        teacher_gain.reshape(tiles),
        critic_gain.reshape(tiles),
        weights[0],
    )
    came = send(away, CORE)
    far = pl.BlockSpec(memory_space=pltpu.HBM)
    scalar = pl.BlockSpec(memory_space=pltpu.SMEM)
    held = jax.ShapeDtypeStruct(weights[1].shape, weights[1].dtype)
    *own_t, weights_c = project(keep, 0, weights_t, hold_copies, (weights[1],), (far,), (held,))
    y_ref = y.reshape(1).astype(jnp.int32)
    rows, columns = teacher_out.shape
    block = jax.ShapeDtypeStruct((2, rows, columns // Y), teacher_out.dtype)
    *own_c, block_1, block_2, block_3 = project(
        keep,
        1,
        weights_c,
        pick_copies,
        (y_ref, teacher_out, critic_out),
        (scalar, far, far),
        (block,) * 3,
    )
    mine = [send(block_1, moved(y=1)), None, send(block_3, moved(y=3))]
    weights = [weights_t, weights_c]
    own = [own_t, own_c]
    other_more = [send(own[m][1], CORE) for m in range(2)]
    cross = [project(came, m, weights[m]) for m in range(2)]
    own_more = [send(cross[m][0], CORE) for m in range(2)]
    parts = []
    for m in range(2):
        parts += [own[m][0], own_more[m], cross[m][1], other_more[m]]

    pair = over_z(join(core_ref, parts, 1, 2))
    pair_x = send(pair, moved(xl=1))
    parts[0], mine[0], mine[2], block_2 = lax.optimization_barrier(
        (parts[0], mine[0], mine[2], block_2)
    )
    mine[1] = send(block_2, moved(y=2))
    query = over_z(join(core_ref, parts, 0, 1))
    pair_c = send(pair, CORE)
    pair_xc = send(pair_x, CORE)
    attn = over_z(attend(query, [pair, pair_c, pair_x, pair_xc]))
    attn, mine[1] = lax.optimization_barrier((attn, mine[1]))
    mine = [pick(y_ref, teacher_out, critic_out)] + mine
    other = [send(block, CORE) for block in mine]

    gathered = [attn] + [send(attn, moved(y=shift)) for shift in range(1, Y)]
    kept, away = finish((core ^ xh).reshape(1).astype(jnp.int32), gathered, mine, other)
    value = kept + send(away, moved(xh=1)).astype(jnp.float32)
    rows = value.shape[0] // 2
    first, second = value[:rows], value[rows:]
    own_part = (level * jnp.where(core == 0, first, second)).astype(jnp.bfloat16)
    other_part = (other_level * jnp.where(core == 0, second, first)).astype(jnp.bfloat16)
    came_part = send(other_part, CORE)
    return jnp.where(
        core == 0,
        jnp.concatenate([own_part, came_part]),
        jnp.concatenate([came_part, own_part]),
    )[None]


def solution(mesh):
    placed = (
        P("dp", "ctx", None),
        P("dp", "ctx", None),
        P("dp"),
        P(),
        P(),
        P("dp", None, "tp"),
        P("dp", None, "tp"),
        P("tp", "dp"),
        P("tp", "dp"),
    )
    return jax.shard_map(
        local, mesh=mesh, in_specs=placed, out_specs=P("dp", "ctx", "tp"), check_vma=False
    )
```

```python
import jax
import jax.numpy as jnp
import numpy as np
from jax import lax
from jax.experimental import pallas as pl
from jax.experimental.pallas import tpu as pltpu
from jax.sharding import PartitionSpec as P

HD = 128
AXES = ("dp", "ctx", "tp")
Z, XL, XH, Y = 4, 2, 2, 4
MIB = 1024 * 1024


def moved(core=0, z=0, xl=0, xh=0, y=0):
    pairs = []
    for d in range(2):
        for a in range(Z):
            for b in range(XL):
                for e in range(XH):
                    for f in range(Y):
                        source = ((d * Z + a) * XL + b) * XH * Y + e * Y + f
                        target = (
                            (((d + core) % 2) * Z + (a + z) % Z) * XL + (b + xl) % XL
                        ) * XH * Y + ((e + xh) % XH) * Y + (f + y) % Y
                        pairs.append((source, target))
    return pairs


CORE = moved(core=1)


def send(value, pairs):
    return lax.ppermute(value, AXES, pairs)


def over_ctx(value):
    return lax.all_to_all(value, "ctx", 0, 0, tiled=True)


def in_hbm(value):
    return pltpu.with_memory_space_constraint(value, pltpu.HBM)


def in_vmem(value):
    return pltpu.with_memory_space_constraint(value, pltpu.VMEM)


SCALAR = pl.BlockSpec(memory_space=pltpu.SMEM)
NEAR = pl.BlockSpec(memory_space=pltpu.VMEM)
ANYWHERE = pl.BlockSpec(memory_space=pl.ANY)


def kernel(body, name, scalars, far, near, made, mib, flops, size, exps=0, scratch=()):
    return pl.pallas_call(
        body,
        in_specs=[SCALAR] * len(scalars) + [ANYWHERE] * len(far) + [NEAR] * len(near),
        out_specs=[NEAR] * len(made),
        out_shape=[pltpu.VMEM(shape, dtype) for shape, dtype in made],
        scratch_shapes=list(scratch),
        compiler_params=pltpu.CompilerParams(vmem_limit_bytes=mib * MIB),
        cost_estimate=pl.CostEstimate(flops=flops, bytes_accessed=size, transcendentals=exps),
        name=name,
    )(
        *[x.reshape(1).astype(jnp.int32) for x in scalars],
        *[in_hbm(x) for x in far],
        *[in_vmem(x) for x in near],
    )


BF16, F32 = jnp.bfloat16, jnp.float32


def pick_copies(y_ref, sources, made, first, sem):
    part = made[0].shape[2]
    moves = []
    for shift, target in enumerate(made, first):
        place = lax.rem(y_ref[0] + shift, Y)
        columns = pl.ds(pl.multiple_of(place * part, 128), part)
        for model in range(2):
            moves.append(
                pltpu.make_async_copy(
                    sources[model].at[:, columns], target.at[model], sem.at[2 * shift + model]
                )
            )
    return moves


def picked(out):
    rows, columns = out.shape
    return ((2, rows, columns // Y), out.dtype)


def norm_kernel(
    core_ref, step_ref, y_ref, clean_ref, noise_ref, gt_ref, gc_ref, w_ref, ot_ref, oc_ref,
    keep_ref, send_ref, held_ref, block_1, block_2, block_3,
    clean_buf, noise_buf, noisy_ref, gt_buf, gc_buf, in_sem, w_sem, pick_sem,
):
    tokens, width = clean_buf.shape
    rows = noisy_ref.shape[0]
    count = tokens // rows
    half = width // 2
    core = core_ref[0]

    def arrival(i):
        part = pl.ds(pl.multiple_of(i * rows, rows), rows)
        return (
            pltpu.make_async_copy(clean_ref.at[part], clean_buf.at[part], in_sem.at[0, i]),
            pltpu.make_async_copy(noise_ref.at[part], noise_buf.at[part], in_sem.at[1, i]),
        )

    kinds = w_ref.shape[0]
    held = [
        pltpu.make_async_copy(w_ref.at[j], held_ref.at[j], w_sem.at[j]) for j in range(kinds)
    ]
    gains = [
        pltpu.make_async_copy(gt_ref, gt_buf, w_sem.at[kinds]),
        pltpu.make_async_copy(gc_ref, gc_buf, w_sem.at[kinds + 1]),
    ]
    for copy in gains:
        copy.start()
    for i in range(count):
        for copy in arrival(i):
            copy.start()
    held += pick_copies(y_ref, (ot_ref, oc_ref), (block_1, block_2, block_3), 1, pick_sem)
    for copy in held[kinds:] + held[:kinds]:
        copy.start()
    step = (jnp.full((rows, 1), step_ref[0], jnp.int32).astype(F32) + 1.0) / 1000.0
    level = 5.0 * step / (1.0 + 4.0 * step)
    for copy in gains:
        copy.wait()

    @pl.loop(0, count)
    def _(i):
        for copy in arrival(i):
            copy.wait()
        part = pl.ds(pl.multiple_of(i * rows, rows), rows)
        noisy = (1.0 - level) * clean_buf[part, :].astype(F32) + level * noise_buf[
            part, :
        ].astype(F32)
        noisy_ref[...] = noisy
        inverse = lax.rsqrt(jnp.mean(noisy * noisy, axis=-1, keepdims=True) + 1e-06)
        place = lax.rem(i + core * (count // 2), count)
        place = pl.ds(pl.multiple_of(place * rows, rows), rows)
        for out, which in ((send_ref, 1 - core), (keep_ref, core)):
            for t in range(half // HD):
                tile = which * (half // HD) + t
                columns = pl.ds(pl.multiple_of(tile * HD, HD), HD)
                scaled = noisy_ref[:, columns] * inverse
                out[0, place, t * HD : (t + 1) * HD] = (
                    scaled * gt_buf[pl.ds(tile, 1), :]
                ).astype(BF16)
                out[1, place, t * HD : (t + 1) * HD] = (
                    scaled * gc_buf[pl.ds(tile, 1), :]
                ).astype(BF16)

    for copy in held:
        copy.wait()


def norm(core, timestep, y, clean, noise, gt, gc, w, ot, oc):
    tokens, width = clean.shape
    rows = 32
    count = tokens // rows
    tiles = (width // HD, HD)
    shape = ((2, tokens, width // 2), BF16)
    return kernel(
        norm_kernel,
        "norm",
        (core, timestep, y),
        (clean, noise, gt.reshape(tiles), gc.reshape(tiles), w, ot, oc),
        (),
        (shape, shape, (w.shape, w.dtype)) + (picked(ot),) * (Y - 1),
        16,
        10 * tokens * width,
        8 * tokens * width,
        scratch=(
            pltpu.VMEM((tokens, width), BF16),
            pltpu.VMEM((tokens, width), BF16),
            pltpu.VMEM((rows, width), F32),
            pltpu.VMEM(tiles, F32),
            pltpu.VMEM(tiles, F32),
            pltpu.SemaphoreType.DMA((2, count)),
            pltpu.SemaphoreType.DMA((w.shape[0] + 2,)),
            pltpu.SemaphoreType.DMA((2 * Y,)),
        ),
    )


def project(model, a, w, copies=None, scalars=(), far=(), made=()):
    _, tokens, depth = a.shape
    kinds, _, panel = w.shape
    first = len(scalars) + len(far)

    def body(*refs):
        a_ref, w_ref, top_ref, bottom_ref = refs[first : first + 4]
        moves = copies(refs[:first], refs[first + 4 : -1], refs[-1]) if copies else []
        for copy in moves:
            copy.start()
        for j in range(kinds):
            value = jnp.dot(a_ref[model], w_ref[j], preferred_element_type=F32)
            top_ref[j] = value[: tokens // 2]
            bottom_ref[j] = value[tokens // 2 :]
        for copy in moves:
            copy.wait()

    shape = ((kinds, tokens // 2, panel), F32)
    return kernel(
        body,
        "project",
        scalars,
        far,
        (a, w),
        (shape, shape) + tuple(made),
        16,
        2 * tokens * depth * panel * kinds,
        2 * depth * (tokens + panel * kinds),
        scratch=(pltpu.SemaphoreType.DMA((8,)),),
    )


def hold_copies(given, made, sem):
    return [
        pltpu.make_async_copy(given[0].at[j], made[0].at[j], sem.at[j])
        for j in range(given[0].shape[0])
    ]


UNITS = 8


def join(core, parts):
    _, rows, panel = parts[0].shape
    half = rows // 2

    def body(core_ref, *refs):
        inputs, out = refs[:-1], refs[-1]
        for model in range(2):
            for which in range(2):
                left, right = inputs[4 * model + 2 * which : 4 * model + 2 * which + 2]
                clip = core_ref[0] if which == 0 else 1 - core_ref[0]
                unit = (2 * model + clip) * 2
                for kind, base in ((1, 0), (2, 2 * rows), (0, 4 * rows)):
                    value = (left[kind] + right[kind]).astype(BF16)
                    for j in range(2):
                        out[unit + j, base : base + rows] = value[
                            :, 2 * j * HD : (2 * j + 1) * HD
                        ]
                        middle = value[:, HD : 2 * HD]
                        if kind == 0:
                            middle = middle[j * half : (j + 1) * half]
                        out[unit + j, base + rows : base + rows + middle.shape[0]] = middle

    return kernel(
        body,
        "join",
        (core,),
        (),
        parts,
        (((UNITS, 5 * rows + half, HD), BF16),),
        8,
        12 * rows * panel,
        120 * rows * panel,
    )[0]


FACTOR = float(np.log2(np.e)) * HD**-0.5


def attend(queries, pairs, state=None):
    _, size, _ = queries.shape
    half = size // 11
    rows = 2 * half
    tokens, length = 3 * half * UNITS, rows * UNITS
    step = 256

    def body(*refs):
        q_ref, kv_ref = refs[:2]
        before, out = refs[2:-3], refs[-3:]
        if state is not None:
            before, out = refs[2:5], refs[5:]
        done = 0
        for middle, held in ((0, rows), (1, half)):
            keys = kv_ref[:, middle * rows : (middle + 1) * rows].reshape(length, HD)
            values = kv_ref[:, (2 + middle) * rows : (3 + middle) * rows].reshape(length, HD)
            several = step // held
            for g in range(0, UNITS, several):
                place = slice(done, done + step)
                done += step
                start = (4 + middle) * rows
                query = q_ref[g : g + several, start : start + held].reshape(step, HD)
                score = lax.dot_general(
                    query, keys, (((1,), (1,)), ((), ())), preferred_element_type=F32
                )
                peak = jnp.max(score, axis=-1, keepdims=True)
                if state is not None:
                    old = before[0][place, :1]
                    peak = jnp.maximum(peak, old)
                weights = jnp.exp2((score - peak) * FACTOR)
                total = jnp.sum(weights, axis=-1, keepdims=True)
                summed = jnp.dot(weights.astype(BF16), values, preferred_element_type=F32)
                if state is None:
                    out[0][place, :] = jnp.broadcast_to(peak, (step, HD))
                    out[1][place, :] = jnp.broadcast_to(total, (step, HD))
                    out[2][place, :] = summed
                else:
                    scale = jnp.exp2((old - peak) * FACTOR)
                    total = total + before[1][place, :1] * scale
                    summed = summed + before[2][place, :] * scale
                    out[0][g : g + several, middle * rows : middle * rows + held] = (
                        (summed / total).astype(BF16).reshape(several, held, HD)
                    )

    if state is None:
        made = (((tokens, HD), F32),) * 3
    else:
        made = (((UNITS, 3 * half, HD), BF16),)
    return kernel(
        body,
        "attend",
        (),
        (),
        (queries, pairs, *(state or ())),
        made,
        24,
        4 * tokens * length * HD,
        4 * HD * (tokens + length),
        tokens * length,
    )


def finish(swap, attn, mine, other, dtype):
    count = len(attn)
    _, size, _ = attn[0].shape
    half = size // 3
    rows, panel = 2 * half, 3 * HD
    width = mine[0].shape[2]

    def body(swap_ref, *refs):
        out = refs[-1]

        def heads(a, model, clip):
            unit = (2 * model + clip) * 2
            middle = jnp.concatenate([a[unit, rows:], a[unit + 1, rows:]])
            return jnp.concatenate([a[unit, :rows], middle, a[unit + 1, :rows]], axis=1)

        lefts = [
            jnp.concatenate(
                [
                    jnp.concatenate([heads(a, 0, clip), -heads(a, 1, clip)], axis=1)
                    for clip in range(2)
                ]
            )
            for a in refs[:count]
        ]

        def product(weights):
            total = None
            for left, w in zip(lefts, weights):
                value = jnp.dot(
                    left, w[...].reshape(2 * panel, width), preferred_element_type=F32
                )
                total = value if total is None else total + value
            out[...] = total.astype(dtype)

        @pl.when(swap_ref[0] == 0)
        def _():
            product(refs[count : 2 * count])

        @pl.when(swap_ref[0] != 0)
        def _():
            product(refs[2 * count : 3 * count])

    return kernel(
        body,
        "finish",
        (swap,),
        (),
        (*attn, *mine, *other),
        (((2 * rows, width), dtype),),
        24,
        8 * count * rows * panel * width,
        4 * count * panel * width,
    )[0]


def local(
    clean,
    noise,
    timestep,
    teacher_gain,
    critic_gain,
    teacher_qkv,
    critic_qkv,
    teacher_out,
    critic_out,
):
    core = lax.axis_index("dp")
    tp = lax.axis_index("tp")
    xh, y = tp // Y, tp % Y

    step = (timestep.astype(F32) + 1.0) / 1000.0
    level = 5.0 * step / (1.0 + 4.0 * step)
    other_level = send(level, CORE)

    weights = [jnp.transpose(w, (1, 0, 2)) for w in (teacher_qkv, critic_qkv)]
    keep, away, weights_t, *blocks = norm(
        core,
        timestep,
        y,
        clean[0],
        noise[0],
        teacher_gain,
        critic_gain,
        weights[0],
        teacher_out,
        critic_out,
    )
    mine = [send(block, moved(y=shift)) for shift, block in enumerate(blocks, 1)]
    came = send(away, CORE)
    came, other_level = lax.optimization_barrier((came, other_level))
    *own_t, weights_c = project(
        0, keep, weights_t, hold_copies, far=(weights[1],),
        made=((weights[1].shape, BF16),),
    )
    *own_c, block_0 = project(
        1,
        keep,
        weights_c,
        lambda given, made, sem: pick_copies(given[0], given[1:], made, 0, sem),
        (y,),
        (teacher_out, critic_out),
        (picked(teacher_out),),
    )
    mine = [block_0] + mine
    held = [weights_t, weights_c]
    own = [own_t, own_c]
    other_more = [send(own[m][1], CORE) for m in range(2)]
    cross = [project(m, came, held[m]) for m in range(2)]
    own_more = [send(cross[m][0], CORE) for m in range(2)]
    parts = []
    for m in range(2):
        parts += [own[m][0], own_more[m], cross[m][1], other_more[m]]

    block = over_ctx(join(core, parts))
    state = list(attend(block, block))
    state[0], *mine[1:] = lax.optimization_barrier((state[0], *mine[1:]))
    attn = over_ctx(attend(block, send(block, CORE), state)[0])
    other = [send(block, CORE) for block in mine]
    gathered = [attn] + [send(attn, moved(y=shift)) for shift in range(1, Y)]
    swap = core ^ xh
    away = finish(1 - swap, gathered, mine, other, BF16)
    kept = finish(swap, gathered, mine, other, F32)
    value = kept + send(away, moved(xh=1)).astype(F32)
    rows = value.shape[0] // 2
    first, second = value[:rows], value[rows:]
    own_part = (level * jnp.where(core == 0, first, second)).astype(BF16)
    other_part = (other_level * jnp.where(core == 0, second, first)).astype(BF16)
    came_part = send(other_part, CORE)
    return jnp.where(
        core == 0,
        jnp.concatenate([own_part, came_part]),
        jnp.concatenate([came_part, own_part]),
    )[None]


def solution(mesh):
    placed = (
        P("dp", "ctx", None),
        P("dp", "ctx", None),
        P("dp"),
        P(),
        P(),
        P("dp", None, "tp"),
        P("dp", None, "tp"),
        P("tp", "dp"),
        P("tp", "dp"),
    )
    return jax.shard_map(
        local, mesh=mesh, in_specs=placed, out_specs=P("dp", "ctx", "tp"), check_vma=False
    )
```

```python
import jax
import jax.numpy as jnp
import numpy as np
from jax import lax
from jax.experimental import pallas as pl
from jax.experimental.pallas import tpu as pltpu
from jax.sharding import PartitionSpec as P

HD = 128
AXES = ("dp", "ctx", "tp")
Z, XL, XH, Y = 4, 2, 2, 4
MIB = 1024 * 1024


def moved(core=0, z=0, xl=0, xh=0, y=0):
    pairs = []
    for d in range(2):
        for a in range(Z):
            for b in range(XL):
                for e in range(XH):
                    for f in range(Y):
                        source = ((d * Z + a) * XL + b) * XH * Y + e * Y + f
                        target = (
                            (((d + core) % 2) * Z + (a + z) % Z) * XL + (b + xl) % XL
                        ) * XH * Y + ((e + xh) % XH) * Y + (f + y) % Y
                        pairs.append((source, target))
    return pairs


CORE = moved(core=1)


def send(value, pairs):
    return lax.ppermute(value, AXES, pairs)


def over_ctx(value):
    return lax.all_to_all(value, "ctx", 0, 0, tiled=True)


def in_hbm(value):
    return pltpu.with_memory_space_constraint(value, pltpu.HBM)


def in_vmem(value):
    return pltpu.with_memory_space_constraint(value, pltpu.VMEM)


SCALAR = pl.BlockSpec(memory_space=pltpu.SMEM)
NEAR = pl.BlockSpec(memory_space=pltpu.VMEM)
ANYWHERE = pl.BlockSpec(memory_space=pl.ANY)


def kernel(body, name, scalars, far, near, made, mib, flops, size, exps=0, scratch=(), loose=()):
    return pl.pallas_call(
        body,
        in_specs=[SCALAR] * len(scalars) + [ANYWHERE] * len(far) + [NEAR] * len(near),
        out_specs=[NEAR] * len(made) + [ANYWHERE] * len(loose),
        out_shape=[pltpu.VMEM(shape, dtype) for shape, dtype in made]
        + [jax.ShapeDtypeStruct(shape, dtype) for shape, dtype in loose],
        scratch_shapes=list(scratch),
        compiler_params=pltpu.CompilerParams(vmem_limit_bytes=mib * MIB),
        cost_estimate=pl.CostEstimate(flops=flops, bytes_accessed=size, transcendentals=exps),
        name=name,
    )(
        *[x.reshape(1).astype(jnp.int32) for x in scalars],
        *far,
        *[in_vmem(x) for x in near],
    )


BF16, F32 = jnp.bfloat16, jnp.float32


def norm_kernel(
    core_ref, step_ref, clean_ref, noise_ref, gt_ref, gc_ref, w_ref,
    keep_ref, send_ref, held_ref,
    clean_buf, noise_buf, noisy_ref, gt_buf, gc_buf, in_sem, w_sem,
):
    tokens, width = clean_buf.shape
    rows = noisy_ref.shape[0]
    count = tokens // rows
    half = width // 2
    core = core_ref[0]

    def arrival(i):
        part = pl.ds(pl.multiple_of(i * rows, rows), rows)
        return (
            pltpu.make_async_copy(clean_ref.at[part], clean_buf.at[part], in_sem.at[0, i]),
            pltpu.make_async_copy(noise_ref.at[part], noise_buf.at[part], in_sem.at[1, i]),
        )

    kinds = w_ref.shape[0]
    held = [
        pltpu.make_async_copy(w_ref.at[j], held_ref.at[j], w_sem.at[j]) for j in range(kinds)
    ]
    gains = [
        pltpu.make_async_copy(gt_ref, gt_buf, w_sem.at[kinds]),
        pltpu.make_async_copy(gc_ref, gc_buf, w_sem.at[kinds + 1]),
    ]
    for copy in gains:
        copy.start()
    for i in range(count):
        for copy in arrival(i):
            copy.start()
    for copy in held:
        copy.start()
    step = (jnp.full((rows, 1), step_ref[0], jnp.int32).astype(F32) + 1.0) / 1000.0
    level = 5.0 * step / (1.0 + 4.0 * step)
    for copy in gains:
        copy.wait()

    @pl.loop(0, count)
    def _(i):
        for copy in arrival(i):
            copy.wait()
        part = pl.ds(pl.multiple_of(i * rows, rows), rows)
        noisy = (1.0 - level) * clean_buf[part, :].astype(F32) + level * noise_buf[
            part, :
        ].astype(F32)
        noisy_ref[...] = noisy
        inverse = lax.rsqrt(jnp.mean(noisy * noisy, axis=-1, keepdims=True) + 1e-06)
        place = lax.rem(i + core * (count // 2), count)
        place = pl.ds(pl.multiple_of(place * rows, rows), rows)
        for out, which in ((send_ref, 1 - core), (keep_ref, core)):
            for t in range(half // HD):
                tile = which * (half // HD) + t
                columns = pl.ds(pl.multiple_of(tile * HD, HD), HD)
                scaled = noisy_ref[:, columns] * inverse
                out[0, place, t * HD : (t + 1) * HD] = (
                    scaled * gt_buf[pl.ds(tile, 1), :]
                ).astype(BF16)
                out[1, place, t * HD : (t + 1) * HD] = (
                    scaled * gc_buf[pl.ds(tile, 1), :]
                ).astype(BF16)

    for copy in held:
        copy.wait()


def norm(core, timestep, clean, noise, gt, gc, w):
    tokens, width = clean.shape
    rows = 32
    count = tokens // rows
    tiles = (width // HD, HD)
    shape = ((2, tokens, width // 2), BF16)
    return kernel(
        norm_kernel,
        "norm",
        (core, timestep),
        tuple(in_hbm(x) for x in (clean, noise, gt.reshape(tiles), gc.reshape(tiles), w)),
        (),
        (shape, shape, (w.shape, w.dtype)),
        16,
        10 * tokens * width,
        8 * tokens * width,
        scratch=(
            pltpu.VMEM((tokens, width), BF16),
            pltpu.VMEM((tokens, width), BF16),
            pltpu.VMEM((rows, width), F32),
            pltpu.VMEM(tiles, F32),
            pltpu.VMEM(tiles, F32),
            pltpu.SemaphoreType.DMA((2, count)),
            pltpu.SemaphoreType.DMA((w.shape[0] + 2,)),
        ),
    )


def project(model, a, w, held=None, y=None, out=(), shifts=()):
    _, tokens, depth = a.shape
    kinds, _, panel = w.shape
    scalars = () if y is None else (y,)
    far = (() if held is None else (held,)) + tuple(out)
    count = len(scalars) + len(far)
    shape = ((kinds, tokens // 2, panel), F32)
    made = (shape, shape) + (() if held is None else ((held.shape, held.dtype),))
    scratch, loose = [pltpu.SemaphoreType.DMA((16,))], ()
    if shifts:
        rows, columns = out[0].shape
        part = columns // Y
        loose = (((2, rows, part), BF16),) * len(shifts)
        scratch.append(pltpu.VMEM((len(shifts), 2, rows, part), BF16))

    def body(*refs):
        given = refs[:count]
        a_ref, w_ref, top_ref, bottom_ref = refs[count : count + 4]
        sem = refs[count + 4 + len(made) - 2 + len(loose)]
        first, second = [], []
        if held is not None:
            first = [
                pltpu.make_async_copy(given[-1].at[j], refs[count + 4].at[j], sem.at[j])
                for j in range(held.shape[0])
            ]
        for i, shift in enumerate(shifts):
            columns = pl.ds(pl.multiple_of(lax.rem(given[0][0] + shift, Y) * part, 128), part)
            for m in range(2):
                first.append(
                    pltpu.make_async_copy(
                        given[1 + m].at[:, columns], refs[-1].at[i, m], sem.at[2 * i + m]
                    )
                )
            target = refs[count + 4 + len(made) - 2 + i]
            second.append(pltpu.make_async_copy(refs[-1].at[i], target, sem.at[8 + i]))
        for copy in first:
            copy.start()
        for j in range(kinds):
            value = jnp.dot(a_ref[model], w_ref[j], preferred_element_type=F32)
            top_ref[j] = value[: tokens // 2]
            bottom_ref[j] = value[tokens // 2 :]
            if j == 1 and second:
                for copy in first:
                    copy.wait()
                for copy in second:
                    copy.start()
        for copy in second or first:
            copy.wait()

    return kernel(
        body,
        "project",
        scalars,
        tuple(in_hbm(x) for x in far),
        (a, w),
        made,
        16,
        2 * tokens * depth * panel * kinds,
        2 * depth * (tokens + panel * kinds),
        scratch=scratch,
        loose=loose,
    )


UNITS = 8


def join(core, parts):
    _, rows, panel = parts[0].shape
    half = rows // 2

    def body(core_ref, *refs):
        inputs, out = refs[:-1], refs[-1]
        for model in range(2):
            for which in range(2):
                left, right = inputs[4 * model + 2 * which : 4 * model + 2 * which + 2]
                clip = core_ref[0] if which == 0 else 1 - core_ref[0]
                unit = (2 * model + clip) * 2
                for kind, base in ((1, 0), (2, 2 * rows), (0, 4 * rows)):
                    value = (left[kind] + right[kind]).astype(BF16)
                    for j in range(2):
                        out[unit + j, base : base + rows] = value[
                            :, 2 * j * HD : (2 * j + 1) * HD
                        ]
                        middle = value[:, HD : 2 * HD]
                        if kind == 0:
                            middle = middle[j * half : (j + 1) * half]
                        out[unit + j, base + rows : base + rows + middle.shape[0]] = middle

    return kernel(
        body,
        "join",
        (core,),
        (),
        parts,
        (((UNITS, 5 * rows + half, HD), BF16),),
        8,
        12 * rows * panel,
        120 * rows * panel,
    )[0]


FACTOR = float(np.log2(np.e)) * HD**-0.5


def attend(queries, pairs, place=None, state=None):
    _, size, _ = queries.shape
    half = size // 11
    rows = 2 * half
    tokens, length = 3 * half * UNITS, rows * UNITS
    step = 256

    def body(*refs):
        if state is None:
            q_ref, kv_ref, *out = refs
        else:
            place_ref, q_ref, kv_ref, *before = refs
            before, out = before[:3], before[3:]
            sign = 1.0 - 2.0 * (place_ref[0] // 4).astype(F32)
        done = 0
        for middle, held in ((0, rows), (1, half)):
            keys = kv_ref[:, middle * rows : (middle + 1) * rows].reshape(length, HD)
            values = kv_ref[:, (2 + middle) * rows : (3 + middle) * rows].reshape(length, HD)
            several = step // held
            for g in range(0, UNITS, several):
                lines = slice(done, done + step)
                done += step
                start = (4 + middle) * rows
                query = q_ref[g : g + several, start : start + held].reshape(step, HD)
                score = lax.dot_general(
                    query, keys, (((1,), (1,)), ((), ())), preferred_element_type=F32
                )
                peak = jnp.max(score, axis=-1, keepdims=True)
                if state is not None:
                    old = before[0][lines, :1]
                    peak = jnp.maximum(peak, old)
                weights = jnp.exp2((score - peak) * FACTOR)
                total = jnp.sum(weights, axis=-1, keepdims=True)
                summed = jnp.dot(weights.astype(BF16), values, preferred_element_type=F32)
                if state is None:
                    out[0][lines, :] = jnp.broadcast_to(peak, (step, HD))
                    out[1][lines, :] = jnp.broadcast_to(total, (step, HD))
                    out[2][lines, :] = summed
                else:
                    scale = jnp.exp2((old - peak) * FACTOR)
                    total = total + before[1][lines, :1] * scale
                    summed = summed + before[2][lines, :] * scale
                    out[0][g : g + several, middle * rows : middle * rows + held] = (
                        (summed * (sign / total)).astype(BF16).reshape(several, held, HD)
                    )

    if state is None:
        made = (((tokens, HD), F32),) * 3
    else:
        made = (((UNITS, 3 * half, HD), BF16),)
    return kernel(
        body,
        "attend",
        () if state is None else (place,),
        (),
        (queries, pairs, *(state or ())),
        made,
        24,
        4 * tokens * length * HD,
        4 * HD * (tokens + length),
        tokens * length,
    )


def stage(swap, mine, other):
    count = len(mine)
    shape = ((count, *mine[0].shape), BF16)

    def body(swap_ref, *refs):
        sent, kept, sem = refs[2 * count :]

        def bring(first, second):
            copies = [
                pltpu.make_async_copy(source, target.at[i], sem.at[n, i])
                for n, (sources, target) in enumerate(((first, sent), (second, kept)))
                for i, source in enumerate(sources)
            ]
            for copy in copies:
                copy.start()
            for copy in copies:
                copy.wait()

        @pl.when(swap_ref[0] == 0)
        def _():
            bring(refs[count : 2 * count], refs[:count])

        @pl.when(swap_ref[0] != 0)
        def _():
            bring(refs[:count], refs[count : 2 * count])

    size = 8 * count * mine[0].size
    return kernel(
        body,
        "stage",
        (swap,),
        (*mine, *other),
        (),
        (shape, shape),
        4,
        0,
        size,
        scratch=(pltpu.SemaphoreType.DMA((2, count)),),
    )


def finish(attn, weights, dtype):
    count = len(attn)
    _, size, _ = attn[0].shape
    half = size // 3
    rows, panel = 2 * half, 3 * HD
    width = weights.shape[3]

    def body(*refs):
        sources, (w_ref, out, blocks, left, sem) = refs[:count], refs[count:]
        copies = [
            pltpu.make_async_copy(source, blocks.at[i], sem.at[i])
            for i, source in enumerate(sources)
        ]
        for copy in copies:
            copy.start()
        total = None
        for i, copy in enumerate(copies):
            copy.wait()
            for unit in range(UNITS):
                model, clip, j = unit // 4, unit // 2 % 2, unit % 2
                line, lane = clip * rows, model * panel
                left[i, line : line + rows, lane + 2 * j * HD : lane + (2 * j + 1) * HD] = blocks[
                    i, unit, :rows
                ]
                line += j * half
                left[i, line : line + half, lane + HD : lane + 2 * HD] = blocks[i, unit, rows:]
            value = jnp.dot(
                left[i], w_ref[i].reshape(2 * panel, width), preferred_element_type=F32
            )
            total = value if total is None else total + value
        out[...] = total.astype(dtype)

    return kernel(
        body,
        "finish",
        (),
        tuple(attn),
        (weights,),
        (((2 * rows, width), dtype),),
        24,
        8 * count * rows * panel * width,
        4 * count * panel * width,
        scratch=(
            pltpu.VMEM((count, UNITS, size, HD), BF16),
            pltpu.VMEM((count, 2 * rows, 2 * panel), BF16),
            pltpu.SemaphoreType.DMA((count,)),
        ),
    )[0]


def local(
    clean,
    noise,
    timestep,
    teacher_gain,
    critic_gain,
    teacher_qkv,
    critic_qkv,
    teacher_out,
    critic_out,
):
    core = lax.axis_index("dp")
    ctx = lax.axis_index("ctx")
    tp = lax.axis_index("tp")
    xh, y = tp // Y, tp % Y

    step = (timestep.astype(F32) + 1.0) / 1000.0
    level = 5.0 * step / (1.0 + 4.0 * step)

    weights = [jnp.transpose(w, (1, 0, 2)) for w in (teacher_qkv, critic_qkv)]
    keep, away, weights_t = norm(
        core, timestep, clean[0], noise[0], teacher_gain, critic_gain, weights[0]
    )
    came = send(away, CORE)
    outs = (teacher_out, critic_out)
    *own_t, weights_c = project(0, keep, weights_t, held=weights[1])
    *own_c, block_1, block_3 = project(1, keep, weights_c, y=y, out=outs, shifts=(1, 3))
    *cross_t, block_0, block_2 = project(0, came, weights_t, y=y, out=outs, shifts=(0, 2))
    cross_c = project(1, came, weights_c)
    mine = [block_0] + [
        send(block, moved(y=shift)) for shift, block in ((1, block_1), (2, block_2), (3, block_3))
    ]
    parts = []
    for own, cross in ((own_t, cross_t), (own_c, cross_c)):
        parts += [own[0], send(cross[0], CORE), cross[1], send(own[1], CORE)]

    block = over_ctx(join(core, parts))
    block, mine[1], mine[3] = lax.optimization_barrier((block, mine[1], mine[3]))
    state = attend(block, block)
    attn = attend(block, send(block, CORE), ctx, state)[0]
    attn, mine[0], mine[1], mine[3] = lax.optimization_barrier(
        (attn, mine[0], mine[1], mine[3])
    )
    attn = over_ctx(attn)
    attn, mine[2] = lax.optimization_barrier((attn, mine[2]))

    other = [send(block, CORE) for block in mine]
    gathered = [attn] + [send(attn, moved(y=shift)) for shift in range(1, Y)]
    to_send, to_keep = stage(core ^ xh, mine, other)
    away = finish(gathered, to_send, BF16)
    value = finish(gathered, to_keep, F32) + send(away, moved(xh=1)).astype(F32)
    rows = value.shape[0] // 2
    first, second = value[:rows], value[rows:]
    own_part = jnp.where(core == 0, first, second)
    came_part = send(jnp.where(core == 0, second, first), CORE)
    whole = jnp.where(
        core == 0,
        jnp.concatenate([own_part, came_part]),
        jnp.concatenate([came_part, own_part]),
    )
    return (level * whole).astype(BF16)[None]


def solution(mesh):
    placed = (
        P("dp", "ctx", None),
        P("dp", "ctx", None),
        P("dp"),
        P(),
        P(),
        P("dp", None, "tp"),
        P("dp", None, "tp"),
        P("tp", "dp"),
        P("tp", "dp"),
    )
    return jax.shard_map(
        local, mesh=mesh, in_specs=placed, out_specs=P("dp", "ctx", "tp"), check_vma=False
    )
```

```python
import jax
import jax.numpy as jnp
import numpy as np
from jax import lax
from jax.experimental import pallas as pl
from jax.experimental.pallas import tpu as pltpu
from jax.sharding import PartitionSpec as P

HD = 128
MIB = 1024 * 1024


def swapped(value):
    return lax.ppermute(value, "dp", [(0, 1), (1, 0)])


def exchange(value, axes):
    return lax.all_to_all(value, axes, 0, 0, tiled=True)


def in_hbm(value):
    return pltpu.with_memory_space_constraint(value, pltpu.HBM)


def in_vmem(value):
    return pltpu.with_memory_space_constraint(value, pltpu.VMEM)


SCALAR = pl.BlockSpec(memory_space=pltpu.SMEM)
NEAR = pl.BlockSpec(memory_space=pltpu.VMEM)
ANYWHERE = pl.BlockSpec(memory_space=pl.ANY)


def kernel(body, name, info, far, near, made, mib, flops, size, exps=0, scratch=(), loose=()):
    return pl.pallas_call(
        body,
        in_specs=[SCALAR] + [ANYWHERE] * len(far) + [NEAR] * len(near),
        out_specs=[NEAR] * len(made) + [ANYWHERE] * len(loose),
        out_shape=[pltpu.VMEM(shape, dtype) for shape, dtype in made]
        + [pltpu.HBM(shape, dtype) for shape, dtype in loose],
        scratch_shapes=list(scratch),
        compiler_params=pltpu.CompilerParams(vmem_limit_bytes=mib * MIB),
        cost_estimate=pl.CostEstimate(flops=flops, bytes_accessed=size, transcendentals=exps),
        name=name,
    )(
        info,
        *far,
        *[in_vmem(x) for x in near],
    )


BF16, F32 = jnp.bfloat16, jnp.float32

AT_CORE, AT_CTX, AT_STEP = range(3)


def noise_level(info_ref, rows):
    step = (jnp.full((rows, 1), info_ref[AT_STEP], jnp.int32).astype(F32) + 1.0) / 1000.0
    return 5.0 * step / (1.0 + 4.0 * step)


def norm_kernel(
    info_ref, clean_ref, noise_ref, gt_ref, gc_ref, w_ref,
    keep_ref, send_ref, held_ref,
    clean_buf, noise_buf, noisy_ref, gt_buf, gc_buf, in_sem, w_sem,
):
    tokens, width = clean_buf.shape
    rows = noisy_ref.shape[0]
    count = tokens // rows
    half = width // 2
    core = info_ref[AT_CORE]

    def arrival(i):
        part = pl.ds(pl.multiple_of(i * rows, rows), rows)
        return (
            pltpu.make_async_copy(clean_ref.at[part], clean_buf.at[part], in_sem.at[0, i]),
            pltpu.make_async_copy(noise_ref.at[part], noise_buf.at[part], in_sem.at[1, i]),
        )

    kinds = w_ref.shape[0]
    held = [
        pltpu.make_async_copy(w_ref.at[j], held_ref.at[j], w_sem.at[j]) for j in range(kinds)
    ]
    gains = [
        pltpu.make_async_copy(gt_ref, gt_buf, w_sem.at[kinds]),
        pltpu.make_async_copy(gc_ref, gc_buf, w_sem.at[kinds + 1]),
    ]
    for copy in gains:
        copy.start()
    for i in range(count):
        for copy in arrival(i):
            copy.start()
    for copy in held:
        copy.start()
    level = noise_level(info_ref, rows)
    for copy in gains:
        copy.wait()

    @pl.loop(0, count)
    def _(i):
        for copy in arrival(i):
            copy.wait()
        part = pl.ds(pl.multiple_of(i * rows, rows), rows)
        noisy = (1.0 - level) * clean_buf[part, :].astype(F32) + level * noise_buf[
            part, :
        ].astype(F32)
        noisy_ref[...] = noisy
        inverse = lax.rsqrt(jnp.mean(noisy * noisy, axis=-1, keepdims=True) + 1e-06)
        place = lax.rem(i + core * (count // 2), count)
        place = pl.ds(pl.multiple_of(place * rows, rows), rows)
        for out, which in ((send_ref, 1 - core), (keep_ref, core)):
            for t in range(half // HD):
                tile = which * (half // HD) + t
                columns = pl.ds(pl.multiple_of(tile * HD, HD), HD)
                scaled = noisy_ref[:, columns] * inverse
                out[0, place, t * HD : (t + 1) * HD] = (
                    scaled * gt_buf[pl.ds(tile, 1), :]
                ).astype(BF16)
                out[1, place, t * HD : (t + 1) * HD] = (
                    scaled * gc_buf[pl.ds(tile, 1), :]
                ).astype(BF16)

    for copy in held:
        copy.wait()


def norm(info, clean, noise, gt, gc, w):
    tokens, width = clean.shape
    rows = 32
    count = tokens // rows
    tiles = (width // HD, HD)
    shape = ((2, tokens, width // 2), BF16)
    return kernel(
        norm_kernel,
        "norm",
        info,
        tuple(in_hbm(x) for x in (clean, noise, gt.reshape(tiles), gc.reshape(tiles), w)),
        (),
        (shape, shape, (w.shape, w.dtype)),
        16,
        10 * tokens * width,
        8 * tokens * width,
        scratch=(
            pltpu.VMEM((tokens, width), BF16),
            pltpu.VMEM((tokens, width), BF16),
            pltpu.VMEM((rows, width), F32),
            pltpu.VMEM(tiles, F32),
            pltpu.VMEM(tiles, F32),
            pltpu.SemaphoreType.DMA((2, count)),
            pltpu.SemaphoreType.DMA((w.shape[0] + 2,)),
        ),
    )


def project(info, model, a, w, held=None):
    _, tokens, depth = a.shape
    kinds, _, panel = w.shape
    far = () if held is None else (in_hbm(held),)
    shape = ((kinds, tokens // 2, panel), F32)

    def body(info_ref, *refs):
        given, (a_ref, w_ref, top_ref, bottom_ref), rest = (
            refs[: len(far)],
            refs[len(far) : len(far) + 4],
            refs[len(far) + 4 :],
        )
        copies = [
            pltpu.make_async_copy(source.at[j], rest[0].at[j], rest[1].at[j])
            for source in given
            for j in range(kinds)
        ]
        for copy in copies:
            copy.start()
        for j in range(kinds):
            value = jnp.dot(a_ref[model], w_ref[j], preferred_element_type=F32)
            top_ref[j] = value[: tokens // 2]
            bottom_ref[j] = value[tokens // 2 :]
        for copy in copies:
            copy.wait()

    return kernel(
        body,
        "project",
        info,
        far,
        (a, w),
        (shape, shape) + (() if held is None else ((held.shape, held.dtype),)),
        8,
        2 * tokens * depth * panel * kinds,
        2 * depth * (tokens + panel * kinds),
        scratch=(pltpu.SemaphoreType.DMA((kinds,)),),
    )


UNITS = 8


def join(info, parts):
    _, rows, panel = parts[0].shape
    half = rows // 2

    def body(info_ref, *refs):
        inputs, (target, out, sem) = refs[:-3], refs[-3:]
        copies = []
        for model in range(2):
            for which in range(2):
                left, right = inputs[4 * model + 2 * which : 4 * model + 2 * which + 2]
                clip = info_ref[AT_CORE] if which == 0 else 1 - info_ref[AT_CORE]
                unit = (2 * model + clip) * 2
                for kind, base in ((1, 0), (2, 2 * rows), (0, 4 * rows)):
                    value = (left[kind] + right[kind]).astype(BF16)
                    for j in range(2):
                        out[unit + j, base : base + rows] = value[
                            :, 2 * j * HD : (2 * j + 1) * HD
                        ]
                        middle = value[:, HD : 2 * HD]
                        if kind == 0:
                            middle = middle[j * half : (j + 1) * half]
                        out[unit + j, base + rows : base + rows + middle.shape[0]] = middle
                copies.append(
                    pltpu.make_async_copy(
                        out.at[pl.ds(unit, 2)], target.at[pl.ds(unit, 2)], sem.at[len(copies)]
                    )
                )
                copies[-1].start()
        for copy in copies:
            copy.wait()

    return kernel(
        body,
        "join",
        info,
        (),
        parts,
        (),
        8,
        12 * rows * panel,
        120 * rows * panel,
        scratch=(
            pltpu.VMEM((UNITS, 5 * rows + half, HD), BF16),
            pltpu.SemaphoreType.DMA((4,)),
        ),
        loose=(((UNITS, 5 * rows + half, HD), BF16),),
    )[0]


FACTOR = float(np.log2(np.e)) * HD**-0.5


def attend(info, queries, pairs, state=None):
    _, size, _ = queries.shape
    half = size // 11
    rows = 2 * half
    tokens, length = 3 * half * UNITS, rows * UNITS
    step = 256

    def body(*refs):
        info_ref, q_ref, kv_ref, *out = refs
        target, sem = out[3 if state else 0], out[-1]
        before, out = ((), out) if state is None else (out[:3], out[4:-1])
        copies = []
        sign = 1.0 - 2.0 * (info_ref[AT_CTX] // 4).astype(F32)
        done = 0
        for middle, held in ((0, rows), (1, half)):
            keys = kv_ref[:, middle * rows : (middle + 1) * rows].reshape(length, HD)
            values = kv_ref[:, (2 + middle) * rows : (3 + middle) * rows].reshape(length, HD)
            several = step // held
            for g in range(0, UNITS, several):
                lines = slice(done, done + step)
                done += step
                start = (4 + middle) * rows
                query = q_ref[g : g + several, start : start + held].reshape(step, HD)
                score = lax.dot_general(
                    query, keys, (((1,), (1,)), ((), ())), preferred_element_type=F32
                )
                peak = jnp.max(score, axis=-1, keepdims=True)
                peak = jnp.broadcast_to(peak, (step, HD))
                if state is not None:
                    old = before[0][lines, :]
                    peak = jnp.maximum(peak, old)
                wide = jnp.concatenate([peak] * (length // HD), axis=1)
                weights = jnp.exp2((score - wide) * FACTOR)
                total = jnp.sum(weights, axis=-1, keepdims=True)
                total = jnp.broadcast_to(total, (step, HD))
                summed = jnp.dot(weights.astype(BF16), values, preferred_element_type=F32)
                if state is None:
                    out[0][lines, :] = peak
                    out[1][lines, :] = total
                    out[2][lines, :] = summed
                else:
                    scale = jnp.exp2((old - peak) * FACTOR)
                    total = total + before[1][lines, :] * scale
                    summed = summed + before[2][lines, :] * scale
                    place = (pl.ds(g, several), pl.ds(middle * rows, held))
                    out[0][place] = (
                        (summed * (sign / total)).astype(BF16).reshape(several, held, HD)
                    )
                    copies.append(
                        pltpu.make_async_copy(
                            out[0].at[place], target.at[place], sem.at[len(copies)]
                        )
                    )
                    copies[-1].start()
        for copy in copies:
            copy.wait()

    shape = ((UNITS, 3 * half, HD), BF16)
    return kernel(
        body,
        "attend",
        info,
        (),
        (queries, pairs, *(state or ())),
        (((tokens, HD), F32),) * 3 if state is None else (),
        24,
        4 * tokens * length * HD,
        4 * HD * (tokens + length),
        tokens * length,
        scratch=()
        if state is None
        else (pltpu.VMEM(*shape), pltpu.SemaphoreType.DMA((tokens // step,))),
        loose=() if state is None else (shape,),
    )


def expand(info, attn, mine, other):
    _, size, _ = attn.shape
    half = size // 3
    rows, panel = 2 * half, 3 * HD
    columns = mine[0].shape[1]
    part = columns // 4
    shape = ((2 * UNITS, rows, part), BF16)

    def body(info_ref, *refs):
        weights, (attn_ref, target, left, held, out, in_sem, out_sem) = refs[:4], refs[4:]
        arrivals = [
            [
                pltpu.make_async_copy(
                    weights[2 * way + model].at[:, q * part : (q + 1) * part],
                    held.at[4 * way + q, model],
                    in_sem.at[4 * way + q, model],
                )
                for model in range(2)
            ]
            for way in range(2)
            for q in range(4)
        ]
        for pair in arrivals:
            for copy in pair:
                copy.start()
        for unit in range(UNITS):
            model, clip, j = unit // 4, unit // 2 % 2, unit % 2
            line, lane = clip * rows, model * panel
            left[line : line + rows, lane + 2 * j * HD : lane + (2 * j + 1) * HD] = attn_ref[
                unit, :rows
            ]
            line += j * half
            left[line : line + half, lane + HD : lane + 2 * HD] = attn_ref[unit, rows:]
        leaving = []
        for i, pair in enumerate(arrivals):
            for copy in pair:
                copy.wait()
            value = jnp.dot(
                left[...], held[i].reshape(2 * panel, part), preferred_element_type=F32
            ).astype(BF16)
            way = info_ref[AT_CORE] if i < 4 else 1 - info_ref[AT_CORE]
            for clip in range(2):
                block = clip * UNITS + way * 4 + i % 4
                out[block] = value[clip * rows : (clip + 1) * rows]
                copy = pltpu.make_async_copy(
                    out.at[block], target.at[block], out_sem.at[len(leaving)]
                )
                copy.start()
                leaving.append(copy)
        for copy in leaving:
            copy.wait()

    return kernel(
        body,
        "expand",
        info,
        (*[in_hbm(w) for w in mine], *other),
        (attn,),
        (),
        24,
        16 * rows * panel * columns,
        8 * panel * columns,
        scratch=(
            pltpu.VMEM((2 * rows, 2 * panel), BF16),
            pltpu.VMEM((8, 2, panel, part), BF16),
            pltpu.VMEM(*shape),
            pltpu.SemaphoreType.DMA((8, 2)),
            pltpu.SemaphoreType.DMA((16,)),
        ),
        loose=(shape,),
    )[0]


def collect(info, blocks):
    _, rows, width = blocks.shape

    def body(info_ref, block_ref, out_ref):
        level = noise_level(info_ref, rows)
        for core in range(2):
            total = block_ref[core * UNITS].astype(F32)
            for tp in range(1, UNITS):
                total = total + block_ref[core * UNITS + tp].astype(F32)
            out_ref[core * rows : (core + 1) * rows] = (level * total).astype(BF16)

    return pl.pallas_call(
        body,
        in_specs=[SCALAR, NEAR],
        out_specs=NEAR,
        out_shape=jax.ShapeDtypeStruct((2 * rows, width), BF16),
        compiler_params=pltpu.CompilerParams(vmem_limit_bytes=8 * MIB),
        name="collect",
    )(info, in_vmem(blocks))


def local(
    clean,
    noise,
    timestep,
    teacher_gain,
    critic_gain,
    teacher_qkv,
    critic_qkv,
    teacher_out,
    critic_out,
):
    places = [lax.axis_index("dp"), lax.axis_index("ctx"), timestep[0]]
    info = lax.optimization_barrier(jnp.stack(places).astype(jnp.int32))

    weights = [jnp.transpose(w, (1, 0, 2)) for w in (teacher_qkv, critic_qkv)]
    keep, away, weights_t = norm(
        info, clean[0], noise[0], teacher_gain, critic_gain, weights[0]
    )
    came = swapped(away)
    *own_t, weights_c = project(info, 0, keep, weights_t, weights[1])
    own_c = project(info, 1, keep, weights_c)
    cross_t = project(info, 0, came, weights_t)
    cross_c = project(info, 1, came, weights_c)
    parts = []
    for own, cross in ((own_t, cross_t), (own_c, cross_c)):
        parts += [own[0], swapped(cross[0]), cross[1], swapped(own[1])]

    block = exchange(join(info, parts), "ctx")
    state = attend(info, block, block)
    attn = exchange(attend(info, block, swapped(block), state)[0], "ctx")
    outs = (teacher_out, critic_out)
    sums = expand(info, attn, outs, [swapped(out) for out in outs])
    return collect(info, exchange(sums, ("dp", "tp")))[None]


def solution(mesh):
    placed = (
        P("dp", "ctx", None),
        P("dp", "ctx", None),
        P("dp"),
        P(),
        P(),
        P("dp", None, "tp"),
        P("dp", None, "tp"),
        P("tp", "dp"),
        P("tp", "dp"),
    )
    return jax.shard_map(
        local, mesh=mesh, in_specs=placed, out_specs=P("dp", "ctx", "tp"), check_vma=False
    )
```

```python
import jax
import jax.numpy as jnp
import numpy as np
from jax import lax
from jax.experimental import pallas as pl
from jax.experimental.pallas import tpu as pltpu
from jax.sharding import PartitionSpec as P

HD = 128
MIB = 1024 * 1024


def swapped(value):
    return lax.ppermute(value, "dp", [(0, 1), (1, 0)])


def exchange(value, axes):
    return lax.all_to_all(value, axes, 0, 0, tiled=True)


def in_hbm(value):
    return pltpu.with_memory_space_constraint(value, pltpu.HBM)


def in_vmem(value):
    return pltpu.with_memory_space_constraint(value, pltpu.VMEM)


SCALAR = pl.BlockSpec(memory_space=pltpu.SMEM)
NEAR = pl.BlockSpec(memory_space=pltpu.VMEM)
ANYWHERE = pl.BlockSpec(memory_space=pl.ANY)


def kernel(body, name, info, far, near, made, mib, flops, size, exps=0, scratch=(), loose=()):
    return pl.pallas_call(
        body,
        in_specs=[SCALAR] + [ANYWHERE] * len(far) + [NEAR] * len(near),
        out_specs=[NEAR] * len(made) + [ANYWHERE] * len(loose),
        out_shape=[pltpu.VMEM(shape, dtype) for shape, dtype in made]
        + [pltpu.HBM(shape, dtype) for shape, dtype in loose],
        scratch_shapes=list(scratch),
        compiler_params=pltpu.CompilerParams(vmem_limit_bytes=mib * MIB),
        cost_estimate=pl.CostEstimate(flops=flops, bytes_accessed=size, transcendentals=exps),
        name=name,
    )(
        info,
        *far,
        *[in_vmem(x) for x in near],
    )


BF16, F32 = jnp.bfloat16, jnp.float32

AT_CORE, AT_CTX, AT_STEP = range(3)


def noise_level(info_ref, rows):
    step = (jnp.full((rows, 1), info_ref[AT_STEP], jnp.int32).astype(F32) + 1.0) / 1000.0
    return 5.0 * step / (1.0 + 4.0 * step)


def norm_kernel(
    info_ref, clean_ref, noise_ref, gt_ref, gc_ref, w_ref,
    keep_ref, send_ref, held_ref,
    clean_buf, noise_buf, noisy_ref, gt_buf, gc_buf, in_sem, w_sem,
):
    tokens, width = clean_buf.shape
    rows = noisy_ref.shape[0]
    count = tokens // rows
    half = width // 2
    core = info_ref[AT_CORE]

    def arrival(i):
        part = pl.ds(pl.multiple_of(i * rows, rows), rows)
        return (
            pltpu.make_async_copy(clean_ref.at[part], clean_buf.at[part], in_sem.at[0, i]),
            pltpu.make_async_copy(noise_ref.at[part], noise_buf.at[part], in_sem.at[1, i]),
        )

    kinds = w_ref.shape[0]
    held = [
        pltpu.make_async_copy(w_ref.at[j], held_ref.at[j], w_sem.at[j]) for j in range(kinds)
    ]
    gains = [
        pltpu.make_async_copy(gt_ref, gt_buf, w_sem.at[kinds]),
        pltpu.make_async_copy(gc_ref, gc_buf, w_sem.at[kinds + 1]),
    ]
    for copy in gains:
        copy.start()
    for i in range(count):
        for copy in arrival(i):
            copy.start()
    for copy in held:
        copy.start()
    level = noise_level(info_ref, rows)
    for copy in gains:
        copy.wait()

    @pl.loop(0, count)
    def _(i):
        for copy in arrival(i):
            copy.wait()
        part = pl.ds(pl.multiple_of(i * rows, rows), rows)
        noisy = (1.0 - level) * clean_buf[part, :].astype(F32) + level * noise_buf[
            part, :
        ].astype(F32)
        noisy_ref[...] = noisy
        inverse = lax.rsqrt(jnp.mean(noisy * noisy, axis=-1, keepdims=True) + 1e-06)
        place = lax.rem(i + core * (count // 2), count)
        place = pl.ds(pl.multiple_of(place * rows, rows), rows)
        for out, which in ((send_ref, 1 - core), (keep_ref, core)):
            for t in range(half // HD):
                tile = which * (half // HD) + t
                columns = pl.ds(pl.multiple_of(tile * HD, HD), HD)
                scaled = noisy_ref[:, columns] * inverse
                out[0, place, t * HD : (t + 1) * HD] = (
                    scaled * gt_buf[pl.ds(tile, 1), :]
                ).astype(BF16)
                out[1, place, t * HD : (t + 1) * HD] = (
                    scaled * gc_buf[pl.ds(tile, 1), :]
                ).astype(BF16)

    for copy in held:
        copy.wait()


def norm(info, clean, noise, gt, gc, w):
    tokens, width = clean.shape
    rows = 32
    count = tokens // rows
    tiles = (width // HD, HD)
    shape = ((2, tokens, width // 2), BF16)
    return kernel(
        norm_kernel,
        "norm",
        info,
        tuple(in_hbm(x) for x in (clean, noise, gt.reshape(tiles), gc.reshape(tiles), w)),
        (),
        (shape, shape, (w.shape, w.dtype)),
        16,
        10 * tokens * width,
        8 * tokens * width,
        scratch=(
            pltpu.VMEM((tokens, width), BF16),
            pltpu.VMEM((tokens, width), BF16),
            pltpu.VMEM((rows, width), F32),
            pltpu.VMEM(tiles, F32),
            pltpu.VMEM(tiles, F32),
            pltpu.SemaphoreType.DMA((2, count)),
            pltpu.SemaphoreType.DMA((w.shape[0] + 2,)),
        ),
    )


def project(info, model, a, w, held=None):
    _, tokens, depth = a.shape
    kinds, _, panel = w.shape
    far = () if held is None else (in_hbm(held),)
    shape = ((kinds, tokens // 2, panel), F32)

    def body(info_ref, *refs):
        given, (a_ref, w_ref, top_ref, bottom_ref), rest = (
            refs[: len(far)],
            refs[len(far) : len(far) + 4],
            refs[len(far) + 4 :],
        )
        copies = [
            pltpu.make_async_copy(source.at[j], rest[0].at[j], rest[1].at[j])
            for source in given
            for j in range(kinds)
        ]
        for copy in copies:
            copy.start()
        right = jnp.concatenate([w_ref[j] for j in range(kinds)], axis=1)
        value = jnp.dot(a_ref[model], right, preferred_element_type=F32)
        for j in range(kinds):
            top_ref[j] = value[: tokens // 2, j * panel : (j + 1) * panel]
            bottom_ref[j] = value[tokens // 2 :, j * panel : (j + 1) * panel]
        for copy in copies:
            copy.wait()

    return kernel(
        body,
        "project",
        info,
        far,
        (a, w),
        (shape, shape) + (() if held is None else ((held.shape, held.dtype),)),
        8,
        2 * tokens * depth * panel * kinds,
        2 * depth * (tokens + panel * kinds),
        scratch=(pltpu.SemaphoreType.DMA((kinds,)),),
    )


UNITS = 8


def join(info, parts):
    _, rows, panel = parts[0].shape
    half = rows // 2

    def body(info_ref, *refs):
        inputs, (target, out, sem) = refs[:-3], refs[-3:]
        copies = []
        for model in range(2):
            for which in range(2):
                left, right = inputs[4 * model + 2 * which : 4 * model + 2 * which + 2]
                clip = info_ref[AT_CORE] if which == 0 else 1 - info_ref[AT_CORE]
                unit = (2 * model + clip) * 2
                for kind, base in ((1, 0), (2, 2 * rows), (0, 4 * rows)):
                    value = (left[kind] + right[kind]).astype(BF16)
                    for j in range(2):
                        out[unit + j, base : base + rows] = value[
                            :, 2 * j * HD : (2 * j + 1) * HD
                        ]
                        middle = value[:, HD : 2 * HD]
                        if kind == 0:
                            middle = middle[j * half : (j + 1) * half]
                        out[unit + j, base + rows : base + rows + middle.shape[0]] = middle
                copies.append(
                    pltpu.make_async_copy(
                        out.at[pl.ds(unit, 2)], target.at[pl.ds(unit, 2)], sem.at[len(copies)]
                    )
                )
                copies[-1].start()
        for copy in copies:
            copy.wait()

    return kernel(
        body,
        "join",
        info,
        (),
        parts,
        (),
        8,
        12 * rows * panel,
        120 * rows * panel,
        scratch=(
            pltpu.VMEM((UNITS, 5 * rows + half, HD), BF16),
            pltpu.SemaphoreType.DMA((4,)),
        ),
        loose=(((UNITS, 5 * rows + half, HD), BF16),),
    )[0]


FACTOR = float(np.log2(np.e)) * HD**-0.5


def attend(info, queries, pairs, hold, state=None):
    _, size, _ = queries.shape
    half = size // 11
    rows = 2 * half
    tokens, length = 3 * half * UNITS, rows * UNITS
    step = 256
    count = len(hold)
    tasks = [
        (middle, held, g)
        for middle, held in ((0, rows), (1, half))
        for g in range(0, UNITS, step // held)
    ]

    def body(info_ref, *refs):
        sources, (q_ref, kv_ref, *rest) = refs[:count], refs[count:]
        before = ()
        if state is not None:
            before, rest = rest[:3], rest[3:]
        held_refs, rest = rest[:count], rest[count:]
        if state is None:
            *outs, sem = rest
        else:
            target, sem, out = rest
        holding = [
            pltpu.make_async_copy(source, place, sem.at[i])
            for i, (source, place) in enumerate(zip(sources, held_refs))
        ]
        for copy in holding:
            copy.start()
        sign = 1.0 - 2.0 * (info_ref[AT_CTX] // 4).astype(F32)

        def tokens_of(kind, middle):
            first = (kind + middle) * rows
            return kv_ref[:, first : first + rows].reshape(length, HD)

        def score(middle, held, g):
            first = (4 + middle) * rows
            query = q_ref[g : g + step // held, first : first + held].reshape(step, HD)
            return lax.dot_general(
                query, tokens_of(0, middle), (((1,), (1,)), ((), ())), preferred_element_type=F32
            )

        copies = []
        coming = score(*tasks[0])
        for n, (middle, held, g) in enumerate(tasks):
            current = coming
            if n + 1 < len(tasks):
                coming = score(*tasks[n + 1])
            lines = slice(n * step, (n + 1) * step)
            peak = jnp.broadcast_to(jnp.max(current, axis=-1, keepdims=True), (step, HD))
            if state is not None:
                old = before[0][lines, :]
                peak = jnp.maximum(peak, old)
            wide = jnp.concatenate([peak] * (length // HD), axis=1)
            weights = jnp.exp2((current - wide) * FACTOR)
            total = jnp.broadcast_to(jnp.sum(weights, axis=-1, keepdims=True), (step, HD))
            summed = jnp.dot(
                weights.astype(BF16), tokens_of(2, middle), preferred_element_type=F32
            )
            if state is None:
                outs[0][lines, :] = peak
                outs[1][lines, :] = total
                outs[2][lines, :] = summed
                continue
            scale = jnp.exp2((old - peak) * FACTOR)
            total = total + before[1][lines, :] * scale
            summed = summed + before[2][lines, :] * scale
            several = step // held
            out[g : g + several, middle * rows : middle * rows + held] = (
                (summed * (sign / total)).astype(BF16).reshape(several, held, HD)
            )
            place = (pl.ds(g, several), pl.ds(middle * rows, held))
            copies.append(
                pltpu.make_async_copy(out.at[place], target.at[place], sem.at[count + n])
            )
            copies[-1].start()
        for copy in holding + copies:
            copy.wait()

    shape = ((UNITS, 3 * half, HD), BF16)
    made = tuple((h.shape, BF16) for h in hold)
    semaphores = pltpu.SemaphoreType.DMA((count + len(tasks),))
    return kernel(
        body,
        "attend",
        info,
        tuple(hold),
        (queries, pairs, *(state or ())),
        made + (((tokens, HD), F32),) * 3 if state is None else made,
        24,
        4 * tokens * length * HD,
        4 * HD * (tokens + length),
        tokens * length,
        scratch=(semaphores,) if state is None else (semaphores, pltpu.VMEM(*shape)),
        loose=() if state is None else (shape,),
    )


def expand(info, attn, mine, other):
    _, size, _ = attn.shape
    half = size // 3
    rows, panel = 2 * half, 3 * HD
    columns = mine[0].shape[1]
    part = columns // 4
    shape = ((2 * UNITS, rows, part), BF16)

    def body(info_ref, attn_ref, *refs):
        weights, (target, left, out, sem) = refs[:4], refs[4:]
        for unit in range(UNITS):
            model, clip, j = unit // 4, unit // 2 % 2, unit % 2
            line, lane = clip * rows, model * panel
            left[line : line + rows, lane + 2 * j * HD : lane + (2 * j + 1) * HD] = attn_ref[
                unit, :rows
            ]
            line += j * half
            left[line : line + half, lane + HD : lane + 2 * HD] = attn_ref[unit, rows:]
        leaving = []
        for i in range(0, 8, 2):
            place = slice(i % 4 * part, (i % 4 + 2) * part)
            right = jnp.concatenate([w[:, place] for w in weights[i // 4 * 2 : i // 4 * 2 + 2]])
            value = jnp.dot(left[...], right, preferred_element_type=F32).astype(BF16)
            way = info_ref[AT_CORE] if i < 4 else 1 - info_ref[AT_CORE]
            for clip in range(2):
                block = clip * UNITS + way * 4 + i % 4
                for n in range(2):
                    out[block + n] = value[
                        clip * rows : (clip + 1) * rows, n * part : (n + 1) * part
                    ]
                place = pl.ds(block, 2)
                copy = pltpu.make_async_copy(
                    out.at[place], target.at[place], sem.at[len(leaving)]
                )
                copy.start()
                leaving.append(copy)
        for copy in leaving:
            copy.wait()

    return kernel(
        body,
        "expand",
        info,
        (),
        (attn, *mine, *other),
        (),
        12,
        16 * rows * panel * columns,
        8 * panel * columns,
        scratch=(
            pltpu.VMEM((2 * rows, 2 * panel), BF16),
            pltpu.VMEM(*shape),
            pltpu.SemaphoreType.DMA((8,)),
        ),
        loose=(shape,),
    )[0]


def collect(info, blocks):
    _, rows, width = blocks.shape

    def body(info_ref, block_ref, out_ref):
        level = noise_level(info_ref, rows)
        for core in range(2):
            total = block_ref[core * UNITS].astype(F32)
            for tp in range(1, UNITS):
                total = total + block_ref[core * UNITS + tp].astype(F32)
            out_ref[core * rows : (core + 1) * rows] = (level * total).astype(BF16)

    return pl.pallas_call(
        body,
        in_specs=[SCALAR, NEAR],
        out_specs=NEAR,
        out_shape=jax.ShapeDtypeStruct((2 * rows, width), BF16),
        compiler_params=pltpu.CompilerParams(vmem_limit_bytes=8 * MIB),
        name="collect",
    )(info, in_vmem(blocks))


def local(
    clean,
    noise,
    timestep,
    teacher_gain,
    critic_gain,
    teacher_qkv,
    critic_qkv,
    teacher_out,
    critic_out,
):
    places = [lax.axis_index("dp"), lax.axis_index("ctx"), timestep[0]]
    info = lax.optimization_barrier(jnp.stack(places).astype(jnp.int32))

    weights = [jnp.transpose(w, (1, 0, 2)) for w in (teacher_qkv, critic_qkv)]
    keep, away, weights_t = norm(
        info, clean[0], noise[0], teacher_gain, critic_gain, weights[0]
    )
    came = swapped(away)
    *own_t, weights_c = project(info, 0, keep, weights_t, weights[1])
    outs = (teacher_out, critic_out)
    other = [swapped(out) for out in outs]
    own_c = project(info, 1, keep, weights_c)
    cross_t = project(info, 0, came, weights_t)
    cross_c = project(info, 1, came, weights_c)
    parts = []
    for own, cross in ((own_t, cross_t), (own_c, cross_c)):
        parts += [own[0], swapped(cross[0]), cross[1], swapped(own[1])]

    block = exchange(join(info, parts), "ctx")
    *mine, peak, total, summed = attend(info, block, block, [in_hbm(out) for out in outs])
    *other, attn = attend(info, block, swapped(block), other, (peak, total, summed))
    sums = expand(info, exchange(attn, "ctx"), mine, other)
    return collect(info, exchange(sums, ("dp", "tp")))[None]


def solution(mesh):
    placed = (
        P("dp", "ctx", None),
        P("dp", "ctx", None),
        P("dp"),
        P(),
        P(),
        P("dp", None, "tp"),
        P("dp", None, "tp"),
        P("tp", "dp"),
        P("tp", "dp"),
    )
    return jax.shard_map(
        local, mesh=mesh, in_specs=placed, out_specs=P("dp", "ctx", "tp"), check_vma=False
    )
```

```python
import jax
import jax.numpy as jnp
import numpy as np
from jax import lax
from jax.experimental import pallas as pl
from jax.experimental.pallas import tpu as pltpu
from jax.sharding import PartitionSpec as P

HD = 128
MIB = 1024 * 1024


def swapped(value):
    return lax.ppermute(value, "dp", [(0, 1), (1, 0)])


def exchange(value, axes):
    return lax.all_to_all(value, axes, 0, 0, tiled=True)


def in_hbm(value):
    return pltpu.with_memory_space_constraint(value, pltpu.HBM)


def in_vmem(value):
    return pltpu.with_memory_space_constraint(value, pltpu.VMEM)


SCALAR = pl.BlockSpec(memory_space=pltpu.SMEM)
NEAR = pl.BlockSpec(memory_space=pltpu.VMEM)
ANYWHERE = pl.BlockSpec(memory_space=pl.ANY)


def kernel(body, name, info, far, near, made, mib, flops, size, exps=0, scratch=(), loose=(), aliases=None):
    return pl.pallas_call(
        body,
        in_specs=[SCALAR] + [ANYWHERE] * len(far) + [NEAR] * len(near),
        out_specs=[NEAR] * len(made) + [ANYWHERE] * len(loose),
        out_shape=[pltpu.VMEM(shape, dtype) for shape, dtype in made]
        + [pltpu.HBM(shape, dtype) for shape, dtype in loose],
        scratch_shapes=list(scratch),
        input_output_aliases=aliases or {},
        compiler_params=pltpu.CompilerParams(vmem_limit_bytes=mib * MIB),
        cost_estimate=pl.CostEstimate(flops=flops, bytes_accessed=size, transcendentals=exps),
        name=name,
    )(
        info,
        *far,
        *[in_vmem(x) for x in near],
    )


BF16, F32 = jnp.bfloat16, jnp.float32

AT_CORE, AT_CTX, AT_STEP = range(3)


def noise_level(info_ref):
    step = (jnp.full((1, 1), info_ref[AT_STEP], jnp.int32).astype(F32) + 1.0) / 1000.0
    return 5.0 * step / (1.0 + 4.0 * step)


def norm_kernel(
    info_ref, clean_ref, noise_ref, gt_ref, gc_ref, w_ref,
    keep_ref, send_ref, held_ref,
    clean_buf, noise_buf, noisy_ref, gt_buf, gc_buf, in_sem, w_sem,
):
    tokens, width = clean_buf.shape
    rows = noisy_ref.shape[0]
    count = tokens // rows
    half = width // 2
    core = info_ref[AT_CORE]

    def arrival(i):
        part = pl.ds(pl.multiple_of(i * rows, rows), rows)
        return (
            pltpu.make_async_copy(clean_ref.at[part], clean_buf.at[part], in_sem.at[0, i]),
            pltpu.make_async_copy(noise_ref.at[part], noise_buf.at[part], in_sem.at[1, i]),
        )

    kinds = w_ref.shape[0]
    held = [
        pltpu.make_async_copy(w_ref.at[j], held_ref.at[j], w_sem.at[j]) for j in range(kinds)
    ]
    gains = [
        pltpu.make_async_copy(gt_ref, gt_buf, w_sem.at[kinds]),
        pltpu.make_async_copy(gc_ref, gc_buf, w_sem.at[kinds + 1]),
    ]
    for copy in gains:
        copy.start()
    for i in range(count):
        for copy in arrival(i):
            copy.start()
    for copy in held:
        copy.start()
    level = noise_level(info_ref)
    for copy in gains:
        copy.wait()

    @pl.loop(0, count)
    def _(i):
        for copy in arrival(i):
            copy.wait()
        part = pl.ds(pl.multiple_of(i * rows, rows), rows)
        squares = jnp.zeros((rows, HD), F32)
        for t in range(width // HD):
            columns = slice(t * HD, (t + 1) * HD)
            noisy = (1.0 - level) * clean_buf[part, columns].astype(
                F32
            ) + level * noise_buf[part, columns].astype(F32)
            noisy_ref[:, columns] = noisy
            squares += noisy * noisy
        mean = jnp.sum(squares, axis=-1, keepdims=True) / width
        inverse = jnp.broadcast_to(lax.rsqrt(mean + 1e-06), (rows, HD))
        place = lax.rem(i + core * (count // 2), count)
        place = pl.ds(pl.multiple_of(place * rows, rows), rows)
        for out, which in ((send_ref, 1 - core), (keep_ref, core)):
            for t in range(half // HD):
                tile = which * (half // HD) + t
                columns = pl.ds(pl.multiple_of(tile * HD, HD), HD)
                scaled = noisy_ref[:, columns] * inverse
                out[0, place, t * HD : (t + 1) * HD] = (
                    scaled * gt_buf[pl.ds(tile, 1), :]
                ).astype(BF16)
                out[1, place, t * HD : (t + 1) * HD] = (
                    scaled * gc_buf[pl.ds(tile, 1), :]
                ).astype(BF16)

    for copy in held:
        copy.wait()


def norm(info, clean, noise, gt, gc, w):
    tokens, width = clean.shape
    rows = 32
    count = tokens // rows
    tiles = (width // HD, HD)
    shape = ((2, tokens, width // 2), BF16)
    return kernel(
        norm_kernel,
        "norm",
        info,
        tuple(in_hbm(x) for x in (clean, noise, gt.reshape(tiles), gc.reshape(tiles), w)),
        (),
        (shape, shape, (w.shape, w.dtype)),
        16,
        10 * tokens * width,
        8 * tokens * width,
        scratch=(
            pltpu.VMEM((tokens, width), BF16),
            pltpu.VMEM((tokens, width), BF16),
            pltpu.VMEM((rows, width), F32),
            pltpu.VMEM(tiles, F32),
            pltpu.VMEM(tiles, F32),
            pltpu.SemaphoreType.DMA((2, count)),
            pltpu.SemaphoreType.DMA((w.shape[0] + 2,)),
        ),
    )


def project(info, model, a, weights, hold=None, fetch=None):
    _, tokens, depth = a.shape
    panel = weights[0].shape[-1]
    kinds = 3
    shape = ((kinds, tokens // 2, panel), F32)
    made = (shape, shape)
    if hold is not None:
        made += (((kinds - 1, depth, panel), BF16),)
    if fetch is not None:
        made += (((1, depth, panel), BF16),)
    far = tuple(in_hbm(w) for w in (hold, fetch) if w is not None)

    def body(info_ref, *refs):
        sources, rest = refs[: len(far)], refs[len(far) :]
        a_ref, *w_refs = rest[: 1 + len(weights)]
        top_ref, bottom_ref, *brought, sem = rest[1 + len(weights) :]
        first = 0 if fetch is None else kinds - 1
        copies = [
            pltpu.make_async_copy(sources[0].at[first + j], brought[0].at[j], sem.at[j])
            for j in range(brought[0].shape[0] if far else 0)
        ]
        for copy in copies:
            copy.start()

        def product(slices, j):
            value = jnp.dot(
                a_ref[model], jnp.concatenate(slices, axis=1), preferred_element_type=F32
            )
            for n in range(len(slices)):
                part = value[:, n * panel : (n + 1) * panel]
                top_ref[j + n] = part[: tokens // 2]
                bottom_ref[j + n] = part[tokens // 2 :]

        product([w[j] for w in w_refs for j in range(w.shape[0])], 0)
        for copy in copies:
            copy.wait()
        if fetch is not None:
            product([brought[0][0]], kinds - 1)

    return kernel(
        body,
        "project",
        info,
        far,
        (a, *weights),
        made,
        8,
        2 * tokens * depth * panel * kinds,
        2 * depth * (tokens + panel * kinds),
        scratch=(pltpu.SemaphoreType.DMA((kinds,)),),
    )


UNITS = 8


def join(info, model, parts, blocks=None):
    _, rows, panel = parts[0].shape
    half = rows // 2
    shape = (UNITS, 5 * rows + half, HD)

    def body(info_ref, *refs):
        target, out, sem = refs[-3:]
        inputs = refs[-3 - len(parts) : -3]
        copies = []
        for which in range(2):
            left, right = inputs[2 * which : 2 * which + 2]
            clip = info_ref[AT_CORE] if which == 0 else 1 - info_ref[AT_CORE]
            for kind, base in ((1, 0), (2, 2 * rows), (0, 4 * rows)):
                value = (left[kind] + right[kind]).astype(BF16)
                for j in range(2):
                    block = 2 * which + j
                    out[block, base : base + rows] = value[:, 2 * j * HD : (2 * j + 1) * HD]
                    middle = value[:, HD : 2 * HD]
                    if kind == 0:
                        middle = middle[j * half : (j + 1) * half]
                    out[block, base + rows : base + rows + middle.shape[0]] = middle
            copies.append(
                pltpu.make_async_copy(
                    out.at[pl.ds(2 * which, 2)],
                    target.at[pl.ds(4 * model + 2 * clip, 2)],
                    sem.at[which],
                )
            )
            copies[-1].start()
        for copy in copies:
            copy.wait()

    return kernel(
        body,
        "join",
        info,
        () if blocks is None else (blocks,),
        parts,
        (),
        8,
        6 * rows * panel,
        60 * rows * panel,
        scratch=(pltpu.VMEM((4, *shape[1:]), BF16), pltpu.SemaphoreType.DMA((2,))),
        loose=((shape, BF16),),
        aliases={} if blocks is None else {1: 0},
    )[0]


FACTOR = float(np.log2(np.e)) * HD**-0.5


def attend(info, queries, pairs, hold, state=None):
    _, size, _ = queries.shape
    half = size // 11
    rows = 2 * half
    tokens, length = 3 * half * UNITS, rows * UNITS
    step = 256
    count = len(hold)
    tasks = [
        (middle, held, g)
        for middle, held in ((0, rows), (1, half))
        for g in range(0, UNITS, step // held)
    ]

    def body(info_ref, *refs):
        sources, (q_ref, kv_ref, *rest) = refs[:count], refs[count:]
        before = ()
        if state is not None:
            before, rest = rest[:3], rest[3:]
        held_refs, rest = rest[:count], rest[count:]
        *outs, sem = rest
        holding = [
            pltpu.make_async_copy(source, place, sem.at[i])
            for i, (source, place) in enumerate(zip(sources, held_refs))
        ]
        for copy in holding:
            copy.start()
        sign = 1.0 - 2.0 * (info_ref[AT_CTX] // 4).astype(F32)

        def tokens_of(kind, middle):
            first = (kind + middle) * rows
            return kv_ref[:, first : first + rows].reshape(length, HD)

        def score(middle, held, g):
            first = (4 + middle) * rows
            query = q_ref[g : g + step // held, first : first + held].reshape(step, HD)
            return lax.dot_general(
                query, tokens_of(0, middle), (((1,), (1,)), ((), ())), preferred_element_type=F32
            )

        coming = score(*tasks[0])
        for n, (middle, held, g) in enumerate(tasks):
            current = coming
            if n + 1 < len(tasks):
                coming = score(*tasks[n + 1])
            lines = slice(n * step, (n + 1) * step)
            peak = jnp.broadcast_to(jnp.max(current, axis=-1, keepdims=True), (step, HD))
            if state is not None:
                old = before[0][lines, :]
                peak = jnp.maximum(peak, old)
            wide = jnp.concatenate([peak] * (length // HD), axis=1)
            weights = jnp.exp2((current - wide) * FACTOR)
            total = jnp.broadcast_to(jnp.sum(weights, axis=-1, keepdims=True), (step, HD))
            summed = jnp.dot(
                weights.astype(BF16), tokens_of(2, middle), preferred_element_type=F32
            )
            if state is None:
                outs[0][lines, :] = peak
                outs[1][lines, :] = total
                outs[2][lines, :] = summed
                continue
            scale = jnp.exp2((old - peak) * FACTOR)
            total = total + before[1][lines, :] * scale
            summed = summed + before[2][lines, :] * scale
            several = step // held
            outs[0][g : g + several, middle * rows : middle * rows + held] = (
                (summed * (sign / total)).astype(BF16).reshape(several, held, HD)
            )
        if state is not None:
            outs[1][...] = jnp.broadcast_to(noise_level(info_ref), (8, HD))
        for copy in holding:
            copy.wait()

    shape = ((UNITS, 3 * half, HD), BF16)
    made = tuple((h.shape, BF16) for h in hold)
    return kernel(
        body,
        "attend",
        info,
        tuple(hold),
        (queries, pairs, *(state or ())),
        made + ((((tokens, HD), F32),) * 3 if state is None else (shape, ((8, HD), F32))),
        24,
        4 * tokens * length * HD,
        4 * HD * (tokens + length),
        tokens * length,
        scratch=(pltpu.SemaphoreType.DMA((count,)),),
    )


def expand(info, attn, mine, other):
    _, size, _ = attn.shape
    half = size // 3
    rows, panel = 2 * half, 3 * HD
    columns = mine[0].shape[1]
    part = columns // 4
    shape = ((2 * UNITS, rows, part), BF16)

    def body(info_ref, attn_ref, *refs):
        weights, (out, left) = refs[:4], refs[4:]
        for unit in range(UNITS):
            model, clip, j = unit // 4, unit // 2 % 2, unit % 2
            line, lane = clip * rows, model * panel
            left[line : line + rows, lane + 2 * j * HD : lane + (2 * j + 1) * HD] = attn_ref[
                unit, :rows
            ]
            line += j * half
            left[line : line + half, lane + HD : lane + 2 * HD] = attn_ref[unit, rows:]
        for i in range(0, 8, 2):
            place = slice(i % 4 * part, (i % 4 + 2) * part)
            right = jnp.concatenate([w[:, place] for w in weights[i // 4 * 2 : i // 4 * 2 + 2]])
            value = jnp.dot(left[...], right, preferred_element_type=F32).astype(BF16)
            way = info_ref[AT_CORE] if i < 4 else 1 - info_ref[AT_CORE]
            for clip in range(2):
                block = clip * UNITS + way * 4 + i % 4
                for n in range(2):
                    out[block + n] = value[
                        clip * rows : (clip + 1) * rows, n * part : (n + 1) * part
                    ]

    return kernel(
        body,
        "expand",
        info,
        (),
        (attn, *mine, *other),
        (shape,),
        12,
        16 * rows * panel * columns,
        8 * panel * columns,
        scratch=(pltpu.VMEM((2 * rows, 2 * panel), BF16),),
    )[0]


def collect(level, blocks):
    _, rows, width = blocks.shape

    def body(level_ref, block_ref, out_ref):
        level = level_ref[:1, :1]
        step = 32
        for core in range(2):
            for line in range(0, rows, step):
                place = slice(line, line + step)
                total = block_ref[core * UNITS, place].astype(F32)
                for tp in range(1, UNITS):
                    total = total + block_ref[core * UNITS + tp, place].astype(F32)
                out_ref[core * rows + line : core * rows + line + step] = (level * total).astype(
                    BF16
                )

    return pl.pallas_call(
        body,
        in_specs=[NEAR, NEAR],
        out_specs=NEAR,
        out_shape=jax.ShapeDtypeStruct((2 * rows, width), BF16),
        compiler_params=pltpu.CompilerParams(vmem_limit_bytes=8 * MIB),
        name="collect",
    )(in_vmem(level), in_vmem(blocks))


def local(
    clean,
    noise,
    timestep,
    teacher_gain,
    critic_gain,
    teacher_qkv,
    critic_qkv,
    teacher_out,
    critic_out,
):
    places = [lax.axis_index("dp"), lax.axis_index("ctx"), timestep[0]]
    info = lax.optimization_barrier(jnp.stack(places).astype(jnp.int32))

    weights = [jnp.transpose(w, (1, 0, 2)) for w in (teacher_qkv, critic_qkv)]
    keep, away, weights_t = norm(
        info, clean[0], noise[0], teacher_gain, critic_gain, weights[0]
    )
    came = swapped(away)
    *own_t, most_c = project(info, 0, keep, (weights_t,), hold=weights[1])
    outs = (teacher_out, critic_out)
    other = [swapped(out) for out in outs]
    *own_c, last_c = project(info, 1, keep, (most_c,), fetch=weights[1])
    cross_t = project(info, 0, came, (weights_t,))
    cross_c = project(info, 1, came, (most_c, last_c))
    blocks = None
    for m, (own, cross) in enumerate(((own_t, cross_t), (own_c, cross_c))):
        parts = (own[0], swapped(cross[0]), cross[1], swapped(own[1]))
        blocks = join(info, m, parts, blocks)

    block = exchange(blocks, "ctx")
    *mine, peak, total, summed = attend(info, block, block, [in_hbm(out) for out in outs])
    *other, attn, level = attend(info, block, swapped(block), other, (peak, total, summed))
    sums = expand(info, exchange(attn, "ctx"), mine, other)
    return collect(level, exchange(sums, ("dp", "tp")))[None]


def solution(mesh):
    placed = (
        P("dp", "ctx", None),
        P("dp", "ctx", None),
        P("dp"),
        P(),
        P(),
        P("dp", None, "tp"),
        P("dp", None, "tp"),
        P("tp", "dp"),
        P("tp", "dp"),
    )
    return jax.shard_map(
        local, mesh=mesh, in_specs=placed, out_specs=P("dp", "ctx", "tp"), check_vma=False
    )
```

```python
import jax
import jax.numpy as jnp
import numpy as np
from jax import lax
from jax.experimental import pallas as pl
from jax.experimental.pallas import tpu as pltpu
from jax.sharding import PartitionSpec as P

HD = 128
MIB = 1024 * 1024
XH, Y = 2, 4


def over_tp(value, xh, y):
    pairs = [
        (e * Y + f, (e + xh) % XH * Y + (f + y) % Y) for e in range(XH) for f in range(Y)
    ]
    return lax.ppermute(value, "tp", pairs)


def swapped(value):
    return lax.ppermute(value, "dp", [(0, 1), (1, 0)])


def exchange(value, axes):
    return lax.all_to_all(value, axes, 0, 0, tiled=True)


def in_hbm(value):
    return pltpu.with_memory_space_constraint(value, pltpu.HBM)


def in_vmem(value):
    return pltpu.with_memory_space_constraint(value, pltpu.VMEM)


SCALAR = pl.BlockSpec(memory_space=pltpu.SMEM)
NEAR = pl.BlockSpec(memory_space=pltpu.VMEM)
ANYWHERE = pl.BlockSpec(memory_space=pl.ANY)


def kernel(body, name, info, far, near, made, mib, flops, size, exps=0, scratch=(), loose=()):
    return pl.pallas_call(
        body,
        in_specs=[SCALAR] + [ANYWHERE] * len(far) + [NEAR] * len(near),
        out_specs=[NEAR] * len(made) + [ANYWHERE] * len(loose),
        out_shape=[pltpu.VMEM(shape, dtype) for shape, dtype in made]
        + [pltpu.HBM(shape, dtype) for shape, dtype in loose],
        scratch_shapes=list(scratch),
        compiler_params=pltpu.CompilerParams(vmem_limit_bytes=mib * MIB),
        cost_estimate=pl.CostEstimate(flops=flops, bytes_accessed=size, transcendentals=exps),
        name=name,
    )(
        info,
        *far,
        *[in_vmem(x) for x in near],
    )


BF16, F32 = jnp.bfloat16, jnp.float32

AT_CORE, AT_CTX, AT_STEP, AT_XH, AT_Y = range(5)


def noise_level(info_ref):
    step = (jnp.full((1, 1), info_ref[AT_STEP], jnp.int32).astype(F32) + 1.0) / 1000.0
    return 5.0 * step / (1.0 + 4.0 * step)


def norm_kernel(
    info_ref, clean_ref, noise_ref, gt_ref, gc_ref, w_ref,
    keep_ref, send_ref, held_ref,
    clean_buf, noise_buf, noisy_ref, gt_buf, gc_buf, in_sem, w_sem,
):
    tokens, width = clean_buf.shape
    rows = noisy_ref.shape[0]
    count = tokens // rows
    half = width // 2
    core = info_ref[AT_CORE]

    def arrival(i):
        part = pl.ds(pl.multiple_of(i * rows, rows), rows)
        return (
            pltpu.make_async_copy(clean_ref.at[part], clean_buf.at[part], in_sem.at[0, i]),
            pltpu.make_async_copy(noise_ref.at[part], noise_buf.at[part], in_sem.at[1, i]),
        )

    kinds = w_ref.shape[0]
    held = [
        pltpu.make_async_copy(w_ref.at[j], held_ref.at[j], w_sem.at[j]) for j in range(kinds)
    ]
    gains = [
        pltpu.make_async_copy(gt_ref, gt_buf, w_sem.at[kinds]),
        pltpu.make_async_copy(gc_ref, gc_buf, w_sem.at[kinds + 1]),
    ]
    for copy in gains:
        copy.start()
    for i in range(count):
        for copy in arrival(i):
            copy.start()
    for copy in held:
        copy.start()
    level = noise_level(info_ref)
    for copy in gains:
        copy.wait()

    @pl.loop(0, count)
    def _(i):
        for copy in arrival(i):
            copy.wait()
        part = pl.ds(pl.multiple_of(i * rows, rows), rows)
        squares = jnp.zeros((rows, HD), F32)
        for t in range(width // HD):
            columns = slice(t * HD, (t + 1) * HD)
            noisy = (1.0 - level) * clean_buf[part, columns].astype(
                F32
            ) + level * noise_buf[part, columns].astype(F32)
            noisy_ref[:, columns] = noisy
            squares += noisy * noisy
        mean = jnp.sum(squares, axis=-1, keepdims=True) / width
        inverse = jnp.broadcast_to(lax.rsqrt(mean + 1e-06), (rows, HD))
        place = lax.rem(i + core * (count // 2), count)
        place = pl.ds(pl.multiple_of(place * rows, rows), rows)
        for out, which in ((send_ref, 1 - core), (keep_ref, core)):
            for t in range(half // HD):
                tile = which * (half // HD) + t
                columns = pl.ds(pl.multiple_of(tile * HD, HD), HD)
                scaled = noisy_ref[:, columns] * inverse
                out[0, place, t * HD : (t + 1) * HD] = (
                    scaled * gt_buf[pl.ds(tile, 1), :]
                ).astype(BF16)
                out[1, place, t * HD : (t + 1) * HD] = (
                    scaled * gc_buf[pl.ds(tile, 1), :]
                ).astype(BF16)

    for copy in held:
        copy.wait()


def norm(info, clean, noise, gt, gc, w):
    tokens, width = clean.shape
    rows = 32
    count = tokens // rows
    tiles = (width // HD, HD)
    shape = ((2, tokens, width // 2), BF16)
    return kernel(
        norm_kernel,
        "norm",
        info,
        tuple(in_hbm(x) for x in (clean, noise, gt.reshape(tiles), gc.reshape(tiles), w)),
        (),
        (shape, shape, (w.shape, w.dtype)),
        16,
        10 * tokens * width,
        8 * tokens * width,
        scratch=(
            pltpu.VMEM((tokens, width), BF16),
            pltpu.VMEM((tokens, width), BF16),
            pltpu.VMEM((rows, width), F32),
            pltpu.VMEM(tiles, F32),
            pltpu.VMEM(tiles, F32),
            pltpu.SemaphoreType.DMA((2, count)),
            pltpu.SemaphoreType.DMA((w.shape[0] + 2,)),
        ),
    )


def project(info, model, a, weights, hold=None, fetch=None, halves=(0, 1)):
    _, tokens, depth = a.shape
    panel = weights[0].shape[-1]
    kinds = 3
    half = tokens // 2
    lines = slice(halves[0] * half, (halves[-1] + 1) * half)
    made = (((kinds, half, panel), F32),) * len(halves)
    if hold is not None:
        made += (((kinds - 1, depth, panel), BF16),)
    if fetch is not None:
        made += (((1, depth, panel), BF16),)
    far = tuple(in_hbm(w) for w in (hold, fetch) if w is not None)

    def body(info_ref, *refs):
        sources, rest = refs[: len(far)], refs[len(far) :]
        a_ref, *w_refs = rest[: 1 + len(weights)]
        *outs, sem = rest[1 + len(weights) :]
        outs, brought = outs[: len(halves)], outs[len(halves) :]
        first = 0 if fetch is None else kinds - 1
        copies = [
            pltpu.make_async_copy(sources[0].at[first + j], brought[0].at[j], sem.at[j])
            for j in range(brought[0].shape[0] if far else 0)
        ]
        for copy in copies:
            copy.start()

        def product(slices, j):
            value = jnp.dot(
                a_ref[model, lines], jnp.concatenate(slices, axis=1), preferred_element_type=F32
            )
            for n in range(len(slices)):
                part = value[:, n * panel : (n + 1) * panel]
                for i, out in enumerate(outs):
                    out[j + n] = part[i * half : (i + 1) * half]

        product([w[j] for w in w_refs for j in range(w.shape[0])], 0)
        for copy in copies:
            copy.wait()
        if fetch is not None:
            product([brought[0][0]], kinds - 1)

    return kernel(
        body,
        "project",
        info,
        far,
        (a, *weights),
        made,
        8,
        2 * half * len(halves) * depth * panel * kinds,
        2 * depth * (tokens + panel * kinds),
        scratch=(pltpu.SemaphoreType.DMA((kinds,)),),
    )


UNITS = 8


def join(info, parts, done=None):
    _, rows, panel = parts[0].shape
    half = rows // 2
    shape = (UNITS, 5 * rows + half, HD)
    part = (4, *shape[1:])

    def body(info_ref, *refs):
        inputs, rest = refs[: len(parts)], refs[len(parts) :]
        copies = []

        def leave(source, model, which):
            clip = info_ref[AT_CORE] if which == 0 else 1 - info_ref[AT_CORE]
            copies.append(
                pltpu.make_async_copy(
                    source.at[pl.ds(2 * which, 2)],
                    target.at[pl.ds(4 * model + 2 * clip, 2)],
                    sem.at[2 * model + which],
                )
            )
            copies[-1].start()

        if done is None:
            (out,) = rest
        else:
            teacher, target, out, sem = rest
            leave(teacher, 0, 0)
            leave(teacher, 0, 1)
        for which in range(2):
            left, right = inputs[2 * which : 2 * which + 2]
            for kind, base in ((1, 0), (2, 2 * rows), (0, 4 * rows)):
                value = (left[kind] + right[kind]).astype(BF16)
                for j in range(2):
                    block = 2 * which + j
                    out[block, base : base + rows] = value[:, 2 * j * HD : (2 * j + 1) * HD]
                    middle = value[:, HD : 2 * HD]
                    if kind == 0:
                        middle = middle[j * half : (j + 1) * half]
                    out[block, base + rows : base + rows + middle.shape[0]] = middle
            if done is not None:
                leave(out, 1, which)
        for copy in copies:
            copy.wait()

    return kernel(
        body,
        "join",
        info,
        (),
        parts if done is None else (*parts, done),
        ((part, BF16),) if done is None else (),
        8,
        6 * rows * panel,
        60 * rows * panel,
        scratch=()
        if done is None
        else (pltpu.VMEM(part, BF16), pltpu.SemaphoreType.DMA((4,))),
        loose=() if done is None else ((shape, BF16),),
    )[0]


FACTOR = float(np.log2(np.e)) * HD**-0.5


def attend(info, queries, pairs, hold, state=None):
    _, size, _ = queries.shape
    half = size // 11
    rows = 2 * half
    tokens, length = 3 * half * UNITS, rows * UNITS
    step = 256
    count = len(hold)
    tasks = [
        (middle, held, g)
        for middle, held in ((0, rows), (1, half))
        for g in range(0, UNITS, step // held)
    ]

    def body(info_ref, *refs):
        sources, (q_ref, kv_ref, *rest) = refs[:count], refs[count:]
        before = ()
        if state is not None:
            before, rest = rest[:3], rest[3:]
        held_refs, rest = rest[:count], rest[count:]
        *outs, sem = rest
        holding = [
            pltpu.make_async_copy(source, place, sem.at[i])
            for i, (source, place) in enumerate(zip(sources, held_refs))
        ]
        for copy in holding:
            copy.start()
        sign = 1.0 - 2.0 * (info_ref[AT_CTX] // 4).astype(F32)

        def tokens_of(kind, middle):
            first = (kind + middle) * rows
            return kv_ref[:, first : first + rows].reshape(length, HD)

        def score(middle, held, g):
            first = (4 + middle) * rows
            query = q_ref[g : g + step // held, first : first + held].reshape(step, HD)
            return lax.dot_general(
                query, tokens_of(0, middle), (((1,), (1,)), ((), ())), preferred_element_type=F32
            )

        coming = score(*tasks[0])
        for n, (middle, held, g) in enumerate(tasks):
            current = coming
            if n + 1 < len(tasks):
                coming = score(*tasks[n + 1])
            lines = slice(n * step, (n + 1) * step)
            peak = jnp.broadcast_to(jnp.max(current, axis=-1, keepdims=True), (step, HD))
            if state is not None:
                old = before[0][lines, :]
                peak = jnp.maximum(peak, old)
            wide = jnp.concatenate([peak] * (length // HD), axis=1)
            weights = jnp.exp2((current - wide) * FACTOR)
            total = jnp.broadcast_to(jnp.sum(weights, axis=-1, keepdims=True), (step, HD))
            summed = jnp.dot(
                weights.astype(BF16), tokens_of(2, middle), preferred_element_type=F32
            )
            if state is None:
                outs[0][lines, :] = peak
                outs[1][lines, :] = total
                outs[2][lines, :] = summed
                continue
            scale = jnp.exp2((old - peak) * FACTOR)
            total = total + before[1][lines, :] * scale
            summed = summed + before[2][lines, :] * scale
            several = step // held
            outs[0][g : g + several, middle * rows : middle * rows + held] = (
                (summed * (sign / total)).astype(BF16).reshape(several, held, HD)
            )
        if state is not None:
            outs[1][...] = jnp.broadcast_to(noise_level(info_ref), (8, HD))
        for copy in holding:
            copy.wait()

    shape = ((UNITS, 3 * half, HD), BF16)
    made = tuple((h.shape, BF16) for h in hold)
    return kernel(
        body,
        "attend",
        info,
        tuple(hold),
        (queries, pairs, *(state or ())),
        made + ((((tokens, HD), F32),) * 3 if state is None else (shape, ((8, HD), F32))),
        24,
        4 * tokens * length * HD,
        4 * HD * (tokens + length),
        tokens * length,
        scratch=(pltpu.SemaphoreType.DMA((count,)),),
    )


def expand(info, attn, mine, other):
    _, size, _ = attn.shape
    half = size // 3
    rows, panel = 2 * half, 3 * HD
    columns = mine[0].shape[1]
    part = columns // Y

    def body(info_ref, attn_ref, *refs):
        weights, (to_x, *to_y, own_y, own_x, left) = refs[:4], refs[4:]
        for unit in range(UNITS):
            model, clip, j = unit // 4, unit // 2 % 2, unit % 2
            line, lane = clip * rows, model * panel
            left[line : line + rows, lane + 2 * j * HD : lane + (2 * j + 1) * HD] = attn_ref[
                unit, :rows
            ]
            line += j * half
            left[line : line + half, lane + HD : lane + 2 * HD] = attn_ref[unit, rows:]
        for i in range(0, 8, 2):
            place = slice(i % 4 * part, (i % 4 + 2) * part)
            right = jnp.concatenate([w[:, place] for w in weights[i // 4 * 2 : i // 4 * 2 + 2]])
            value = jnp.dot(left[...], right, preferred_element_type=F32)
            xh = info_ref[AT_CORE] if i < 4 else 1 - info_ref[AT_CORE]
            here = xh == info_ref[AT_XH]
            for n in range(2):
                y = i % 4 + n
                shift = lax.rem(y - info_ref[AT_Y] + Y, Y)
                first = value[:rows, n * part : (n + 1) * part]
                second = value[rows:, n * part : (n + 1) * part]
                for f, target in enumerate((own_y, *to_y)):

                    @pl.when(shift == f)
                    def _():
                        target[xh] = first.astype(target.dtype)

                @pl.when(here)
                def _():
                    own_x[y] = second

                @pl.when(jnp.logical_not(here))
                def _():
                    to_x[y] = second.astype(BF16)

    by_x, by_y = (Y, rows, part), (XH, rows, part)
    return kernel(
        body,
        "expand",
        info,
        (),
        (attn, *mine, *other),
        ((by_x, BF16), *[(by_y, BF16)] * (Y - 1), (by_y, F32), (by_x, F32)),
        12,
        16 * rows * panel * columns,
        8 * panel * columns,
        scratch=(pltpu.VMEM((2 * rows, 2 * panel), BF16),),
    )


def turn(info, own_y, own_x, from_x, from_y):
    _, rows, part = own_y.shape

    def body(info_ref, own_y_ref, own_x_ref, from_x_ref, *refs):
        from_y_refs, (keep_a, keep_b, to_x, *to_y) = refs[: Y - 1], refs[Y - 1 :]
        xh, y = info_ref[AT_XH], info_ref[AT_Y]
        for out, place in ((to_x, 1 - xh), (keep_a, xh)):
            total = own_y_ref[place]
            for ref in from_y_refs:
                total = total + ref[place].astype(F32)
            out[...] = total.astype(out.dtype)
        for f, out in enumerate((keep_b, *to_y)):
            place = lax.rem(y + f, Y)
            total = own_x_ref[place] + from_x_ref[place].astype(F32)
            out[...] = total.astype(out.dtype)

    shape = (rows, part)
    return kernel(
        body,
        "turn",
        info,
        (),
        (own_y, own_x, from_x, *from_y),
        ((shape, F32), (shape, F32), *[(shape, BF16)] * Y),
        8,
        12 * rows * part,
        60 * rows * part,
    )


def collect(info, keep_a, keep_b, from_x, from_y):
    shape = keep_a.shape

    def body(info_ref, a_ref, b_ref, x_ref, *refs):
        y_refs, (own, away) = refs[: Y - 1], refs[Y - 1 :]
        for core, (first, second) in enumerate(((own, away), (away, own))):

            @pl.when(info_ref[AT_CORE] == core)
            def _():
                first[...] = a_ref[...] + x_ref[...].astype(F32)
                total = b_ref[...]
                for ref in y_refs:
                    total = total + ref[...].astype(F32)
                second[...] = total

    return kernel(
        body,
        "collect",
        info,
        (),
        (keep_a, keep_b, from_x, *from_y),
        ((shape, F32), (shape, F32)),
        4,
        4 * shape[0] * shape[1],
        30 * shape[0] * shape[1],
    )


def scale(info, level, own, came):
    rows, width = own.shape

    def body(info_ref, level_ref, own_ref, came_ref, out_ref):
        level = level_ref[:1, :1]
        for source, part in ((own_ref, info_ref[AT_CORE]), (came_ref, 1 - info_ref[AT_CORE])):
            place = pl.ds(pl.multiple_of(part * rows, rows), rows)
            out_ref[place, :] = (level * source[...]).astype(BF16)

    return pl.pallas_call(
        body,
        in_specs=[SCALAR, NEAR, NEAR, NEAR],
        out_specs=NEAR,
        out_shape=jax.ShapeDtypeStruct((2 * rows, width), BF16),
        compiler_params=pltpu.CompilerParams(vmem_limit_bytes=4 * MIB),
        name="scale",
    )(info, in_vmem(level), in_vmem(own), in_vmem(came))


def local(
    clean,
    noise,
    timestep,
    teacher_gain,
    critic_gain,
    teacher_qkv,
    critic_qkv,
    teacher_out,
    critic_out,
):
    tp = lax.axis_index("tp")
    places = [lax.axis_index("dp"), lax.axis_index("ctx"), timestep[0], tp // Y, tp % Y]
    info = lax.optimization_barrier(jnp.stack(places).astype(jnp.int32))

    weights = [jnp.transpose(w, (1, 0, 2)) for w in (teacher_qkv, critic_qkv)]
    keep, away, weights_t = norm(
        info, clean[0], noise[0], teacher_gain, critic_gain, weights[0]
    )
    came = swapped(away)
    *own_t, most_c = project(info, 0, keep, (weights_t,), hold=weights[1])
    outs = (teacher_out, critic_out)
    other = [swapped(out) for out in outs]
    *own_c, last_c = project(info, 1, keep, (most_c,), fetch=weights[1])
    cross_t = project(info, 0, came, (weights_t,))
    cross_c = [project(info, 1, came, (most_c, last_c), halves=(i,))[0] for i in range(2)]
    blocks = None
    for own, cross in ((own_t, cross_t), (own_c, cross_c)):
        parts = (own[0], swapped(cross[0]), cross[1], swapped(own[1]))
        blocks = join(info, parts, blocks)

    block = exchange(blocks, "ctx")
    *mine, peak, total, summed = attend(info, block, block, [in_hbm(out) for out in outs])
    *other, attn, level = attend(info, block, swapped(block), other, (peak, total, summed))
    to_x, *to_y, own_y, own_x = expand(info, exchange(attn, "ctx"), mine, other)
    from_x = over_tp(to_x, 1, 0)
    from_y = [over_tp(value, 0, f) for f, value in enumerate(to_y, 1)]
    keep_a, keep_b, to_x, *to_y = turn(info, own_y, own_x, from_x, from_y)
    from_x = over_tp(to_x, 1, 0)
    from_y = [over_tp(value, 0, f) for f, value in enumerate(to_y, 1)]
    own, away = collect(info, keep_a, keep_b, from_x, from_y)
    return scale(info, level, own, swapped(away))[None]


def solution(mesh):
    placed = (
        P("dp", "ctx", None),
        P("dp", "ctx", None),
        P("dp"),
        P(),
        P(),
        P("dp", None, "tp"),
        P("dp", None, "tp"),
        P("tp", "dp"),
        P("tp", "dp"),
    )
    return jax.shard_map(
        local, mesh=mesh, in_specs=placed, out_specs=P("dp", "ctx", "tp"), check_vma=False
    )
```

```python
import jax
import jax.numpy as jnp
import numpy as np
from jax import lax
from jax.experimental import pallas as pl
from jax.experimental.pallas import tpu as pltpu
from jax.sharding import PartitionSpec as P

HD = 128
MIB = 1024 * 1024
XH, Y = 2, 4


def over_tp(value, xh, y, core=0):
    pairs = [
        ((d * XH + e) * Y + f, ((d + core) % 2 * XH + (e + xh) % XH) * Y + (f + y) % Y)
        for d in range(2)
        for e in range(XH)
        for f in range(Y)
    ]
    return lax.ppermute(value, ("dp", "tp"), pairs)


def swapped(value):
    return lax.ppermute(value, "dp", [(0, 1), (1, 0)])


def exchange(value, axes):
    return lax.all_to_all(value, axes, 0, 0, tiled=True)


def in_hbm(value):
    return pltpu.with_memory_space_constraint(value, pltpu.HBM)


def in_vmem(value):
    return pltpu.with_memory_space_constraint(value, pltpu.VMEM)


SCALAR = pl.BlockSpec(memory_space=pltpu.SMEM)
NEAR = pl.BlockSpec(memory_space=pltpu.VMEM)
ANYWHERE = pl.BlockSpec(memory_space=pl.ANY)


def kernel(body, name, info, far, near, made, mib, flops, size, exps=0, scratch=(), loose=()):
    return pl.pallas_call(
        body,
        in_specs=[SCALAR] + [ANYWHERE] * len(far) + [NEAR] * len(near),
        out_specs=[NEAR] * len(made) + [ANYWHERE] * len(loose),
        out_shape=[pltpu.VMEM(shape, dtype) for shape, dtype in made]
        + [pltpu.HBM(shape, dtype) for shape, dtype in loose],
        scratch_shapes=list(scratch),
        compiler_params=pltpu.CompilerParams(vmem_limit_bytes=mib * MIB),
        cost_estimate=pl.CostEstimate(flops=flops, bytes_accessed=size, transcendentals=exps),
        name=name,
    )(
        info,
        *far,
        *[in_vmem(x) for x in near],
    )


BF16, F32 = jnp.bfloat16, jnp.float32

AT_CORE, AT_CTX, AT_STEP, AT_XH, AT_Y = range(5)


def noise_level(info_ref):
    step = (jnp.full((1, 1), info_ref[AT_STEP], jnp.int32).astype(F32) + 1.0) / 1000.0
    return 5.0 * step / (1.0 + 4.0 * step)


def norm_kernel(
    info_ref, clean_ref, noise_ref, gt_ref, gc_ref, w_ref,
    keep_ref, send_ref, held_ref,
    clean_buf, noise_buf, noisy_ref, gt_buf, gc_buf, in_sem, w_sem,
):
    tokens, width = clean_buf.shape
    rows = noisy_ref.shape[0]
    count = tokens // rows
    half = width // 2
    core = info_ref[AT_CORE]

    def arrival(i):
        part = pl.ds(pl.multiple_of(i * rows, rows), rows)
        return (
            pltpu.make_async_copy(clean_ref.at[part], clean_buf.at[part], in_sem.at[0, i]),
            pltpu.make_async_copy(noise_ref.at[part], noise_buf.at[part], in_sem.at[1, i]),
        )

    kinds = w_ref.shape[0]
    held = [
        pltpu.make_async_copy(w_ref.at[j], held_ref.at[j], w_sem.at[j]) for j in range(kinds)
    ]
    gains = [
        pltpu.make_async_copy(gt_ref, gt_buf, w_sem.at[kinds]),
        pltpu.make_async_copy(gc_ref, gc_buf, w_sem.at[kinds + 1]),
    ]
    for copy in gains:
        copy.start()
    for i in range(count):
        for copy in arrival(i):
            copy.start()
    for copy in held:
        copy.start()
    level = noise_level(info_ref)
    for copy in gains:
        copy.wait()

    @pl.loop(0, count)
    def _(i):
        for copy in arrival(i):
            copy.wait()
        part = pl.ds(pl.multiple_of(i * rows, rows), rows)
        squares = jnp.zeros((rows, HD), F32)
        for t in range(width // HD):
            columns = slice(t * HD, (t + 1) * HD)
            noisy = (1.0 - level) * clean_buf[part, columns].astype(
                F32
            ) + level * noise_buf[part, columns].astype(F32)
            noisy_ref[:, columns] = noisy
            squares += noisy * noisy
        mean = jnp.sum(squares, axis=-1, keepdims=True) / width
        inverse = jnp.broadcast_to(lax.rsqrt(mean + 1e-06), (rows, HD))
        place = lax.rem(i + core * (count // 2), count)
        place = pl.ds(pl.multiple_of(place * rows, rows), rows)
        for out, which in ((send_ref, 1 - core), (keep_ref, core)):
            for t in range(half // HD):
                tile = which * (half // HD) + t
                columns = pl.ds(pl.multiple_of(tile * HD, HD), HD)
                scaled = noisy_ref[:, columns] * inverse
                out[0, place, t * HD : (t + 1) * HD] = (
                    scaled * gt_buf[pl.ds(tile, 1), :]
                ).astype(BF16)
                out[1, place, t * HD : (t + 1) * HD] = (
                    scaled * gc_buf[pl.ds(tile, 1), :]
                ).astype(BF16)

    for copy in held:
        copy.wait()


def norm(info, clean, noise, gt, gc, w):
    tokens, width = clean.shape
    rows = 32
    count = tokens // rows
    tiles = (width // HD, HD)
    shape = ((2, tokens, width // 2), BF16)
    return kernel(
        norm_kernel,
        "norm",
        info,
        tuple(in_hbm(x) for x in (clean, noise, gt.reshape(tiles), gc.reshape(tiles), w)),
        (),
        (shape, shape, (w.shape, w.dtype)),
        16,
        10 * tokens * width,
        8 * tokens * width,
        scratch=(
            pltpu.VMEM((tokens, width), BF16),
            pltpu.VMEM((tokens, width), BF16),
            pltpu.VMEM((rows, width), F32),
            pltpu.VMEM(tiles, F32),
            pltpu.VMEM(tiles, F32),
            pltpu.SemaphoreType.DMA((2, count)),
            pltpu.SemaphoreType.DMA((w.shape[0] + 2,)),
        ),
    )


def project(info, model, a, weights, hold=None, fetch=None, halves=(0, 1)):
    _, tokens, depth = a.shape
    panel = weights[0].shape[-1]
    kinds = 3
    half = tokens // 2
    lines = slice(halves[0] * half, (halves[-1] + 1) * half)
    made = (((kinds, half, panel), F32),) * len(halves)
    if hold is not None:
        made += (((kinds - 1, depth, panel), BF16),)
    if fetch is not None:
        made += (((1, depth, panel), BF16),)
    far = tuple(in_hbm(w) for w in (hold, fetch) if w is not None)

    def body(info_ref, *refs):
        sources, rest = refs[: len(far)], refs[len(far) :]
        a_ref, *w_refs = rest[: 1 + len(weights)]
        *outs, sem = rest[1 + len(weights) :]
        outs, brought = outs[: len(halves)], outs[len(halves) :]
        first = 0 if fetch is None else kinds - 1
        copies = [
            pltpu.make_async_copy(sources[0].at[first + j], brought[0].at[j], sem.at[j])
            for j in range(brought[0].shape[0] if far else 0)
        ]
        for copy in copies:
            copy.start()

        def product(slices, j):
            value = jnp.dot(
                a_ref[model, lines], jnp.concatenate(slices, axis=1), preferred_element_type=F32
            )
            for n in range(len(slices)):
                part = value[:, n * panel : (n + 1) * panel]
                for i, out in enumerate(outs):
                    out[j + n] = part[i * half : (i + 1) * half]

        product([w[j] for w in w_refs for j in range(w.shape[0])], 0)
        for copy in copies:
            copy.wait()
        if fetch is not None:
            product([brought[0][0]], kinds - 1)

    return kernel(
        body,
        "project",
        info,
        far,
        (a, *weights),
        made,
        8,
        2 * half * len(halves) * depth * panel * kinds,
        2 * depth * (tokens + panel * kinds),
        scratch=(pltpu.SemaphoreType.DMA((kinds,)),),
    )


UNITS = 8


def join(info, parts, done=None):
    _, rows, panel = parts[0].shape
    half = rows // 2
    shape = (UNITS, 5 * rows + half, HD)
    part = (4, *shape[1:])

    def body(info_ref, *refs):
        inputs, rest = refs[: len(parts)], refs[len(parts) :]
        copies = []

        def leave(source, model, which):
            clip = info_ref[AT_CORE] if which == 0 else 1 - info_ref[AT_CORE]
            copies.append(
                pltpu.make_async_copy(
                    source.at[pl.ds(2 * which, 2)],
                    target.at[pl.ds(4 * model + 2 * clip, 2)],
                    sem.at[2 * model + which],
                )
            )
            copies[-1].start()

        if done is None:
            (out,) = rest
        else:
            teacher, target, out, sem = rest
            leave(teacher, 0, 0)
            leave(teacher, 0, 1)
        for which in range(2):
            left, right = inputs[2 * which : 2 * which + 2]
            for kind, base in ((1, 0), (2, 2 * rows), (0, 4 * rows)):
                value = (left[kind] + right[kind]).astype(BF16)
                for j in range(2):
                    block = 2 * which + j
                    out[block, base : base + rows] = value[:, 2 * j * HD : (2 * j + 1) * HD]
                    middle = value[:, HD : 2 * HD]
                    if kind == 0:
                        middle = middle[j * half : (j + 1) * half]
                    out[block, base + rows : base + rows + middle.shape[0]] = middle
            if done is not None:
                leave(out, 1, which)
        for copy in copies:
            copy.wait()

    return kernel(
        body,
        "join",
        info,
        (),
        parts if done is None else (*parts, done),
        ((part, BF16),) if done is None else (),
        8,
        6 * rows * panel,
        60 * rows * panel,
        scratch=()
        if done is None
        else (pltpu.VMEM(part, BF16), pltpu.SemaphoreType.DMA((4,))),
        loose=() if done is None else ((shape, BF16),),
    )[0]


FACTOR = float(np.log2(np.e)) * HD**-0.5


def attend(info, queries, pairs, hold, state=None):
    _, size, _ = queries.shape
    half = size // 11
    rows = 2 * half
    tokens, length = 3 * half * UNITS, rows * UNITS
    step = 256
    count = len(hold)
    tasks = [
        (middle, held, g)
        for middle, held in ((0, rows), (1, half))
        for g in range(0, UNITS, step // held)
    ]

    def body(info_ref, *refs):
        sources, (q_ref, kv_ref, *rest) = refs[:count], refs[count:]
        before = ()
        if state is not None:
            before, rest = rest[:3], rest[3:]
        held_refs, rest = rest[:count], rest[count:]
        *outs, sem = rest
        holding = [
            pltpu.make_async_copy(source, place, sem.at[i])
            for i, (source, place) in enumerate(zip(sources, held_refs))
        ]
        for copy in holding:
            copy.start()
        sign = 1.0 - 2.0 * (info_ref[AT_CTX] // 4).astype(F32)

        def tokens_of(kind, middle):
            first = (kind + middle) * rows
            return kv_ref[:, first : first + rows].reshape(length, HD)

        def score(middle, held, g):
            first = (4 + middle) * rows
            query = q_ref[g : g + step // held, first : first + held].reshape(step, HD)
            return lax.dot_general(
                query, tokens_of(0, middle), (((1,), (1,)), ((), ())), preferred_element_type=F32
            )

        coming = score(*tasks[0])
        for n, (middle, held, g) in enumerate(tasks):
            current = coming
            if n + 1 < len(tasks):
                coming = score(*tasks[n + 1])
            lines = slice(n * step, (n + 1) * step)
            peak = jnp.broadcast_to(jnp.max(current, axis=-1, keepdims=True), (step, HD))
            if state is not None:
                old = before[0][lines, :]
                peak = jnp.maximum(peak, old)
            wide = jnp.concatenate([peak] * (length // HD), axis=1)
            weights = jnp.exp2((current - wide) * FACTOR)
            total = jnp.broadcast_to(jnp.sum(weights, axis=-1, keepdims=True), (step, HD))
            summed = jnp.dot(
                weights.astype(BF16), tokens_of(2, middle), preferred_element_type=F32
            )
            if state is None:
                outs[0][lines, :] = peak
                outs[1][lines, :] = total
                outs[2][lines, :] = summed
                continue
            scale = jnp.exp2((old - peak) * FACTOR)
            total = total + before[1][lines, :] * scale
            summed = summed + before[2][lines, :] * scale
            several = step // held
            outs[0][g : g + several, middle * rows : middle * rows + held] = (
                (summed * (sign / total)).astype(BF16).reshape(several, held, HD)
            )
        if state is not None:
            outs[1][...] = jnp.broadcast_to(noise_level(info_ref), (8, HD))
        for copy in holding:
            copy.wait()

    shape = ((UNITS, 3 * half, HD), BF16)
    made = tuple((h.shape, BF16) for h in hold)
    return kernel(
        body,
        "attend",
        info,
        tuple(hold),
        (queries, pairs, *(state or ())),
        made + ((((tokens, HD), F32),) * 3 if state is None else (shape, ((8, HD), F32))),
        24,
        4 * tokens * length * HD,
        4 * HD * (tokens + length),
        tokens * length,
        scratch=(pltpu.SemaphoreType.DMA((count,)),),
    )


def expand(info, attn, mine, other):
    _, size, _ = attn.shape
    half = size // 3
    rows, panel = 2 * half, 3 * HD
    columns = mine[0].shape[1]
    part = columns // Y

    def body(info_ref, attn_ref, *refs):
        weights, (to_x, *to_y, own_y, own_x, left) = refs[:4], refs[4:]
        for unit in range(UNITS):
            model, clip, j = unit // 4, unit // 2 % 2, unit % 2
            lane = model * panel
            line = lax.rem(clip + info_ref[AT_CORE], 2) * rows
            left[
                pl.ds(pl.multiple_of(line, rows), rows),
                lane + 2 * j * HD : lane + (2 * j + 1) * HD,
            ] = attn_ref[unit, :rows]
            line += j * half
            left[pl.ds(pl.multiple_of(line, half), half), lane + HD : lane + 2 * HD] = attn_ref[
                unit, rows:
            ]
        for i in range(0, 8, 2):
            place = slice(i % 4 * part, (i % 4 + 2) * part)
            right = jnp.concatenate([w[:, place] for w in weights[i // 4 * 2 : i // 4 * 2 + 2]])
            value = jnp.dot(left[...], right, preferred_element_type=F32)
            xh = info_ref[AT_CORE] if i < 4 else 1 - info_ref[AT_CORE]
            here = xh == info_ref[AT_XH]
            for n in range(2):
                y = i % 4 + n
                shift = lax.rem(y - info_ref[AT_Y] + Y, Y)
                first = value[:rows, n * part : (n + 1) * part]
                second = value[rows:, n * part : (n + 1) * part]
                for f, target in enumerate((own_y, *to_y)):

                    @pl.when(shift == f)
                    def _():
                        target[xh] = first.astype(target.dtype)

                @pl.when(here)
                def _():
                    own_x[y] = second

                @pl.when(jnp.logical_not(here))
                def _():
                    to_x[y] = second.astype(BF16)

    by_x, by_y = (Y, rows, part), (XH, rows, part)
    return kernel(
        body,
        "expand",
        info,
        (),
        (attn, *mine, *other),
        ((by_x, BF16), *[(by_y, BF16)] * (Y - 1), (by_y, F32), (by_x, F32)),
        12,
        16 * rows * panel * columns,
        8 * panel * columns,
        scratch=(pltpu.VMEM((2 * rows, 2 * panel), BF16),),
    )


def turn(info, own_y, own_x, from_x, from_y):
    _, rows, part = own_y.shape

    def body(info_ref, own_y_ref, own_x_ref, from_x_ref, *refs):
        from_y_refs, (keep_a, keep_b, to_x, *to_y) = refs[: Y - 1], refs[Y - 1 :]
        xh, y = info_ref[AT_XH], info_ref[AT_Y]
        for out, place in ((to_x, 1 - xh), (keep_a, xh)):
            total = own_y_ref[place]
            for ref in from_y_refs:
                total = total + ref[place].astype(F32)
            out[...] = total.astype(out.dtype)
        for f, out in enumerate((keep_b, *to_y)):
            place = lax.rem(y + f, Y)
            total = own_x_ref[place] + from_x_ref[place].astype(F32)
            out[...] = total.astype(out.dtype)

    shape = (rows, part)
    return kernel(
        body,
        "turn",
        info,
        (),
        (own_y, own_x, from_x, *from_y),
        ((shape, F32), (shape, F32), *[(shape, BF16)] * Y),
        8,
        12 * rows * part,
        60 * rows * part,
    )


def collect(info, level, own, from_x, other, from_y):
    rows, width = own.shape

    def body(info_ref, level_ref, own_ref, x_ref, other_ref, *refs):
        y_refs, out_ref = refs[:-1], refs[-1]
        level = level_ref[:1, :1]
        core = info_ref[AT_CORE]
        for part, terms in ((core, (own_ref, x_ref)), (1 - core, (other_ref, *y_refs))):
            total = terms[0][...]
            for ref in terms[1:]:
                total = total + ref[...].astype(F32)
            place = pl.ds(pl.multiple_of(part * rows, rows), rows)
            out_ref[place, :] = (level * total).astype(BF16)

    operands = (level, own, from_x, other, *from_y)
    return pl.pallas_call(
        body,
        in_specs=[SCALAR] + [NEAR] * len(operands),
        out_specs=NEAR,
        out_shape=jax.ShapeDtypeStruct((2 * rows, width), BF16),
        compiler_params=pltpu.CompilerParams(vmem_limit_bytes=4 * MIB),
        name="collect",
    )(info, *[in_vmem(x) for x in operands])


def local(
    clean,
    noise,
    timestep,
    teacher_gain,
    critic_gain,
    teacher_qkv,
    critic_qkv,
    teacher_out,
    critic_out,
):
    tp = lax.axis_index("tp")
    places = [lax.axis_index("dp"), lax.axis_index("ctx"), timestep[0], tp // Y, tp % Y]
    info = lax.optimization_barrier(jnp.stack(places).astype(jnp.int32))

    weights = [jnp.transpose(w, (1, 0, 2)) for w in (teacher_qkv, critic_qkv)]
    keep, away, weights_t = norm(
        info, clean[0], noise[0], teacher_gain, critic_gain, weights[0]
    )
    came = swapped(away)
    *own_t, most_c = project(info, 0, keep, (weights_t,), hold=weights[1])
    outs = (teacher_out, critic_out)
    other = [swapped(out) for out in outs]
    *own_c, last_c = project(info, 1, keep, (most_c,), fetch=weights[1])
    cross_t = project(info, 0, came, (weights_t,))
    cross_c = [project(info, 1, came, (most_c, last_c), halves=(i,))[0] for i in range(2)]
    blocks = None
    for own, cross in ((own_t, cross_t), (own_c, cross_c)):
        parts = (own[0], swapped(cross[0]), cross[1], swapped(own[1]))
        blocks = join(info, parts, blocks)

    block = exchange(blocks, "ctx")
    *mine, peak, total, summed = attend(info, block, block, [in_hbm(out) for out in outs])
    *other, attn, level = attend(info, block, swapped(block), other, (peak, total, summed))
    to_x, *to_y, own_y, own_x = expand(info, exchange(attn, "ctx"), mine, other)
    from_x = over_tp(to_x, 1, 0)
    from_y = [over_tp(value, 0, f) for f, value in enumerate(to_y, 1)]
    own, other, to_x, *to_y = turn(info, own_y, own_x, from_x, from_y)
    from_x = over_tp(to_x, 1, 0)
    from_y = [over_tp(value, 0, f, 1) for f, value in enumerate(to_y, 1)]
    return collect(info, level, own, from_x, swapped(other), from_y)[None]


def solution(mesh):
    placed = (
        P("dp", "ctx", None),
        P("dp", "ctx", None),
        P("dp"),
        P(),
        P(),
        P("dp", None, "tp"),
        P("dp", None, "tp"),
        P("tp", "dp"),
        P("tp", "dp"),
    )
    return jax.shard_map(
        local, mesh=mesh, in_specs=placed, out_specs=P("dp", "ctx", "tp"), check_vma=False
    )
```

```python
import jax
import jax.numpy as jnp
import numpy as np
from jax import lax
from jax.experimental import pallas as pl
from jax.experimental.pallas import tpu as pltpu
from jax.sharding import PartitionSpec as P

HD = 128
MIB = 1024 * 1024
XH, Y = 2, 4


def over_tp(value, xh, y, core=0):
    pairs = [
        ((d * XH + e) * Y + f, ((d + core) % 2 * XH + (e + xh) % XH) * Y + (f + y) % Y)
        for d in range(2)
        for e in range(XH)
        for f in range(Y)
    ]
    return lax.ppermute(value, ("dp", "tp"), pairs)


def swapped(value):
    return lax.ppermute(value, "dp", [(0, 1), (1, 0)])


def exchange(value, axes):
    return lax.all_to_all(value, axes, 0, 0, tiled=True)


def in_hbm(value):
    return pltpu.with_memory_space_constraint(value, pltpu.HBM)


def in_vmem(value):
    return pltpu.with_memory_space_constraint(value, pltpu.VMEM)


SCALAR = pl.BlockSpec(memory_space=pltpu.SMEM)
NEAR = pl.BlockSpec(memory_space=pltpu.VMEM)
ANYWHERE = pl.BlockSpec(memory_space=pl.ANY)


def kernel(body, name, info, far, near, made, mib, flops, size, exps=0, scratch=(), loose=()):
    return pl.pallas_call(
        body,
        in_specs=[SCALAR] + [ANYWHERE] * len(far) + [NEAR] * len(near),
        out_specs=[NEAR] * len(made) + [ANYWHERE] * len(loose),
        out_shape=[pltpu.VMEM(shape, dtype) for shape, dtype in made]
        + [pltpu.HBM(shape, dtype) for shape, dtype in loose],
        scratch_shapes=list(scratch),
        compiler_params=pltpu.CompilerParams(vmem_limit_bytes=mib * MIB),
        cost_estimate=pl.CostEstimate(flops=flops, bytes_accessed=size, transcendentals=exps),
        name=name,
    )(
        info,
        *far,
        *[in_vmem(x) for x in near],
    )


BF16, F32 = jnp.bfloat16, jnp.float32

AT_CORE, AT_CTX, AT_STEP, AT_XH, AT_Y = range(5)


def noise_level(info_ref):
    step = (jnp.full((1, 1), info_ref[AT_STEP], jnp.int32).astype(F32) + 1.0) / 1000.0
    return 5.0 * step / (1.0 + 4.0 * step)


def norm_kernel(
    info_ref, clean_ref, noise_ref, gt_ref, gc_ref, w_ref,
    keep_ref, send_ref, held_ref,
    clean_buf, noise_buf, noisy_ref, gt_buf, gc_buf, in_sem, w_sem,
):
    tokens, width = clean_buf.shape
    rows = noisy_ref.shape[0]
    count = tokens // rows
    half = width // 2
    core = info_ref[AT_CORE]

    def arrival(i):
        part = pl.ds(pl.multiple_of(i * rows, rows), rows)
        return (
            pltpu.make_async_copy(clean_ref.at[part], clean_buf.at[part], in_sem.at[0, i]),
            pltpu.make_async_copy(noise_ref.at[part], noise_buf.at[part], in_sem.at[1, i]),
        )

    kinds = w_ref.shape[0]
    held = [
        pltpu.make_async_copy(w_ref.at[j], held_ref.at[j], w_sem.at[j]) for j in range(kinds)
    ]
    gains = [
        pltpu.make_async_copy(gt_ref, gt_buf, w_sem.at[kinds]),
        pltpu.make_async_copy(gc_ref, gc_buf, w_sem.at[kinds + 1]),
    ]
    for copy in gains:
        copy.start()
    for i in range(count):
        for copy in arrival(i):
            copy.start()
    for copy in held:
        copy.start()
    level = noise_level(info_ref)
    for copy in gains:
        copy.wait()

    @pl.loop(0, count)
    def _(i):
        for copy in arrival(i):
            copy.wait()
        part = pl.ds(pl.multiple_of(i * rows, rows), rows)
        squares = jnp.zeros((rows, HD), F32)
        for t in range(width // HD):
            columns = slice(t * HD, (t + 1) * HD)
            noisy = (1.0 - level) * clean_buf[part, columns].astype(
                F32
            ) + level * noise_buf[part, columns].astype(F32)
            noisy_ref[:, columns] = noisy
            squares += noisy * noisy
        mean = jnp.sum(squares, axis=-1, keepdims=True) / width
        inverse = jnp.broadcast_to(lax.rsqrt(mean + 1e-06), (rows, HD))
        place = lax.rem(i + core * (count // 2), count)
        place = pl.ds(pl.multiple_of(place * rows, rows), rows)
        for out, which in ((send_ref, 1 - core), (keep_ref, core)):
            for t in range(half // HD):
                tile = which * (half // HD) + t
                columns = pl.ds(pl.multiple_of(tile * HD, HD), HD)
                scaled = noisy_ref[:, columns] * inverse
                out[0, place, t * HD : (t + 1) * HD] = (
                    scaled * gt_buf[pl.ds(tile, 1), :]
                ).astype(BF16)
                out[1, place, t * HD : (t + 1) * HD] = (
                    scaled * gc_buf[pl.ds(tile, 1), :]
                ).astype(BF16)

    for copy in held:
        copy.wait()


def norm(info, clean, noise, gt, gc, w):
    tokens, width = clean.shape
    rows = 32
    count = tokens // rows
    tiles = (width // HD, HD)
    shape = ((2, tokens, width // 2), BF16)
    return kernel(
        norm_kernel,
        "norm",
        info,
        tuple(in_hbm(x) for x in (clean, noise, gt.reshape(tiles), gc.reshape(tiles), w)),
        (),
        (shape, shape, (w.shape, w.dtype)),
        16,
        10 * tokens * width,
        8 * tokens * width,
        scratch=(
            pltpu.VMEM((tokens, width), BF16),
            pltpu.VMEM((tokens, width), BF16),
            pltpu.VMEM((rows, width), F32),
            pltpu.VMEM(tiles, F32),
            pltpu.VMEM(tiles, F32),
            pltpu.SemaphoreType.DMA((2, count)),
            pltpu.SemaphoreType.DMA((w.shape[0] + 2,)),
        ),
    )


def project(info, model, a, weights, hold=None, fetch=None, halves=(0, 1)):
    _, tokens, depth = a.shape
    panel = weights[0].shape[-1]
    kinds = 3
    half = tokens // 2
    lines = slice(halves[0] * half, (halves[-1] + 1) * half)
    made = (((kinds, half, panel), F32),) * len(halves)
    if hold is not None:
        made += (((kinds - 1, depth, panel), BF16),)
    if fetch is not None:
        made += (((1, depth, panel), BF16),)
    far = tuple(in_hbm(w) for w in (hold, fetch) if w is not None)

    def body(info_ref, *refs):
        sources, rest = refs[: len(far)], refs[len(far) :]
        a_ref, *w_refs = rest[: 1 + len(weights)]
        *outs, sem = rest[1 + len(weights) :]
        outs, brought = outs[: len(halves)], outs[len(halves) :]
        first = 0 if fetch is None else kinds - 1
        copies = [
            pltpu.make_async_copy(sources[0].at[first + j], brought[0].at[j], sem.at[j])
            for j in range(brought[0].shape[0] if far else 0)
        ]
        for copy in copies:
            copy.start()

        def product(slices, j):
            value = jnp.dot(
                a_ref[model, lines], jnp.concatenate(slices, axis=1), preferred_element_type=F32
            )
            for n in range(len(slices)):
                part = value[:, n * panel : (n + 1) * panel]
                for i, out in enumerate(outs):
                    out[j + n] = part[i * half : (i + 1) * half]

        product([w[j] for w in w_refs for j in range(w.shape[0])], 0)
        for copy in copies:
            copy.wait()
        if fetch is not None:
            product([brought[0][0]], kinds - 1)

    return kernel(
        body,
        "project",
        info,
        far,
        (a, *weights),
        made,
        8,
        2 * half * len(halves) * depth * panel * kinds,
        2 * depth * (tokens + panel * kinds),
        scratch=(pltpu.SemaphoreType.DMA((kinds,)),),
    )


UNITS = 8


def join(info, parts, done=None):
    _, rows, panel = parts[0].shape
    half = rows // 2
    shape = (UNITS, 5 * rows + half, HD)
    part = (4, *shape[1:])

    def body(info_ref, *refs):
        inputs, rest = refs[: len(parts)], refs[len(parts) :]
        copies = []

        def leave(source, model, which):
            clip = info_ref[AT_CORE] if which == 0 else 1 - info_ref[AT_CORE]
            copies.append(
                pltpu.make_async_copy(
                    source.at[pl.ds(2 * which, 2)],
                    target.at[pl.ds(4 * model + 2 * clip, 2)],
                    sem.at[2 * model + which],
                )
            )
            copies[-1].start()

        if done is None:
            (out,) = rest
        else:
            teacher, target, out, sem = rest
            leave(teacher, 0, 0)
            leave(teacher, 0, 1)
        for which in range(2):
            left, right = inputs[2 * which : 2 * which + 2]
            for kind, base in ((1, 0), (2, 2 * rows), (0, 4 * rows)):
                value = (left[kind] + right[kind]).astype(BF16)
                for j in range(2):
                    block = 2 * which + j
                    out[block, base : base + rows] = value[:, 2 * j * HD : (2 * j + 1) * HD]
                    middle = value[:, HD : 2 * HD]
                    if kind == 0:
                        middle = middle[j * half : (j + 1) * half]
                    out[block, base + rows : base + rows + middle.shape[0]] = middle
            if done is not None:
                leave(out, 1, which)
        for copy in copies:
            copy.wait()

    return kernel(
        body,
        "join",
        info,
        (),
        parts if done is None else (*parts, done),
        ((part, BF16),) if done is None else (),
        8,
        6 * rows * panel,
        60 * rows * panel,
        scratch=()
        if done is None
        else (pltpu.VMEM(part, BF16), pltpu.SemaphoreType.DMA((4,))),
        loose=() if done is None else ((shape, BF16),),
    )[0]


FACTOR = float(np.log2(np.e)) * HD**-0.5


def attend(info, queries, pairs, hold, state=None):
    _, size, _ = queries.shape
    half = size // 11
    rows = 2 * half
    tokens, length = 3 * half * UNITS, rows * UNITS
    step = 256
    count = len(hold)
    tasks = [
        (middle, held, g)
        for middle, held in ((0, rows), (1, half))
        for g in range(0, UNITS, step // held)
    ]

    def body(info_ref, *refs):
        sources, (q_ref, kv_ref, *rest) = refs[:count], refs[count:]
        before = ()
        if state is not None:
            before, rest = rest[:3], rest[3:]
        held_refs, rest = rest[:count], rest[count:]
        *outs, sem = rest
        holding = [
            pltpu.make_async_copy(source, place, sem.at[i])
            for i, (source, place) in enumerate(zip(sources, held_refs))
        ]
        for copy in holding:
            copy.start()
        sign = 1.0 - 2.0 * (info_ref[AT_CTX] // 4).astype(F32)

        def tokens_of(kind, middle):
            first = (kind + middle) * rows
            return kv_ref[:, first : first + rows].reshape(length, HD)

        def score(middle, held, g):
            first = (4 + middle) * rows
            query = q_ref[g : g + step // held, first : first + held].reshape(step, HD)
            return lax.dot_general(
                query, tokens_of(0, middle), (((1,), (1,)), ((), ())), preferred_element_type=F32
            )

        coming = score(*tasks[0])
        for n, (middle, held, g) in enumerate(tasks):
            current = coming
            if n + 1 < len(tasks):
                coming = score(*tasks[n + 1])
            lines = slice(n * step, (n + 1) * step)
            peak = jnp.broadcast_to(jnp.max(current, axis=-1, keepdims=True), (step, HD))
            if state is not None:
                old = before[0][lines, :]
                peak = jnp.maximum(peak, old)
            wide = jnp.concatenate([peak] * (length // HD), axis=1)
            weights = jnp.exp2((current - wide) * FACTOR)
            total = jnp.broadcast_to(jnp.sum(weights, axis=-1, keepdims=True), (step, HD))
            summed = jnp.dot(
                weights.astype(BF16), tokens_of(2, middle), preferred_element_type=F32
            )
            if state is None:
                outs[0][lines, :] = peak
                outs[1][lines, :] = total
                outs[2][lines, :] = summed
                continue
            scale = jnp.exp2((old - peak) * FACTOR)
            total = total + before[1][lines, :] * scale
            summed = summed + before[2][lines, :] * scale
            several = step // held
            outs[0][g : g + several, middle * rows : middle * rows + held] = (
                (summed * (sign / total)).astype(BF16).reshape(several, held, HD)
            )
        if state is not None:
            outs[1][...] = jnp.broadcast_to(noise_level(info_ref), (8, HD))
        for copy in holding:
            copy.wait()

    shape = ((UNITS, 3 * half, HD), BF16)
    made = tuple((h.shape, BF16) for h in hold)
    return kernel(
        body,
        "attend",
        info,
        tuple(hold),
        (queries, pairs, *(state or ())),
        made + ((((tokens, HD), F32),) * 3 if state is None else (shape, ((8, HD), F32))),
        24,
        4 * tokens * length * HD,
        4 * HD * (tokens + length),
        tokens * length,
        scratch=(pltpu.SemaphoreType.DMA((count,)),),
    )


def expand(info, attn, mine, other, leaving):
    _, size, _ = attn.shape
    half = size // 3
    rows, panel = 2 * half, 3 * HD
    part = mine[0].shape[1] // Y
    shifts = range(1, Y) if leaving else (0,)

    def body(info_ref, attn_ref, *refs):
        weights, (by_x, *by_y, left) = refs[:4], refs[4:]
        core = info_ref[AT_CORE]
        for unit in range(UNITS):
            model, clip, j = unit // 4, unit // 2 % 2, unit % 2
            lane = model * panel
            line = lax.rem(clip + core, 2) * rows
            left[
                pl.ds(pl.multiple_of(line, rows), rows),
                lane + 2 * j * HD : lane + (2 * j + 1) * HD,
            ] = attn_ref[unit, :rows]
            line += j * half
            left[pl.ds(pl.multiple_of(line, half), half), lane + HD : lane + 2 * HD] = attn_ref[
                unit, rows:
            ]

        def over_x(pair):
            for y in range(0, Y, 2):
                columns = slice(y * part, (y + 2) * part)
                right = jnp.concatenate([w[:, columns] for w in pair])
                value = jnp.dot(left[rows:], right, preferred_element_type=F32)
                for n in range(2):
                    by_x[y + n] = value[:, n * part : (n + 1) * part].astype(by_x.dtype)

        near = (core == info_ref[AT_XH]) != leaving
        pl.when(near)(lambda: over_x(weights[:2]))
        pl.when(jnp.logical_not(near))(lambda: over_x(weights[2:]))
        for shift, out in zip(shifts, by_y):
            place = lax.rem(info_ref[AT_Y] + shift, Y) * part
            columns = pl.ds(pl.multiple_of(place, HD), part)
            right = jnp.concatenate(
                [
                    jnp.concatenate([w[:, columns] for w in pair])
                    for pair in (weights[:2], weights[2:])
                ],
                axis=1,
            )
            value = jnp.dot(left[:rows], right, preferred_element_type=F32).astype(out.dtype)
            out[core] = value[:, :part]
            out[1 - core] = value[:, part:]

    kind = BF16 if leaving else F32
    return kernel(
        body,
        "expand",
        info,
        (),
        (attn, *mine, *other),
        (((Y, rows, part), kind), *[((XH, rows, part), kind)] * len(shifts)),
        12,
        8 * rows * panel * part * Y,
        8 * panel * part * Y,
        scratch=(pltpu.VMEM((2 * rows, 2 * panel), BF16),),
    )


def turn(info, own_y, own_x, from_x, from_y):
    _, rows, part = own_y.shape

    def body(info_ref, own_y_ref, own_x_ref, from_x_ref, *refs):
        from_y_refs, (keep_a, keep_b, to_x, *to_y) = refs[: Y - 1], refs[Y - 1 :]
        xh, y = info_ref[AT_XH], info_ref[AT_Y]
        for out, place in ((to_x, 1 - xh), (keep_a, xh)):
            total = own_y_ref[place]
            for ref in from_y_refs:
                total = total + ref[place].astype(F32)
            out[...] = total.astype(out.dtype)
        for f, out in enumerate((keep_b, *to_y)):
            place = lax.rem(y + f, Y)
            total = own_x_ref[place] + from_x_ref[place].astype(F32)
            out[...] = total.astype(out.dtype)

    shape = (rows, part)
    return kernel(
        body,
        "turn",
        info,
        (),
        (own_y, own_x, from_x, *from_y),
        ((shape, F32), (shape, F32), *[(shape, BF16)] * Y),
        8,
        12 * rows * part,
        60 * rows * part,
    )


def collect(info, level, own, from_x, other, from_y):
    rows, width = own.shape

    def body(info_ref, level_ref, own_ref, x_ref, other_ref, *refs):
        y_refs, out_ref = refs[:-1], refs[-1]
        level = level_ref[:1, :1]
        core = info_ref[AT_CORE]
        for part, terms in ((core, (own_ref, x_ref)), (1 - core, (other_ref, *y_refs))):
            total = terms[0][...]
            for ref in terms[1:]:
                total = total + ref[...].astype(F32)
            place = pl.ds(pl.multiple_of(part * rows, rows), rows)
            out_ref[place, :] = (level * total).astype(BF16)

    operands = (level, own, from_x, other, *from_y)
    return pl.pallas_call(
        body,
        in_specs=[SCALAR] + [NEAR] * len(operands),
        out_specs=NEAR,
        out_shape=jax.ShapeDtypeStruct((2 * rows, width), BF16),
        compiler_params=pltpu.CompilerParams(vmem_limit_bytes=4 * MIB),
        name="collect",
    )(info, *[in_vmem(x) for x in operands])


def local(
    clean,
    noise,
    timestep,
    teacher_gain,
    critic_gain,
    teacher_qkv,
    critic_qkv,
    teacher_out,
    critic_out,
):
    tp = lax.axis_index("tp")
    places = [lax.axis_index("dp"), lax.axis_index("ctx"), timestep[0], tp // Y, tp % Y]
    info = lax.optimization_barrier(jnp.stack(places).astype(jnp.int32))

    weights = [jnp.transpose(w, (1, 0, 2)) for w in (teacher_qkv, critic_qkv)]
    keep, away, weights_t = norm(
        info, clean[0], noise[0], teacher_gain, critic_gain, weights[0]
    )
    came = swapped(away)
    *own_t, most_c = project(info, 0, keep, (weights_t,), hold=weights[1])
    outs = (teacher_out, critic_out)
    other = [swapped(out) for out in outs]
    *own_c, last_c = project(info, 1, keep, (most_c,), fetch=weights[1])
    cross_t = project(info, 0, came, (weights_t,))
    cross_c = [project(info, 1, came, (most_c, last_c), halves=(i,))[0] for i in range(2)]
    blocks = None
    for own, cross in ((own_t, cross_t), (own_c, cross_c)):
        parts = (own[0], swapped(cross[0]), cross[1], swapped(own[1]))
        blocks = join(info, parts, blocks)

    block = exchange(blocks, "ctx")
    *mine, peak, total, summed = attend(info, block, block, [in_hbm(out) for out in outs])
    *other, attn, level = attend(info, block, swapped(block), other, (peak, total, summed))
    attn = exchange(attn, "ctx")
    to_x, *to_y = expand(info, attn, mine, other, True)
    from_x = over_tp(to_x, 1, 0)
    from_y = [over_tp(value, 0, f) for f, value in enumerate(to_y, 1)]
    own_x, own_y = expand(info, attn, mine, other, False)
    own, other, to_x, *to_y = turn(info, own_y, own_x, from_x, from_y)
    from_x = over_tp(to_x, 1, 0)
    from_y = [over_tp(value, 0, f, 1) for f, value in enumerate(to_y, 1)]
    return collect(info, level, own, from_x, swapped(other), from_y)[None]


def solution(mesh):
    placed = (
        P("dp", "ctx", None),
        P("dp", "ctx", None),
        P("dp"),
        P(),
        P(),
        P("dp", None, "tp"),
        P("dp", None, "tp"),
        P("tp", "dp"),
        P("tp", "dp"),
    )
    return jax.shard_map(
        local, mesh=mesh, in_specs=placed, out_specs=P("dp", "ctx", "tp"), check_vma=False
    )
```

```python
import jax
import jax.numpy as jnp
import numpy as np
from jax import lax
from jax.experimental import pallas as pl
from jax.experimental.pallas import tpu as pltpu
from jax.sharding import PartitionSpec as P

HD = 128
MIB = 1024 * 1024
XH, Y = 2, 4


def over_tp(value, xh, y, core=0):
    pairs = [
        ((d * XH + e) * Y + f, ((d + core) % 2 * XH + (e + xh) % XH) * Y + (f + y) % Y)
        for d in range(2)
        for e in range(XH)
        for f in range(Y)
    ]
    return lax.ppermute(value, ("dp", "tp"), pairs)


def swapped(value):
    return lax.ppermute(value, "dp", [(0, 1), (1, 0)])


def exchange(value, axes):
    return lax.all_to_all(value, axes, 0, 0, tiled=True)


def in_hbm(value):
    return pltpu.with_memory_space_constraint(value, pltpu.HBM)


def in_vmem(value):
    return pltpu.with_memory_space_constraint(value, pltpu.VMEM)


SCALAR = pl.BlockSpec(memory_space=pltpu.SMEM)
NEAR = pl.BlockSpec(memory_space=pltpu.VMEM)
ANYWHERE = pl.BlockSpec(memory_space=pl.ANY)


def kernel(body, name, info, far, near, made, mib, flops, size, exps=0, scratch=(), loose=()):
    return pl.pallas_call(
        body,
        in_specs=[SCALAR] + [ANYWHERE] * len(far) + [NEAR] * len(near),
        out_specs=[NEAR] * len(made) + [ANYWHERE] * len(loose),
        out_shape=[pltpu.VMEM(shape, dtype) for shape, dtype in made]
        + [pltpu.HBM(shape, dtype) for shape, dtype in loose],
        scratch_shapes=list(scratch),
        compiler_params=pltpu.CompilerParams(vmem_limit_bytes=mib * MIB),
        cost_estimate=pl.CostEstimate(flops=flops, bytes_accessed=size, transcendentals=exps),
        name=name,
    )(
        info,
        *far,
        *[in_vmem(x) for x in near],
    )


BF16, F32 = jnp.bfloat16, jnp.float32

AT_CORE, AT_CTX, AT_STEP, AT_XH, AT_Y = range(5)


def noise_level(info_ref):
    step = (jnp.full((1, 1), info_ref[AT_STEP], jnp.int32).astype(F32) + 1.0) / 1000.0
    return 5.0 * step / (1.0 + 4.0 * step)


def norm_kernel(
    info_ref, clean_ref, noise_ref, gt_ref, gc_ref, w_ref,
    keep_ref, send_ref, held_ref,
    clean_buf, noise_buf, noisy_ref, gt_buf, gc_buf, in_sem, w_sem,
):
    tokens, width = clean_buf.shape
    rows = noisy_ref.shape[0]
    count = tokens // rows
    half = width // 2
    core = info_ref[AT_CORE]

    def arrival(i):
        part = pl.ds(pl.multiple_of(i * rows, rows), rows)
        return (
            pltpu.make_async_copy(clean_ref.at[part], clean_buf.at[part], in_sem.at[0, i]),
            pltpu.make_async_copy(noise_ref.at[part], noise_buf.at[part], in_sem.at[1, i]),
        )

    kinds = w_ref.shape[0]
    held = [
        pltpu.make_async_copy(w_ref.at[j], held_ref.at[j], w_sem.at[j]) for j in range(kinds)
    ]
    gains = [
        pltpu.make_async_copy(gt_ref, gt_buf, w_sem.at[kinds]),
        pltpu.make_async_copy(gc_ref, gc_buf, w_sem.at[kinds + 1]),
    ]
    for copy in gains:
        copy.start()
    for i in range(count):
        for copy in arrival(i):
            copy.start()
    for copy in held:
        copy.start()
    level = noise_level(info_ref)
    for copy in gains:
        copy.wait()

    @pl.loop(0, count)
    def _(i):
        for copy in arrival(i):
            copy.wait()
        part = pl.ds(pl.multiple_of(i * rows, rows), rows)
        squares = jnp.zeros((rows, HD), F32)
        for t in range(width // HD):
            columns = slice(t * HD, (t + 1) * HD)
            noisy = (1.0 - level) * clean_buf[part, columns].astype(
                F32
            ) + level * noise_buf[part, columns].astype(F32)
            noisy_ref[:, columns] = noisy
            squares += noisy * noisy
        mean = jnp.sum(squares, axis=-1, keepdims=True) / width
        inverse = jnp.broadcast_to(lax.rsqrt(mean + 1e-06), (rows, HD))
        place = lax.rem(i + core * (count // 2), count)
        place = pl.ds(pl.multiple_of(place * rows, rows), rows)
        for out, which in ((send_ref, 1 - core), (keep_ref, core)):
            for t in range(half // HD):
                tile = which * (half // HD) + t
                columns = pl.ds(pl.multiple_of(tile * HD, HD), HD)
                scaled = noisy_ref[:, columns] * inverse
                out[0, place, t * HD : (t + 1) * HD] = (
                    scaled * gt_buf[pl.ds(tile, 1), :]
                ).astype(BF16)
                out[1, place, t * HD : (t + 1) * HD] = (
                    scaled * gc_buf[pl.ds(tile, 1), :]
                ).astype(BF16)

    for copy in held:
        copy.wait()


def norm(info, clean, noise, gt, gc, w):
    tokens, width = clean.shape
    rows = 64
    count = tokens // rows
    tiles = (width // HD, HD)
    shape = ((2, tokens, width // 2), BF16)
    return kernel(
        norm_kernel,
        "norm",
        info,
        tuple(in_hbm(x) for x in (clean, noise, gt.reshape(tiles), gc.reshape(tiles), w)),
        (),
        (shape, shape, (w.shape, w.dtype)),
        16,
        10 * tokens * width,
        8 * tokens * width,
        scratch=(
            pltpu.VMEM((tokens, width), BF16),
            pltpu.VMEM((tokens, width), BF16),
            pltpu.VMEM((rows, width), F32),
            pltpu.VMEM(tiles, F32),
            pltpu.VMEM(tiles, F32),
            pltpu.SemaphoreType.DMA((2, count)),
            pltpu.SemaphoreType.DMA((w.shape[0] + 2,)),
        ),
    )


def project(info, model, a, weights, hold=None, fetch=None, halves=(0, 1)):
    _, tokens, depth = a.shape
    panel = weights[0].shape[-1]
    kinds = 3
    half = tokens // 2
    lines = slice(halves[0] * half, (halves[-1] + 1) * half)
    made = (((kinds, half, panel), F32),) * len(halves)
    if hold is not None:
        made += (((kinds - 1, depth, panel), BF16),)
    if fetch is not None:
        made += (((1, depth, panel), BF16),)
    far = tuple(in_hbm(w) for w in (hold, fetch) if w is not None)

    def body(info_ref, *refs):
        sources, rest = refs[: len(far)], refs[len(far) :]
        a_ref, *w_refs = rest[: 1 + len(weights)]
        *outs, sem = rest[1 + len(weights) :]
        outs, brought = outs[: len(halves)], outs[len(halves) :]
        first = 0 if fetch is None else kinds - 1
        copies = [
            pltpu.make_async_copy(sources[0].at[first + j], brought[0].at[j], sem.at[j])
            for j in range(brought[0].shape[0] if far else 0)
        ]
        for copy in copies:
            copy.start()

        def product(slices, j):
            value = jnp.dot(
                a_ref[model, lines], jnp.concatenate(slices, axis=1), preferred_element_type=F32
            )
            for n in range(len(slices)):
                part = value[:, n * panel : (n + 1) * panel]
                for i, out in enumerate(outs):
                    out[j + n] = part[i * half : (i + 1) * half]

        product([w[j] for w in w_refs for j in range(w.shape[0])], 0)
        for copy in copies:
            copy.wait()
        if fetch is not None:
            product([brought[0][0]], kinds - 1)

    return kernel(
        body,
        "project",
        info,
        far,
        (a, *weights),
        made,
        8,
        2 * half * len(halves) * depth * panel * kinds,
        2 * depth * (tokens + panel * kinds),
        scratch=(pltpu.SemaphoreType.DMA((kinds,)),),
    )


UNITS = 8


def join(info, parts, done=None):
    _, rows, panel = parts[0].shape
    half = rows // 2
    shape = (UNITS, 5 * rows + half, HD)
    part = (4, *shape[1:])

    def body(info_ref, *refs):
        inputs, rest = refs[: len(parts)], refs[len(parts) :]
        copies = []

        def leave(source, model, which, base, size):
            lines = pl.ds(base, size)
            clip = info_ref[AT_CORE] if which == 0 else 1 - info_ref[AT_CORE]
            copies.append(
                pltpu.make_async_copy(
                    source.at[pl.ds(2 * which, 2), lines],
                    target.at[pl.ds(4 * model + 2 * clip, 2), lines],
                    sem.at[len(copies)],
                )
            )
            copies[-1].start()

        if done is None:
            (out,) = rest
        else:
            teacher, target, out, sem = rest
            leave(teacher, 0, 0, 0, shape[1])
            leave(teacher, 0, 1, 0, shape[1])
        for which in range(2):
            left, right = inputs[2 * which : 2 * which + 2]
            for kind, base in ((1, 0), (2, 2 * rows), (0, 4 * rows)):
                value = (left[kind] + right[kind]).astype(BF16)
                for j in range(2):
                    block = 2 * which + j
                    out[block, base : base + rows] = value[:, 2 * j * HD : (2 * j + 1) * HD]
                    middle = value[:, HD : 2 * HD]
                    if kind == 0:
                        middle = middle[j * half : (j + 1) * half]
                    out[block, base + rows : base + rows + middle.shape[0]] = middle
                if done is not None:
                    leave(out, 1, which, base, rows + middle.shape[0])
        for copy in copies:
            copy.wait()

    return kernel(
        body,
        "join",
        info,
        (),
        parts if done is None else (*parts, done),
        ((part, BF16),) if done is None else (),
        8,
        6 * rows * panel,
        60 * rows * panel,
        scratch=()
        if done is None
        else (pltpu.VMEM(part, BF16), pltpu.SemaphoreType.DMA((8,))),
        loose=() if done is None else ((shape, BF16),),
    )[0]


FACTOR = float(np.log2(np.e)) * HD**-0.5


def attend(info, queries, pairs, hold, state=None):
    _, size, _ = queries.shape
    half = size // 11
    rows = 2 * half
    tokens, length = 3 * half * UNITS, rows * UNITS
    step = 256
    count = len(hold)
    tasks = [
        (middle, held, g)
        for middle, held in ((0, rows), (1, half))
        for g in range(0, UNITS, step // held)
    ]

    def body(info_ref, *refs):
        sources, (q_ref, kv_ref, *rest) = refs[:count], refs[count:]
        before = ()
        if state is not None:
            before, rest = rest[:3], rest[3:]
        held_refs, rest = rest[:count], rest[count:]
        *outs, sem = rest
        holding = [
            pltpu.make_async_copy(source, place, sem.at[i])
            for i, (source, place) in enumerate(zip(sources, held_refs))
        ]
        for copy in holding:
            copy.start()
        sign = 1.0 - 2.0 * (info_ref[AT_CTX] // 4).astype(F32)

        def tokens_of(kind, middle):
            first = (kind + middle) * rows
            return kv_ref[:, first : first + rows].reshape(length, HD)

        def score(middle, held, g):
            first = (4 + middle) * rows
            query = q_ref[g : g + step // held, first : first + held].reshape(step, HD)
            return lax.dot_general(
                query, tokens_of(0, middle), (((1,), (1,)), ((), ())), preferred_element_type=F32
            )

        coming = score(*tasks[0])
        for n, (middle, held, g) in enumerate(tasks):
            current = coming
            if n + 1 < len(tasks):
                coming = score(*tasks[n + 1])
            lines = slice(n * step, (n + 1) * step)
            peak = jnp.broadcast_to(jnp.max(current, axis=-1, keepdims=True), (step, HD))
            if state is not None:
                old = before[0][lines, :]
                peak = jnp.maximum(peak, old)
            wide = jnp.concatenate([peak] * (length // HD), axis=1)
            weights = jnp.exp2((current - wide) * FACTOR)
            total = jnp.broadcast_to(jnp.sum(weights, axis=-1, keepdims=True), (step, HD))
            summed = jnp.dot(
                weights.astype(BF16), tokens_of(2, middle), preferred_element_type=F32
            )
            if state is None:
                outs[0][lines, :] = peak
                outs[1][lines, :] = total
                outs[2][lines, :] = summed
                continue
            scale = jnp.exp2((old - peak) * FACTOR)
            total = total + before[1][lines, :] * scale
            summed = summed + before[2][lines, :] * scale
            several = step // held
            outs[0][g : g + several, middle * rows : middle * rows + held] = (
                (summed * (sign / total)).astype(BF16).reshape(several, held, HD)
            )
        if state is not None:
            outs[1][...] = jnp.broadcast_to(noise_level(info_ref), (8, HD))
        for copy in holding:
            copy.wait()

    shape = ((UNITS, 3 * half, HD), BF16)
    made = tuple((h.shape, BF16) for h in hold)
    return kernel(
        body,
        "attend",
        info,
        tuple(hold),
        (queries, pairs, *(state or ())),
        made + ((((tokens, HD), F32),) * 3 if state is None else (shape, ((8, HD), F32))),
        24,
        4 * tokens * length * HD,
        4 * HD * (tokens + length),
        tokens * length,
        scratch=(pltpu.SemaphoreType.DMA((count,)),),
    )


def expand(info, attn, mine, other, leaving):
    _, size, _ = attn.shape
    half = size // 3
    rows, panel = 2 * half, 3 * HD
    part = mine[0].shape[1] // Y
    shifts = range(1, Y) if leaving else (0,)

    def body(info_ref, attn_ref, *refs):
        weights, (by_x, *by_y, left) = refs[:4], refs[4:]
        core = info_ref[AT_CORE]
        for unit in range(UNITS):
            model, clip, j = unit // 4, unit // 2 % 2, unit % 2
            lane = model * panel
            line = lax.rem(clip + core, 2) * rows
            left[
                pl.ds(pl.multiple_of(line, rows), rows),
                lane + 2 * j * HD : lane + (2 * j + 1) * HD,
            ] = attn_ref[unit, :rows]
            line += j * half
            left[pl.ds(pl.multiple_of(line, half), half), lane + HD : lane + 2 * HD] = attn_ref[
                unit, rows:
            ]

        def over_x(pair):
            for y in range(0, Y, 2):
                columns = slice(y * part, (y + 2) * part)
                right = jnp.concatenate([w[:, columns] for w in pair])
                value = jnp.dot(left[rows:], right, preferred_element_type=F32)
                for n in range(2):
                    by_x[y + n] = value[:, n * part : (n + 1) * part].astype(by_x.dtype)

        near = (core == info_ref[AT_XH]) != leaving
        pl.when(near)(lambda: over_x(weights[:2]))
        pl.when(jnp.logical_not(near))(lambda: over_x(weights[2:]))
        for shift, out in zip(shifts, by_y):
            place = lax.rem(info_ref[AT_Y] + shift, Y) * part
            columns = pl.ds(pl.multiple_of(place, HD), part)
            right = jnp.concatenate(
                [
                    jnp.concatenate([w[:, columns] for w in pair])
                    for pair in (weights[:2], weights[2:])
                ],
                axis=1,
            )
            value = jnp.dot(left[:rows], right, preferred_element_type=F32).astype(out.dtype)
            out[core] = value[:, :part]
            out[1 - core] = value[:, part:]

    kind = BF16 if leaving else F32
    return kernel(
        body,
        "expand",
        info,
        (),
        (attn, *mine, *other),
        (((Y, rows, part), kind), *[((XH, rows, part), kind)] * len(shifts)),
        12,
        8 * rows * panel * part * Y,
        8 * panel * part * Y,
        scratch=(pltpu.VMEM((2 * rows, 2 * panel), BF16),),
    )


def turn(info, own_y, own_x, from_x, from_y):
    _, rows, part = own_y.shape

    def body(info_ref, own_y_ref, own_x_ref, from_x_ref, *refs):
        from_y_refs, (keep_a, keep_b, to_x, *to_y) = refs[: Y - 1], refs[Y - 1 :]
        xh, y = info_ref[AT_XH], info_ref[AT_Y]
        for out, place in ((to_x, 1 - xh), (keep_a, xh)):
            total = own_y_ref[place]
            for ref in from_y_refs:
                total = total + ref[place].astype(F32)
            out[...] = total.astype(out.dtype)
        for f, out in enumerate((keep_b, *to_y)):
            place = lax.rem(y + f, Y)
            total = own_x_ref[place] + from_x_ref[place].astype(F32)
            out[...] = total.astype(out.dtype)

    shape = (rows, part)
    return kernel(
        body,
        "turn",
        info,
        (),
        (own_y, own_x, from_x, *from_y),
        ((shape, F32), (shape, F32), *[(shape, BF16)] * Y),
        8,
        12 * rows * part,
        60 * rows * part,
    )


def collect(info, level, own, from_x, other, from_y):
    rows, width = own.shape
    step = 32

    def body(info_ref, level_ref, own_ref, x_ref, other_ref, *refs):
        y_refs, out_ref = refs[:-1], refs[-1]
        level = level_ref[:1, :1]
        core = info_ref[AT_CORE]
        for part, terms in ((core, (own_ref, x_ref)), (1 - core, (other_ref, *y_refs))):
            for line in range(0, rows, step):
                lines = slice(line, line + step)
                total = terms[0][lines, :]
                for ref in terms[1:]:
                    total = total + ref[lines, :].astype(F32)
                place = pl.ds(pl.multiple_of(part * rows + line, step), step)
                out_ref[place, :] = (level * total).astype(BF16)

    operands = (level, own, from_x, other, *from_y)
    return pl.pallas_call(
        body,
        in_specs=[SCALAR] + [NEAR] * len(operands),
        out_specs=NEAR,
        out_shape=jax.ShapeDtypeStruct((2 * rows, width), BF16),
        compiler_params=pltpu.CompilerParams(vmem_limit_bytes=4 * MIB),
        name="collect",
    )(info, *[in_vmem(x) for x in operands])


def local(
    clean,
    noise,
    timestep,
    teacher_gain,
    critic_gain,
    teacher_qkv,
    critic_qkv,
    teacher_out,
    critic_out,
):
    tp = lax.axis_index("tp")
    places = [lax.axis_index("dp"), lax.axis_index("ctx"), timestep[0], tp // Y, tp % Y]
    info = lax.optimization_barrier(jnp.stack(places).astype(jnp.int32))

    weights = [jnp.transpose(w, (1, 0, 2)) for w in (teacher_qkv, critic_qkv)]
    keep, away, weights_t = norm(
        info, clean[0], noise[0], teacher_gain, critic_gain, weights[0]
    )
    came = swapped(away)
    *own_t, most_c = project(info, 0, keep, (weights_t,), hold=weights[1])
    outs = (teacher_out, critic_out)
    other = [swapped(out) for out in outs]
    *own_c, last_c = project(info, 1, keep, (most_c,), fetch=weights[1])
    cross_t = project(info, 0, came, (weights_t,))
    cross_c = [project(info, 1, came, (most_c, last_c), halves=(i,))[0] for i in range(2)]
    blocks = None
    for own, cross in ((own_t, cross_t), (own_c, cross_c)):
        parts = (own[0], swapped(cross[0]), cross[1], swapped(own[1]))
        blocks = join(info, parts, blocks)

    block = exchange(blocks, "ctx")
    *mine, peak, total, summed = attend(info, block, block, [in_hbm(out) for out in outs])
    *other, attn, level = attend(info, block, swapped(block), other, (peak, total, summed))
    attn = exchange(attn, "ctx")
    to_x, *to_y = expand(info, attn, mine, other, True)
    from_x = over_tp(to_x, 1, 0)
    from_y = [over_tp(value, 0, f) for f, value in enumerate(to_y, 1)]
    own_x, own_y = expand(info, attn, mine, other, False)
    own, other, to_x, *to_y = turn(info, own_y, own_x, from_x, from_y)
    from_x = over_tp(to_x, 1, 0)
    from_y = [over_tp(value, 0, f, 1) for f, value in enumerate(to_y, 1)]
    return collect(info, level, own, from_x, swapped(other), from_y)[None]


def solution(mesh):
    placed = (
        P("dp", "ctx", None),
        P("dp", "ctx", None),
        P("dp"),
        P(),
        P(),
        P("dp", None, "tp"),
        P("dp", None, "tp"),
        P("tp", "dp"),
        P("tp", "dp"),
    )
    return jax.shard_map(
        local, mesh=mesh, in_specs=placed, out_specs=P("dp", "ctx", "tp"), check_vma=False
    )
```
